128 devices in a mesh: section: 4 (over x), seq: 16 (over z_lo, y, core), head: 2 (over z_hi).
Axes of the slice: x: 4, y: 4, z: 4 (z_hi: 2, z_lo: 2; z = z_hi * 2 + z_lo), core: 2. Of those that a mesh axis runs over, the one named last changes fastest.
Arguments:
- notes: bfloat16 [4, 4096, 2048], P('section', 'seq'), may hold values from -18 to 18
- frames: bfloat16 [4, 16384, 2048], P('section', 'seq'), may hold values from -18 to 18
- w_query: bfloat16 [2048, 2048], P(None, 'head'), may hold values from -0.125 to 0.125
- w_key: bfloat16 [2048, 2048], P(None, 'head'), may hold values from -0.125 to 0.125
- w_value: bfloat16 [2048, 2048], P(None, 'head'), may hold values from -0.125 to 0.125
- w_out: bfloat16 [2048, 2048], P('head'), may hold values from -0.125 to 0.125
- band_blocks: int32 [4, 2, 128], P('section', None, 'seq'), may hold values from 0 to 31, as said below
- grad_mixed: bfloat16 [4, 16384, 2048], P('section', 'seq'), may hold values from -6 to 6
Outputs:
- frame_grad: bfloat16 [4, 16384, 2048], P('section', 'seq', 'head')
- note_grad: bfloat16 [4, 4096, 2048], P('section', 'seq', 'head')
The draws below stay inside these ranges and needn't reach their ends.
Inputs may be any that keep to these rules, and one draw needn't show every extreme that they name: band_blocks[m, 0, b] <= band_blocks[m, 1, b]; both lie among the note blocks of seq shards b // 8 - 1 to b // 8 + 1.
All inputs are finite; a program needn't handle non-finite values.
Results may differ from the reference program's by a relative error of at most 0.017.
The reference program's roundings to bfloat16 on the way (of `queries`, `grad_ctx`, `probs_low`, `grad_scores` and `grad_queries`) count: a program that leaves them out, or rounds other values in their place, can miss the bound.
Values may be sent and summed in bfloat16 or wider, within the bound.
No kernel may reach another device: no remote copies, remote signals or barrier semaphores. Data moves between devices by JAX's collectives and lax.ppermute only.
A program may use at most 192 MiB of HBM per device.

```python
import jax
import jax.numpy as jnp
from jax import lax

D = 2048
HEADS = 16
BLK = 128
FR_DEV = 1024
NT_DEV = 256
MB = 4
FRAMES = 16384
NOTES = 4096
FBLK = 128
NBLK = 32
N_SEQ = 16
N_HEAD = 2


def scaled_rows(key, rows):
    base = jax.random.truncated_normal(key, -6.0, 6.0, (MB, rows, D), jnp.float32)
    return base


def draw_notes(key, part):
    return scaled_rows(key, NOTES).astype(jnp.bfloat16)


def draw_frames(key, part):
    return scaled_rows(key, FRAMES).astype(jnp.bfloat16)


def draw_band_blocks(key, part):
    frame_blocks_dev = FR_DEV // BLK
    note_blocks_dev = NT_DEV // BLK
    block_ids = jnp.arange(FBLK, dtype=jnp.int32)
    centre = block_ids * note_blocks_dev // frame_blocks_dev
    back = jax.random.randint(jax.random.fold_in(key, 1), (MB, FBLK), 0, note_blocks_dev + 1)
    ahead = jax.random.randint(jax.random.fold_in(key, 2), (MB, FBLK), 0, note_blocks_dev + 1)
    first = jnp.maximum(centre[None, :] - back, 0)
    last = jnp.minimum(centre[None, :] + ahead, NBLK - 1)
    return jnp.stack([first, last], axis=1).astype(jnp.int32)


def steps_of(stream_key, shape, shards, smallest, largest):
    level = 1.0
    for position, shards_of in shards:
        steps = jax.random.uniform(jax.random.fold_in(jax.random.fold_in(stream_key, 6), position), (shards_of,), jnp.float32, smallest / len(shards), largest / len(shards))
        level = level * jnp.repeat(jnp.exp(steps), shape[position] // shards_of).reshape((-1,) + (1,) * (len(shape) - 1 - position))
    return level


def gaussian(key, shape, scale, bound, shards=(), kind=jnp.bfloat16):
    level = steps_of(key, shape, shards, -0.22, 0.18) if shards else 1.0
    array = jax.random.normal(key, shape, jnp.float32) * scale * level
    return jnp.minimum(jnp.maximum(array, -bound), bound).astype(kind)


def setup_inputs(seed: int = 0) -> dict:
    streams_of = jax.random.split(jax.random.key(seed), 9)
    return {
        "notes": draw_notes(jax.random.fold_in(streams_of[8], 71), 0),
        "frames": draw_frames(jax.random.fold_in(streams_of[8], 71), 0),
        "w_query": gaussian(streams_of[2], (D, D), D ** -0.5, 0.125, ((1, 2),)),
        "w_key": gaussian(streams_of[3], (D, D), D ** -0.5, 0.125, ((1, 2),)),
        "w_value": gaussian(streams_of[4], (D, D), D ** -0.5, 0.125, ((1, 2),)),
        "w_out": gaussian(streams_of[5], (D, D), D ** -0.5, 0.125, ((0, 2),)),
        "band_blocks": draw_band_blocks(jax.random.fold_in(streams_of[8], 71), 0),
        "grad_mixed": gaussian(streams_of[7], (MB, FRAMES, D), 1.0, 6.0, ((0, 4), (1, 16))),
    }


def attend_shard(queries, grad_ctx, key_win, value_win, first_rows, last_rows, shard, score_scale):
    f32 = jnp.float32
    scores = jnp.einsum('rhd,nhd->hrn', queries.astype(f32), key_win.astype(f32)) * score_scale
    window_blocks = (shard - 1) * (NT_DEV // BLK) + jnp.arange(key_win.shape[0], dtype=jnp.int32) // BLK
    allowed = (window_blocks[None, :] >= first_rows[:, None]) & (window_blocks[None, :] <= last_rows[:, None])
    scores = jnp.where(allowed[None], scores, -jnp.inf)
    peak = jnp.max(scores, axis=-1, keepdims=True)
    expos = jnp.exp(scores - peak)
    probs = expos / jnp.sum(expos, axis=-1, keepdims=True)
    grad_probs = jnp.einsum('rhd,nhd->hrn', grad_ctx.astype(f32), value_win.astype(f32))
    probs_low = probs.astype(jnp.bfloat16)
    value_sum = jnp.einsum('hrn,rhd->nhd', probs_low.astype(f32), grad_ctx.astype(f32))
    delta = jnp.sum(probs * grad_probs, axis=-1, keepdims=True)
    grad_scores = (probs * (grad_probs - delta) * score_scale).astype(jnp.bfloat16)
    grad_queries = jnp.einsum('hrn,nhd->rhd', grad_scores.astype(f32), key_win.astype(f32)).astype(jnp.bfloat16)
    key_sum = jnp.einsum('hrn,rhd->nhd', grad_scores.astype(f32), queries.astype(f32))
    return grad_queries, key_sum, value_sum


def fold_windows(windows):
    parts = windows.reshape(N_SEQ, 3, NT_DEV, D)
    acc = jnp.zeros((N_SEQ + 2, NT_DEV, D), jnp.float32)
    acc = acc.at[0:N_SEQ].add(parts[:, 0]).at[1:N_SEQ + 1].add(parts[:, 1]).at[2:N_SEQ + 2].add(parts[:, 2])
    return acc[1:N_SEQ + 1].reshape(NOTES, D)


def group_sum(pieces):
    summed = jnp.zeros(pieces[0].shape, jnp.float32)
    for piece in pieces:
        rounded = lax.optimization_barrier(piece.astype(jnp.bfloat16))
        summed = summed + rounded.astype(jnp.float32)
    return summed.astype(jnp.bfloat16)


def reference(notes, frames, w_query, w_key, w_value, w_out, band_blocks, grad_mixed):
    head_size = D // HEADS
    score_scale = head_size ** -0.5
    group_cols = D // N_HEAD
    frame_list = []
    note_list = [None] * MB
    for song in range(MB):
        source = (song - 1) % MB
        keys = jnp.dot(notes[source], w_key, preferred_element_type=jnp.float32).astype(jnp.bfloat16)
        values = jnp.dot(notes[source], w_value, preferred_element_type=jnp.float32).astype(jnp.bfloat16)
        queries = jnp.dot(frames[song], w_query, preferred_element_type=jnp.float32).astype(jnp.bfloat16)
        grad_ctx = lax.dot_general(grad_mixed[song], w_out, (((1,), (1,)), ((), ())), preferred_element_type=jnp.float32).astype(jnp.bfloat16)
        key_pad = jnp.pad(keys, ((NT_DEV, NT_DEV), (0, 0)))
        value_pad = jnp.pad(values, ((NT_DEV, NT_DEV), (0, 0)))
        first_rows = jnp.repeat(band_blocks[song, 0], BLK)
        last_rows = jnp.repeat(band_blocks[song, 1], BLK)

        def per_shard(shard):
            row_start = (shard * FR_DEV).astype(jnp.int32)
            note_start = (shard * NT_DEV).astype(jnp.int32)
            query_rows = lax.dynamic_slice_in_dim(queries, row_start, FR_DEV, 0).reshape(FR_DEV, HEADS, head_size)
            grad_rows = lax.dynamic_slice_in_dim(grad_ctx, row_start, FR_DEV, 0).reshape(FR_DEV, HEADS, head_size)
            key_win = lax.dynamic_slice_in_dim(key_pad, note_start, 3 * NT_DEV, 0).reshape(3 * NT_DEV, HEADS, head_size)
            value_win = lax.dynamic_slice_in_dim(value_pad, note_start, 3 * NT_DEV, 0).reshape(3 * NT_DEV, HEADS, head_size)
            first_here = lax.dynamic_slice_in_dim(first_rows, row_start, FR_DEV, 0)
            last_here = lax.dynamic_slice_in_dim(last_rows, row_start, FR_DEV, 0)
            return attend_shard(query_rows, grad_rows, key_win, value_win, first_here, last_here, shard, score_scale)

        grad_queries, key_windows, value_windows = lax.map(per_shard, jnp.arange(N_SEQ, dtype=jnp.int32))
        grad_queries = grad_queries.reshape(FRAMES, D)
        grad_keys = fold_windows(key_windows).astype(jnp.bfloat16)
        grad_values = fold_windows(value_windows).astype(jnp.bfloat16)
        frame_parts = []
        note_parts = []
        for group in range(N_HEAD):
            cols = slice(group * group_cols, (group + 1) * group_cols)
            frame_parts.append(lax.dot_general(grad_queries[:, cols], w_query[:, cols], (((1,), (1,)), ((), ())), preferred_element_type=jnp.float32))
            note_parts.append(lax.dot_general(grad_keys[:, cols], w_key[:, cols], (((1,), (1,)), ((), ())), preferred_element_type=jnp.float32)
                              + lax.dot_general(grad_values[:, cols], w_value[:, cols], (((1,), (1,)), ((), ())), preferred_element_type=jnp.float32))
        frame_list.append(group_sum(frame_parts))
        note_list[source] = group_sum(note_parts)
    return jnp.stack(frame_list), jnp.stack(note_list)
```

```python
import jax
import jax.numpy as jnp
from jax import lax
from jax.experimental import pallas as pl
from jax.experimental.pallas import tpu as pltpu
from jax.sharding import PartitionSpec as P

D = 2048
HEADS = 16
BLK = 128
HD = D // HEADS
SCALE = HD**-0.5
LOG2E = 1.4426950408889634
CHUNKS = ((0, 2), (2, 2), (4, 4))
MIB = 2**20

F32 = jnp.float32
BF16 = jnp.bfloat16
NN = (((1,), (0,)), ((), ()))
NT = (((1,), (1,)), ((), ()))
TN = (((0,), (0,)), ((), ()))


def dot(a, b, dims):
    return lax.dot_general(a, b, dims, preferred_element_type=F32)


def section_shift(block, distance):
    count = lax.axis_size("section")
    return lax.ppermute(
        block, "section", [(i, (i + distance) % count) for i in range(count)]
    )


def seq_shift(block, distance):
    count = lax.axis_size("seq")
    return lax.ppermute(
        block, "seq", [(i, i + distance) for i in range(count) if 0 <= i + distance < count]
    )


def seq_flip(block, mask):
    count = lax.axis_size("seq")
    return lax.ppermute(block, "seq", [(i, i ^ mask) for i in range(count)])


def head_swap(block):
    return lax.ppermute(block, "head", [(0, 1), (1, 0)])


def across(block, mask):
    count = lax.axis_size("seq")
    route = [(2 * i + g, 2 * (i ^ mask) + 1 - g) for i in range(count) for g in range(2)]
    return lax.ppermute(block, ("seq", "head"), route)


def key_value_body(notes_ref, wk_ref, wv_ref, out_ref):
    rows = notes_ref[...]
    out_ref[0] = dot(rows, wk_ref[...], NN).astype(BF16)
    out_ref[1] = dot(rows, wv_ref[...], NN).astype(BF16)


def key_values(notes, w_key, w_value, h0, hc):
    rows = notes.shape[0]
    wide = 2 * HD
    base = h0 * HD // wide
    weight = pl.BlockSpec((D, wide), lambda j: (0, base + j))
    return pl.pallas_call(
        key_value_body,
        grid=(hc * HD // wide,),
        in_specs=[pl.BlockSpec((rows, D), lambda j: (0, 0)), weight, weight],
        out_specs=pl.BlockSpec((2, rows, wide), lambda j: (0, 0, j)),
        out_shape=jax.ShapeDtypeStruct((2, rows, hc * HD), BF16),
        compiler_params=pltpu.CompilerParams(vmem_limit_bytes=16 * MIB),
        cost_estimate=pl.CostEstimate(
            flops=4 * rows * D * hc * HD,
            bytes_accessed=2 * (rows * D + 2 * D * hc * HD + 2 * rows * hc * HD),
            transcendentals=0,
        ),
        name="key_values",
    )(notes, w_key, w_value)


def attention_body(
    bias_ref, q_ref, g_ref, kvl_ref, kvo_ref, kvr_ref, dq_ref, own_ref, left_ref, right_ref,
    p_scr, ds_scr,
):
    scale2 = SCALE * LOG2E
    frames = q_ref.shape[0]
    nt = kvo_ref.shape[1]
    step = 256
    blocks = 3 * nt // BLK
    keys = jnp.concatenate([kvl_ref[0], kvo_ref[0], kvr_ref[0]], axis=0)
    values = jnp.concatenate([kvl_ref[1], kvo_ref[1], kvr_ref[1]], axis=0)
    for f in range(frames // step):
        cols = slice(f * step, (f + 1) * step)
        s = dot(keys, q_ref[cols, :], NT)
        gp = dot(values, g_ref[cols, :], NT)
        rows = [slice(j * BLK, (j + 1) * BLK) for j in range(blocks)]
        bias = [bias_ref[j : j + 1, cols] for j in range(blocks)]
        peak = None
        for j in range(blocks):
            top = jnp.max(s[rows[j]], axis=0, keepdims=True) + bias[j]
            peak = top if peak is None else jnp.maximum(peak, top)
        expos = []
        total = jnp.zeros((1, step), F32)
        mixed = jnp.zeros((1, step), F32)
        for j in range(blocks):
            e = jnp.exp2(s[rows[j]] * scale2 + (bias[j] - peak) * scale2)
            expos.append(e)
            total = total + jnp.sum(e, axis=0, keepdims=True)
            mixed = mixed + jnp.sum(e * gp[rows[j]], axis=0, keepdims=True)
        inv = 1.0 / total
        delta = mixed * inv
        for j in range(blocks):
            p = expos[j] * inv
            p_scr[rows[j], cols] = p.astype(BF16)
            ds_scr[rows[j], cols] = (p * (gp[rows[j]] - delta)).astype(BF16)
    dq_ref[...] = (dot(ds_scr[...], keys, TN) * SCALE).astype(BF16)
    dv = dot(p_scr[...], g_ref[...], NN)
    dk = dot(ds_scr[...], q_ref[...], NN) * SCALE
    for i, grad in enumerate((dk, dv)):
        left_ref[i] = grad[:nt].astype(BF16)
        own_ref[i] = grad[nt : 2 * nt]
        right_ref[i] = grad[2 * nt :].astype(BF16)


def attention(bias, queries, grad_ctx, kv_left, kv_own, kv_right, h0, hc):
    frames = queries.shape[0]
    nt = kv_own.shape[1]
    frame_in = pl.BlockSpec((frames, HD), lambda h: (0, h0 + h))
    note_io = pl.BlockSpec((2, nt, HD), lambda h: (0, 0, h))
    pairs = frames * 3 * nt * hc
    return pl.pallas_call(
        attention_body,
        grid=(hc,),
        in_specs=[
            pl.BlockSpec(bias.shape, lambda h: (0, 0)), frame_in, frame_in, note_io, note_io, note_io,
        ],
        out_specs=[pl.BlockSpec((frames, HD), lambda h: (0, h)), note_io, note_io, note_io],
        out_shape=[
            jax.ShapeDtypeStruct((frames, hc * HD), BF16),
            jax.ShapeDtypeStruct((2, nt, hc * HD), F32),
            jax.ShapeDtypeStruct((2, nt, hc * HD), BF16),
            jax.ShapeDtypeStruct((2, nt, hc * HD), BF16),
        ],
        scratch_shapes=[pltpu.VMEM((3 * nt, frames), BF16), pltpu.VMEM((3 * nt, frames), BF16)],
        compiler_params=pltpu.CompilerParams(vmem_limit_bytes=32 * MIB),
        cost_estimate=pl.CostEstimate(
            flops=20 * pairs * HD,
            bytes_accessed=hc * HD * (6 * frames + 32 * nt),
            transcendentals=pairs,
        ),
        name="attention",
    )(bias, queries, grad_ctx, kv_left, kv_own, kv_right)


def per_device(notes, frames, w_query, w_key, w_value, w_out, band_blocks, grad_mixed):
    nt = notes.shape[1]
    fr = frames.shape[1]
    cols = w_query.shape[1]
    half = D // 2
    shard = lax.axis_index("seq")
    group = lax.axis_index("head")
    core = shard % 2

    block_ids = (shard - 1) * (nt // BLK) + jnp.arange(8, dtype=jnp.int32)
    inside = (block_ids[:, None] >= band_blocks[0, 0][None]) & (
        block_ids[:, None] <= band_blocks[0, 1][None]
    )
    bias = jnp.repeat(jnp.where(inside, 0.0, -jnp.inf).astype(F32), BLK, axis=1)

    moved = []
    for h0, hc in CHUNKS:
        moved.append(section_shift(key_values(notes[0], w_key, w_value, h0, hc), 1))

    quarter = half // 2
    give = lax.dynamic_slice_in_dim(w_query, (1 - group) * half + core * quarter, quarter, 0)
    mine = across(give, 8)
    theirs = seq_flip(mine, 1)
    w_other = jnp.where(
        core == 0, jnp.concatenate([mine, theirs]), jnp.concatenate([theirs, mine])
    )
    w_own = lax.dynamic_slice_in_dim(w_query, group * half, half, 0)

    queries = dot(frames[0], w_query, NN).astype(BF16)
    grad_ctx = dot(grad_mixed[0], w_out, NT).astype(BF16)

    grad_q = []
    grad_q_other = []
    note_cols = []
    for (h0, hc), kv in zip(CHUNKS, moved):
        kv_left = seq_shift(kv, 1)
        kv_right = seq_shift(kv, -1)
        dq, own, left, right = attention(bias, queries, grad_ctx, kv_left, kv, kv_right, h0, hc)
        grad_q.append(dq)
        grad_q_other.append(head_swap(dq))
        summed = own + seq_shift(right, 1).astype(F32) + seq_shift(left, -1).astype(F32)
        note_cols.append(section_shift(summed.astype(BF16), -1))

    frame_sum = None
    for weight, grads in ((w_own, grad_q), (w_other, grad_q_other)):
        for (h0, hc), grad in zip(CHUNKS, grads):
            term = dot(grad, weight[:, h0 * HD : (h0 + hc) * HD], NT)
            frame_sum = term if frame_sum is None else frame_sum + term

    note_term = None
    for (h0, hc), grad in zip(CHUNKS, note_cols):
        part = slice(h0 * HD, (h0 + hc) * HD)
        term = dot(grad[0], w_key[:, part], NT) + dot(grad[1], w_value[:, part], NT)
        note_term = term if note_term is None else note_term + term
    note_term = note_term.astype(BF16)
    give_notes = lax.dynamic_slice_in_dim(note_term, (1 - group) * half, half, 1)
    keep_notes = lax.dynamic_slice_in_dim(note_term, group * half, half, 1)
    note_sum = keep_notes.astype(F32) + head_swap(give_notes).astype(F32)
    return (frame_sum.astype(BF16)[None], note_sum.astype(BF16)[None])


def solution(mesh):
    placed = (
        P("section", "seq", None),
        P("section", "seq", None),
        P(None, "head"),
        P(None, "head"),
        P(None, "head"),
        P("head", None),
        P("section", None, "seq"),
        P("section", "seq", None),
    )
    return jax.shard_map(
        per_device,
        mesh=mesh,
        in_specs=placed,
        out_specs=(P("section", "seq", "head"), P("section", "seq", "head")),
        check_vma=False,
    )
```

```python
import jax
import jax.numpy as jnp
from jax import lax
from jax.experimental import pallas as pl
from jax.experimental.pallas import tpu as pltpu
from jax.sharding import PartitionSpec as P

D = 2048
HEADS = 16
BLK = 128
HD = D // HEADS
SCALE = HD**-0.5
LOG2E = 1.4426950408889634
CHUNKS = ((0, 2), (2, 3), (5, 3))
MIB = 2**20

F32 = jnp.float32
BF16 = jnp.bfloat16
NN = (((1,), (0,)), ((), ()))
NT = (((1,), (1,)), ((), ()))
TN = (((0,), (0,)), ((), ()))


def dot(a, b, dims):
    return lax.dot_general(a, b, dims, preferred_element_type=F32)


def section_shift(block, distance):
    count = lax.axis_size("section")
    return lax.ppermute(
        block, "section", [(i, (i + distance) % count) for i in range(count)]
    )


def near_swap(block):
    count = lax.axis_size("seq")
    return lax.ppermute(block, "seq", [(i, i ^ 1) for i in range(count)])


def far_swap(block):
    count = lax.axis_size("seq")
    pairs = [(i, i + 1) for i in range(1, count - 1, 2)]
    return lax.ppermute(block, "seq", pairs + [(j, i) for i, j in pairs])


def head_swap(block):
    return lax.ppermute(block, "head", [(0, 1), (1, 0)])


def other_columns(give):
    count = lax.axis_size("seq")
    quads = [
        [2 * i, 2 * i + 2, 2 * (i ^ 8) + 1, 2 * (i ^ 8) + 3] for i in range(0, count, 2)
    ]
    return lax.all_gather(give, ("seq", "head"), axis_index_groups=quads)


def in_hbm(shape):
    return pltpu.HBM(shape.shape, shape.dtype)


def call(body, grid, in_specs, out_specs, out_shape, args, name, after=(), scalars=0, scratch=(), flops=0):
    first = scalars + len(in_specs)
    unread = len(after)

    def reads(*refs):
        body(*refs[:first], *refs[first + unread :])

    in_specs = list(in_specs) + [pl.BlockSpec(memory_space=pl.ANY)] * unread
    return pl.pallas_call(
        reads,
        grid_spec=pltpu.PrefetchScalarGridSpec(
            num_scalar_prefetch=scalars,
            grid=grid,
            in_specs=in_specs,
            out_specs=out_specs,
            scratch_shapes=scratch,
        ),
        out_shape=jax.tree.map(in_hbm, out_shape),
        compiler_params=pltpu.CompilerParams(vmem_limit_bytes=64 * MIB - 64 * 1024),
        cost_estimate=pl.CostEstimate(flops=flops, bytes_accessed=0, transcendentals=0),
        name=name,
    )(*args, *after)


def key_value_body(notes_ref, wk_ref, wv_ref, out_ref):
    weights = jnp.concatenate([wk_ref[...], wv_ref[...]], axis=1)
    both = dot(notes_ref[...], weights, NN).astype(BF16)
    out_ref[0] = both[:, :HD]
    out_ref[1] = both[:, HD:]


def key_values(notes, w_key, w_value, h0, hc, after):
    rows = notes.shape[0]
    weight = pl.BlockSpec((D, HD), lambda h: (0, h0 + h))
    return call(
        key_value_body,
        (hc,),
        [pl.BlockSpec((rows, D), lambda h: (0, 0)), weight, weight],
        pl.BlockSpec((2, rows, HD), lambda h: (0, 0, h)),
        jax.ShapeDtypeStruct((2, rows, hc * HD), BF16),
        (notes, w_key, w_value),
        "key_values",
        after,
    )


def project(rows, weight, transposed, name, after):
    count, depth = rows.shape
    width = weight.shape[0 if transposed else 1]
    step = 256
    dims = NT if transposed else NN

    def body(a_ref, w_ref, out_ref):
        out_ref[...] = dot(a_ref[...], w_ref[...], dims).astype(BF16)

    if transposed:
        weight_in = pl.BlockSpec((step, depth), lambda n: (n, 0))
    else:
        weight_in = pl.BlockSpec((depth, step), lambda n: (0, n))
    return call(
        body,
        (width // step,),
        [pl.BlockSpec((count, depth), lambda n: (0, 0)), weight_in],
        pl.BlockSpec((count, step), lambda n: (0, n)),
        jax.ShapeDtypeStruct((count, width), BF16),
        (rows, weight),
        name,
        after,
    )


def give_body(scalars_ref, w_ref, out_ref):
    out_ref[...] = w_ref[...]


def give_columns(scalars, w_query, after):
    cols = w_query.shape[1]
    rows = D // 4
    step = rows // 2
    return call(
        give_body,
        (2,),
        [pl.BlockSpec((step, cols), lambda n, s: (4 * (1 - s[0]) + 2 * s[1] + n, 0))],
        pl.BlockSpec((step, cols), lambda n, s: (n, 0)),
        jax.ShapeDtypeStruct((rows, cols), BF16),
        (scalars, w_query),
        "give_columns",
        after,
        scalars=1,
    )


def frame_sum_own(scalars, grads, grads_other, w_query, w_other, chunks_other, after):
    rows = grads[0].shape[0]
    half = D // 2
    cols = w_query.shape[1]
    step = 256
    nother = len(grads_other)
    other_width = sum(hc for _, hc in chunks_other) * HD

    def body(s_ref, *refs):
        own = refs[: len(grads)]
        other = refs[len(grads) : len(grads) + nother]
        w_ref, wo_ref, out_ref = refs[len(grads) + nother :]
        left = jnp.concatenate([r[...] for r in own], axis=1)
        total = dot(left, w_ref[...], NT)
        right = jnp.concatenate([r[...] for r in other], axis=1)
        out_ref[...] = total + dot(right, wo_ref[0, :, :other_width], NT)

    whole = lambda g: pl.BlockSpec(g.shape, lambda n, s: (0, 0))
    return call(
        body,
        (half // step,),
        [whole(g) for g in grads]
        + [whole(g) for g in grads_other]
        + [
            pl.BlockSpec((step, cols), lambda n, s: (4 * s[0] + n, 0)),
            pl.BlockSpec((1, step, cols), lambda n, s: (2 * (1 - s[0]) + n // 2, n % 2, 0)),
        ],
        pl.BlockSpec((rows, step), lambda n, s: (0, n)),
        jax.ShapeDtypeStruct((rows, half), F32),
        (scalars, *grads, *grads_other, w_query, w_other),
        "frame_sum_own",
        after,
        scalars=1,
    )


def frame_sum_last(scalars, total, grad, w_other, h0, hc, after):
    rows, half = total.shape
    step = 256

    def body(s_ref, t_ref, g_ref, *refs):
        weight = jnp.concatenate([r[0] for r in refs[:hc]], axis=1)
        refs[hc][...] = (t_ref[...] + dot(g_ref[...], weight, NT)).astype(BF16)

    def weight_in(k):
        return pl.BlockSpec((1, step, HD), lambda n, s: (2 * (1 - s[0]) + n // 2, n % 2, h0 + k))

    return call(
        body,
        (half // step,),
        [
            pl.BlockSpec((rows, step), lambda n, s: (0, n)),
            pl.BlockSpec(grad.shape, lambda n, s: (0, 0)),
        ]
        + [weight_in(k) for k in range(hc)],
        pl.BlockSpec((rows, step), lambda n, s: (0, n)),
        jax.ShapeDtypeStruct((rows, half), BF16),
        (scalars, total, grad) + (w_other,) * hc,
        "frame_sum_last",
        after,
        scalars=1,
    )


def note_product(scalars, grads, chunks, w_key, w_value, after, before=None):
    nt = grads[0].shape[1]
    half = D // 2
    heads = [h for h0, hc in chunks for h in range(h0, h0 + hc)]
    hc = len(heads)
    last = before is not None

    def body(s_ref, *refs):
        grad_refs, refs = refs[: len(grads)], refs[len(grads) :]
        wk = jnp.concatenate([r[...] for r in refs[:hc]], axis=1)
        wv = jnp.concatenate([r[...] for r in refs[hc : 2 * hc]], axis=1)
        gk = jnp.concatenate([r[0] for r in grad_refs], axis=1)
        gv = jnp.concatenate([r[1] for r in grad_refs], axis=1)
        total = dot(gk, wk, NT) + dot(gv, wv, NT)
        if last:
            total = total + refs[2 * hc][0]
        out_ref = refs[-1]
        out_ref[0] = total.astype(out_ref.dtype)

    def weight_in(h):
        return pl.BlockSpec((half, HD), lambda n, s: (jnp.where(n == 0, 1 - s[0], s[0]), h))

    half_io = pl.BlockSpec((1, nt, half), lambda n, s: (n, 0, 0))
    return call(
        body,
        (2,),
        [pl.BlockSpec(g.shape, lambda n, s: (0, 0, 0)) for g in grads]
        + [weight_in(h) for h in heads] * 2
        + ([half_io] if last else []),
        half_io,
        jax.ShapeDtypeStruct((2, nt, half), BF16 if last else F32),
        (scalars, *grads) + (w_key,) * hc + (w_value,) * hc + ((before,) if last else ()),
        "note_product",
        after,
        scalars=1,
    )


def attention_body(
    bias_ref, q_ref, g_ref, kvo_ref, kvn_ref, kvf_ref, dq_ref, own_ref, near_ref, far_ref,
    p_scr, ds_scr,
):
    scale2 = SCALE * LOG2E
    frames = q_ref.shape[0]
    nt = kvo_ref.shape[1]
    step = 256
    blocks = 3 * nt // BLK
    keys = jnp.concatenate([kvo_ref[0], kvn_ref[0], kvf_ref[0]], axis=0)
    values = jnp.concatenate([kvo_ref[1], kvn_ref[1], kvf_ref[1]], axis=0)
    for f in range(frames // step):
        cols = slice(f * step, (f + 1) * step)
        s = dot(keys, q_ref[cols, :], NT)
        gp = dot(values, g_ref[cols, :], NT)
        rows = [slice(j * BLK, (j + 1) * BLK) for j in range(blocks)]
        bias = [bias_ref[j : j + 1, cols] for j in range(blocks)]
        peak = None
        for j in range(blocks):
            top = jnp.max(s[rows[j]], axis=0, keepdims=True) + bias[j]
            peak = top if peak is None else jnp.maximum(peak, top)
        expos = []
        total = jnp.zeros((1, step), F32)
        mixed = jnp.zeros((1, step), F32)
        for j in range(blocks):
            e = jnp.exp2(s[rows[j]] * scale2 + (bias[j] - peak) * scale2)
            expos.append(e)
            total = total + jnp.sum(e, axis=0, keepdims=True)
            mixed = mixed + jnp.sum(e * gp[rows[j]], axis=0, keepdims=True)
        inv = 1.0 / total
        delta = mixed * inv
        for j in range(blocks):
            p = expos[j] * inv
            p_scr[rows[j], cols] = p.astype(BF16)
            ds_scr[rows[j], cols] = (p * (gp[rows[j]] - delta)).astype(BF16)
    dq_ref[...] = (dot(ds_scr[...], keys, TN) * SCALE).astype(BF16)
    dv = dot(p_scr[...], g_ref[...], NN)
    dk = dot(ds_scr[...], q_ref[...], NN) * SCALE
    for i, grad in enumerate((dk, dv)):
        own_ref[i] = grad[:nt]
        near_ref[i] = grad[nt : 2 * nt].astype(BF16)
        far_ref[i] = grad[2 * nt :].astype(BF16)


def attention(bias, queries, grad_ctx, kv_own, kv_near, kv_far, h0, hc, after):
    frames = queries.shape[0]
    nt = kv_own.shape[1]
    frame_in = pl.BlockSpec((frames, HD), lambda h: (0, h0 + h))
    note_io = pl.BlockSpec((2, nt, HD), lambda h: (0, 0, h))
    notes_out = jax.ShapeDtypeStruct((2, nt, hc * HD), BF16)
    return call(
        attention_body,
        (hc,),
        [pl.BlockSpec(bias.shape, lambda h: (0, 0)), frame_in, frame_in, note_io, note_io, note_io],
        [pl.BlockSpec((frames, HD), lambda h: (0, h)), note_io, note_io, note_io],
        [
            jax.ShapeDtypeStruct((frames, hc * HD), BF16),
            jax.ShapeDtypeStruct((2, nt, hc * HD), F32),
            notes_out,
            notes_out,
        ],
        (bias, queries, grad_ctx, kv_own, kv_near, kv_far),
        "attention",
        after,
        scratch=[pltpu.VMEM((3 * nt, frames), BF16), pltpu.VMEM((3 * nt, frames), BF16)],
        flops=90 * frames * nt * hc * HD,
    )


def per_device(notes, frames, w_query, w_key, w_value, w_out, band_blocks, grad_mixed):
    nt = notes.shape[1]
    shard = lax.axis_index("seq")
    group = lax.axis_index("head")
    core = shard % 2
    scalars = jnp.stack([group, core]).astype(jnp.int32)

    made = []
    moved = []
    for h0, hc in CHUNKS:
        made.append(key_values(notes[0], w_key, w_value, h0, hc, made[-1:]))
        moved.append(section_shift(made[-1], 1))
    given = give_columns(scalars, w_query, made[-1:])
    w_other = other_columns(given)

    far_shard = jnp.where(core == 0, shard - 1, shard + 1)
    shards = jnp.stack([shard, shard ^ 1, far_shard, shard])
    per_shard = nt // BLK
    block_ids = (shards[:, None] * per_shard + jnp.arange(per_shard, dtype=jnp.int32)).reshape(-1)
    inside = (block_ids[:, None] >= band_blocks[0, 0][None]) & (
        block_ids[:, None] <= band_blocks[0, 1][None]
    )
    bias = jnp.repeat(jnp.where(inside, 0.0, -jnp.inf).astype(F32), BLK, axis=1)

    queries = project(frames[0], w_query, False, "queries", (given,))
    moved[0], queries = lax.optimization_barrier((moved[0], queries))
    grad_ctx = project(grad_mixed[0], w_out, True, "grad_ctx", (queries, moved[0]))

    grad_q = []
    grad_q_other = []
    note_cols = []
    summed_all = []

    def send_back(own, near, far, also=None):
        near = near_swap(near)
        far = far_swap(far)
        if also:
            near, also[-1] = lax.optimization_barrier((near, also[-1]))
        summed_all.append((own + near.astype(F32) + far.astype(F32)).astype(BF16))
        note_cols.append(section_shift(summed_all[-1], -1))

    for step, (h0, hc) in enumerate(CHUNKS):
        kv = moved[step]
        after = grad_q[-1:]
        kv_near, kv_far = near_swap(kv), far_swap(kv)
        if step == 1:
            near, far, kv_near, kv_far = lax.optimization_barrier((near, far, kv_near, kv_far))
            send_back(own, near, far)
        if step == 2:
            after = after + [grad_q_other[0], summed_all[0]]
        dq, own, near, far = attention(
            bias, queries, grad_ctx, kv, kv_near, kv_far, h0, hc, after
        )
        if step == 0:
            moved[2], dq = lax.optimization_barrier((moved[2], dq))
        grad_q.append(dq)
        grad_q_other.append(head_swap(dq))
        if step == 1:
            send_back(own, near, far, grad_q_other)
    near, far, note_cols[0] = lax.optimization_barrier((near, far, note_cols[0]))
    send_back(own, near, far)

    total = frame_sum_own(
        scalars, grad_q, grad_q_other[:-1], w_query, w_other, CHUNKS[:-1], ()
    )
    before = note_product(scalars, note_cols[:-1], CHUNKS[:-1], w_key, w_value, (total,))
    frame_sum = frame_sum_last(
        scalars, total, grad_q_other[-1], w_other, *CHUNKS[-1], (before,)
    )
    halves = note_product(
        scalars, note_cols[-1:], CHUNKS[-1:], w_key, w_value, (frame_sum,), before
    )
    give_notes = head_swap(halves[0])
    note_sum = halves[1].astype(F32) + give_notes.astype(F32)
    return (frame_sum[None], note_sum.astype(BF16)[None])


def solution(mesh):
    placed = (
        P("section", "seq", None),
        P("section", "seq", None),
        P(None, "head"),
        P(None, "head"),
        P(None, "head"),
        P("head", None),
        P("section", None, "seq"),
        P("section", "seq", None),
    )
    return jax.shard_map(
        per_device,
        mesh=mesh,
        in_specs=placed,
        out_specs=(P("section", "seq", "head"), P("section", "seq", "head")),
        check_vma=False,
    )
```

```python
import jax
import jax.numpy as jnp
from jax import lax
from jax.experimental import pallas as pl
from jax.experimental.pallas import tpu as pltpu
from jax.sharding import PartitionSpec as P

D = 2048
HEADS = 16
BLK = 128
HD = D // HEADS
SCALE = HD**-0.5
LOG2E = 1.4426950408889634
CHUNKS = ((0, 2), (2, 3), (5, 3))
VMEM = 64 * 2**20 - 2**16

F32 = jnp.float32
BF16 = jnp.bfloat16
NN = (((1,), (0,)), ((), ()))
NT = (((1,), (1,)), ((), ()))
TN = (((0,), (0,)), ((), ()))


def dot(a, b, dims):
    return lax.dot_general(a, b, dims, preferred_element_type=F32)


def section_shift(block, distance):
    count = lax.axis_size("section")
    return lax.ppermute(
        block, "section", [(i, (i + distance) % count) for i in range(count)]
    )


def near_swap(block):
    count = lax.axis_size("seq")
    return lax.ppermute(block, "seq", [(i, i ^ 1) for i in range(count)])


def far_swap(block):
    count = lax.axis_size("seq")
    pairs = [(i, i + 1) for i in range(1, count - 1, 2)]
    return lax.ppermute(block, "seq", pairs + [(j, i) for i, j in pairs])


def head_swap(block):
    return lax.ppermute(block, "head", [(0, 1), (1, 0)])


def other_columns(give):
    count = lax.axis_size("seq")
    quads = [
        [2 * i, 2 * i + 2, 2 * (i ^ 8) + 1, 2 * (i ^ 8) + 3] for i in range(0, count, 2)
    ]
    return lax.all_gather(give, ("seq", "head"), axis_index_groups=quads)


def call(
    body, grid, in_specs, out_specs, out_shape, args, name, after=(), scalars=0, scratch=(),
    flops=0,
):
    first = scalars + len(in_specs)
    unread = len(after)

    def reads(*refs):
        body(*refs[:first], *refs[first + unread :])

    in_specs = list(in_specs) + [pl.BlockSpec(memory_space=pl.ANY)] * unread
    return pl.pallas_call(
        reads,
        grid_spec=pltpu.PrefetchScalarGridSpec(
            num_scalar_prefetch=scalars,
            grid=grid,
            in_specs=in_specs,
            out_specs=out_specs,
            scratch_shapes=scratch,
        ),
        out_shape=out_shape,
        compiler_params=pltpu.CompilerParams(vmem_limit_bytes=VMEM),
        cost_estimate=pl.CostEstimate(flops=flops, bytes_accessed=0, transcendentals=0),
        name=name,
    )(*args, *after)


def key_values(scalars, notes, w_key, w_value, w_query):
    rows = notes.shape[0]
    cols = w_key.shape[1]
    wide = 2 * HD
    pieces = cols // wide
    quarter = D // 4

    def body(s_ref, notes_ref, wk_ref, wv_ref, wq_ref, *refs):
        outs = refs[: len(CHUNKS)]
        give_ref, wk_scr, wv_scr, *made_scr, sems, out_sems, give_sem = refs[len(CHUNKS) :]
        copies = []
        for p in range(pieces):
            part = slice(p * wide, (p + 1) * wide)
            for i, (src, dst) in enumerate(((wk_ref, wk_scr), (wv_ref, wv_scr))):
                copy = pltpu.make_async_copy(src.at[:, part], dst.at[:, part], sems.at[p, i])
                copy.start()
                copies.append(copy)
        offset = pl.multiple_of((1 - s_ref[0]) * (2 * quarter) + s_ref[1] * quarter, quarter)
        give = pltpu.make_async_copy(wq_ref.at[pl.ds(offset, quarter), :], give_ref, give_sem)
        give.start()
        left = notes_ref[...]
        sent = []
        for p in range(pieces):
            part = slice(p * wide, (p + 1) * wide)
            for i, scr in enumerate((wk_scr, wv_scr)):
                copies[2 * p + i].wait()
                made = dot(left, scr[:, part], NN).astype(BF16)
                for k in range(2):
                    head = 2 * p + k
                    for c, (h0, hc) in enumerate(CHUNKS):
                        if h0 <= head < h0 + hc:
                            at = (head - h0) * HD
                            made_scr[c][i, :, at : at + HD] = made[:, k * HD : (k + 1) * HD]
                        if i == 1 and head == h0 + hc - 1:
                            out = pltpu.make_async_copy(made_scr[c], outs[c], out_sems.at[c])
                            out.start()
                            sent.append(out)
        for copy in sent + [give]:
            copy.wait()

    far = pl.BlockSpec(memory_space=pl.ANY)
    here = pl.BlockSpec(memory_space=pltpu.VMEM)
    return call(
        body,
        (),
        [here, far, far, far],
        [far] * (len(CHUNKS) + 1),
        [jax.ShapeDtypeStruct((2, rows, hc * HD), BF16) for _, hc in CHUNKS]
        + [jax.ShapeDtypeStruct((quarter, cols), BF16)],
        (scalars, notes, w_key, w_value, w_query),
        "key_values",
        scalars=1,
        scratch=[
            pltpu.VMEM((D, cols), BF16),
            pltpu.VMEM((D, cols), BF16),
            *[pltpu.VMEM((2, rows, hc * HD), BF16) for _, hc in CHUNKS],
            pltpu.SemaphoreType.DMA((pieces, 2)),
            pltpu.SemaphoreType.DMA((len(CHUNKS),)),
            pltpu.SemaphoreType.DMA,
        ],
    )


def project(frames, w_query, grad_mixed, w_out, after):
    rows, depth = frames.shape
    width = w_query.shape[1]
    step = 256
    steps = rows // step
    parts = 4

    def body(a_ref, w_ref, b_ref, v_ref, q_ref, g_ref, a_scr, w_scr, b_scr, v_scr, q_scr, g_scr,
             w_sems, row_sems, out_sems):
        waits = []
        for i, (rows_ref, rows_scr, weight_ref, weight_scr) in enumerate(
            ((a_ref, a_scr, w_ref, w_scr), (b_ref, b_scr, v_ref, v_scr))
        ):
            size = weight_ref.shape[0] // parts
            weight_copies = []
            row_copies = []
            for p in range(parts):
                at = slice(p * size, (p + 1) * size)
                copy = pltpu.make_async_copy(weight_ref.at[at], weight_scr.at[at], w_sems.at[i, p])
                copy.start()
                weight_copies.append(copy)
            for m in range(steps):
                at = slice(m * step, (m + 1) * step)
                copy = pltpu.make_async_copy(rows_ref.at[at], rows_scr.at[at], row_sems.at[i, m])
                copy.start()
                row_copies.append(copy)
            waits.append((weight_copies, row_copies))
        sent = []
        for i, (rows_scr, weight_scr, out_scr, out_ref, dims) in enumerate(
            ((a_scr, w_scr, q_scr, q_ref, NN), (b_scr, v_scr, g_scr, g_ref, NT))
        ):
            for copy in waits[i][0]:
                copy.wait()
            for m in range(steps):
                at = slice(m * step, (m + 1) * step)
                waits[i][1][m].wait()
                out_scr[at, :] = dot(rows_scr[at, :], weight_scr[...], dims).astype(BF16)
                copy = pltpu.make_async_copy(out_scr.at[at], out_ref.at[at], out_sems.at[i, m])
                copy.start()
                sent.append(copy)
        for copy in sent:
            copy.wait()

    far = pl.BlockSpec(memory_space=pl.ANY)
    out = jax.ShapeDtypeStruct((rows, width), BF16)
    return call(
        body,
        (),
        [far] * 4,
        [far] * 2,
        [out, out],
        (frames, w_query, grad_mixed, w_out),
        "queries_and_grad_ctx",
        after,
        scratch=[
            pltpu.VMEM(frames.shape, BF16),
            pltpu.VMEM(w_query.shape, BF16),
            pltpu.VMEM(grad_mixed.shape, BF16),
            pltpu.VMEM(w_out.shape, BF16),
            pltpu.VMEM((rows, width), BF16),
            pltpu.VMEM((rows, width), BF16),
            pltpu.SemaphoreType.DMA((2, parts)),
            pltpu.SemaphoreType.DMA((2, steps)),
            pltpu.SemaphoreType.DMA((2, steps)),
        ],
    )


def frame_sum_own(scalars, grads, grads_other, w_query, w_other, chunks_other, after):
    rows = grads[0].shape[0]
    half = D // 2
    cols = w_query.shape[1]
    step = 256
    nother = len(grads_other)
    other_width = sum(hc for _, hc in chunks_other) * HD

    def body(s_ref, *refs):
        own = refs[: len(grads)]
        other = refs[len(grads) : len(grads) + nother]
        w_ref, wo_ref, out_ref = refs[len(grads) + nother :]
        left = jnp.concatenate([r[...] for r in own], axis=1)
        total = dot(left, w_ref[...], NT)
        right = jnp.concatenate([r[...] for r in other], axis=1)
        out_ref[...] = total + dot(right, wo_ref[0, :, :other_width], NT)

    whole = lambda g: pl.BlockSpec(g.shape, lambda n, s: (0, 0))
    return call(
        body,
        (half // step,),
        [whole(g) for g in grads]
        + [whole(g) for g in grads_other]
        + [
            pl.BlockSpec((step, cols), lambda n, s: (4 * s[0] + n, 0)),
            pl.BlockSpec((1, step, cols), lambda n, s: (2 * (1 - s[0]) + n // 2, n % 2, 0)),
        ],
        pl.BlockSpec((rows, step), lambda n, s: (0, n)),
        jax.ShapeDtypeStruct((rows, half), F32),
        (scalars, *grads, *grads_other, w_query, w_other),
        "frame_sum_own",
        after,
        scalars=1,
    )


def frame_sum_last(scalars, total, grad, w_other, h0, hc, after):
    rows, half = total.shape
    step = 256

    def body(s_ref, t_ref, g_ref, *refs):
        weight = jnp.concatenate([r[0] for r in refs[:hc]], axis=1)
        refs[hc][...] = (t_ref[...] + dot(g_ref[...], weight, NT)).astype(BF16)

    def weight_in(k):
        return pl.BlockSpec((1, step, HD), lambda n, s: (2 * (1 - s[0]) + n // 2, n % 2, h0 + k))

    return call(
        body,
        (half // step,),
        [
            pl.BlockSpec((rows, step), lambda n, s: (0, n)),
            pl.BlockSpec(grad.shape, lambda n, s: (0, 0)),
        ]
        + [weight_in(k) for k in range(hc)],
        pl.BlockSpec((rows, step), lambda n, s: (0, n)),
        jax.ShapeDtypeStruct((rows, half), BF16),
        (scalars, total, grad) + (w_other,) * hc,
        "frame_sum_last",
        after,
        scalars=1,
    )


def note_product(scalars, grads, chunks, w_key, w_value, after, before=None, which=(0, 1)):
    nt = grads[0].shape[1]
    half = D // 2
    heads = [h for h0, hc in chunks for h in range(h0, h0 + hc)]
    hc = len(heads)
    last = before is not None
    start = which[0]

    def body(s_ref, *refs):
        grad_refs, refs = refs[: len(grads)], refs[len(grads) :]
        wk = jnp.concatenate([r[...] for r in refs[:hc]], axis=1)
        wv = jnp.concatenate([r[...] for r in refs[hc : 2 * hc]], axis=1)
        gk = jnp.concatenate([r[0] for r in grad_refs], axis=1)
        gv = jnp.concatenate([r[1] for r in grad_refs], axis=1)
        total = dot(gk, wk, NT) + dot(gv, wv, NT)
        if last:
            total = total + refs[2 * hc][0]
        out_ref = refs[-1]
        out_ref[0] = total.astype(out_ref.dtype)

    def weight_in(h):
        return pl.BlockSpec(
            (half, HD), lambda n, s: (jnp.where(n + start == 0, 1 - s[0], s[0]), h)
        )

    return call(
        body,
        (len(which),),
        [pl.BlockSpec(g.shape, lambda n, s: (0, 0, 0)) for g in grads]
        + [weight_in(h) for h in heads] * 2
        + ([pl.BlockSpec((1, nt, half), lambda n, s: (n + start, 0, 0))] if last else []),
        pl.BlockSpec((1, nt, half), lambda n, s: (n, 0, 0)),
        jax.ShapeDtypeStruct((len(which), nt, half), BF16 if last else F32),
        (scalars, *grads) + (w_key,) * hc + (w_value,) * hc + ((before,) if last else ()),
        "note_product",
        after,
        scalars=1,
    )


def attention_body(
    s_ref, band_ref, q_ref, g_ref, kvo_ref, kvn_ref, kvf_ref, dq_ref, own_ref, near_ref, far_ref,
    p_scr, ds_scr, bias_ref,
):
    @pl.when(pl.program_id(0) == 0)
    def _():
        row = lax.broadcasted_iota(jnp.int32, (8, BLK), 0)
        shard = s_ref[2]
        far = shard - 1 + 2 * s_ref[1]
        block = jnp.where(row < 2, 2 * shard, jnp.where(row < 4, 2 * (shard ^ 1), 2 * far)) + row % 2
        for b in range(q_ref.shape[0] // BLK):
            inside = (block >= band_ref[0, b]) & (block <= band_ref[1, b])
            bias_ref[:, b * BLK : (b + 1) * BLK] = jnp.where(inside, 0.0, -jnp.inf)

    scale2 = SCALE * LOG2E
    frames = q_ref.shape[0]
    nt = kvo_ref.shape[1]
    step = 256
    blocks = 3 * nt // BLK
    keys = jnp.concatenate([kvo_ref[0], kvn_ref[0], kvf_ref[0]], axis=0)
    values = jnp.concatenate([kvo_ref[1], kvn_ref[1], kvf_ref[1]], axis=0)
    for f in range(frames // step):
        cols = slice(f * step, (f + 1) * step)
        s = dot(keys, q_ref[cols, :], NT)
        gp = dot(values, g_ref[cols, :], NT)
        rows = [slice(j * BLK, (j + 1) * BLK) for j in range(blocks)]
        bias = [bias_ref[j : j + 1, cols] for j in range(blocks)]
        peak = None
        for j in range(blocks):
            top = jnp.max(s[rows[j]], axis=0, keepdims=True) + bias[j]
            peak = top if peak is None else jnp.maximum(peak, top)
        expos = []
        total = jnp.zeros((1, step), F32)
        mixed = jnp.zeros((1, step), F32)
        for j in range(blocks):
            e = jnp.exp2(s[rows[j]] * scale2 + (bias[j] - peak) * scale2)
            expos.append(e)
            total = total + jnp.sum(e, axis=0, keepdims=True)
            mixed = mixed + jnp.sum(e * gp[rows[j]], axis=0, keepdims=True)
        inv = 1.0 / total
        delta = mixed * inv
        for j in range(blocks):
            p = expos[j] * inv
            p_scr[rows[j], cols] = p.astype(BF16)
            ds_scr[rows[j], cols] = (p * (gp[rows[j]] - delta)).astype(BF16)
    dq_ref[...] = (dot(ds_scr[...], keys, TN) * SCALE).astype(BF16)
    dv = dot(p_scr[...], g_ref[...], NN)
    dk = dot(ds_scr[...], q_ref[...], NN) * SCALE
    for i, grad in enumerate((dk, dv)):
        own_ref[i] = grad[:nt]
        near_ref[i] = grad[nt : 2 * nt].astype(BF16)
        far_ref[i] = grad[2 * nt :].astype(BF16)


def attention(scalars, band, queries, grad_ctx, kv_own, kv_near, kv_far, h0, hc, after):
    frames = queries.shape[0]
    nt = kv_own.shape[1]
    frame_in = pl.BlockSpec((frames, HD), lambda h, s, b: (0, h0 + h))
    note_io = pl.BlockSpec((2, nt, HD), lambda h, s, b: (0, 0, h))
    notes_out = jax.ShapeDtypeStruct((2, nt, hc * HD), BF16)
    return call(
        attention_body,
        (hc,),
        [frame_in, frame_in, note_io, note_io, note_io],
        [pl.BlockSpec((frames, HD), lambda h, s, b: (0, h)), note_io, note_io, note_io],
        [
            jax.ShapeDtypeStruct((frames, hc * HD), BF16),
            jax.ShapeDtypeStruct((2, nt, hc * HD), F32),
            notes_out,
            notes_out,
        ],
        (scalars, band, queries, grad_ctx, kv_own, kv_near, kv_far),
        "attention",
        after,
        scalars=2,
        scratch=[
            pltpu.VMEM((3 * nt, frames), BF16),
            pltpu.VMEM((3 * nt, frames), BF16),
            pltpu.VMEM((8, frames), F32),
        ],
        flops=90 * frames * nt * hc * HD if h0 else 0,
    )


def per_device(notes, frames, w_query, w_key, w_value, w_out, band_blocks, grad_mixed):
    shard = lax.axis_index("seq")
    group = lax.axis_index("head")
    core = shard % 2
    scalars = jnp.stack([group, core, shard]).astype(jnp.int32)
    band = band_blocks[0]

    *made, given = key_values(scalars, notes[0], w_key, w_value, w_query)
    moved = [section_shift(kv, 1) for kv in made]
    w_other = other_columns(given)
    queries, grad_ctx = project(frames[0], w_query, grad_mixed[0], w_out, (given,))
    moved[0], queries = lax.optimization_barrier((moved[0], queries))

    grad_q = []
    grad_q_other = []
    note_cols = []
    summed_all = []

    def send_back(own, near, far, also=None):
        near = near_swap(near)
        far = far_swap(far)
        if also:
            near, also[-1] = lax.optimization_barrier((near, also[-1]))
        summed_all.append((own + near.astype(F32) + far.astype(F32)).astype(BF16))
        note_cols.append(section_shift(summed_all[-1], -1))

    for step, (h0, hc) in enumerate(CHUNKS):
        kv = moved[step]
        after = grad_q[-1:]
        kv_near, kv_far = near_swap(kv), far_swap(kv)
        if step == 0:
            kv_far, moved[1] = lax.optimization_barrier((kv_far, moved[1]))
        if step == 1:
            near, far, kv_near, kv_far = lax.optimization_barrier((near, far, kv_near, kv_far))
            send_back(own, near, far)
        if step == 2:
            after = after + [grad_q_other[0], summed_all[0]]
        dq, own, near, far = attention(
            scalars, band, queries, grad_ctx, kv, kv_near, kv_far, h0, hc, after
        )
        if step == 0:
            moved[2], dq = lax.optimization_barrier((moved[2], dq))
        grad_q.append(dq)
        grad_q_other.append(head_swap(dq))
        if step == 1:
            send_back(own, near, far, grad_q_other)
    near, far, note_cols[0] = lax.optimization_barrier((near, far, note_cols[0]))
    send_back(own, near, far)

    total = frame_sum_own(
        scalars, grad_q, grad_q_other[:-1], w_query, w_other, CHUNKS[:-1], ()
    )
    before = note_product(scalars, note_cols[:-1], CHUNKS[:-1], w_key, w_value, (total, grad_q_other[-1]))
    last = (scalars, note_cols[-1:], CHUNKS[-1:], w_key, w_value)
    give_notes = note_product(*last, (), before, (0,))
    notes_other = head_swap(give_notes)
    keep_notes = note_product(*last, (give_notes,), before, (1,))
    frame_sum = frame_sum_last(
        scalars, total, grad_q_other[-1], w_other, *CHUNKS[-1], (keep_notes,)
    )
    note_sum = keep_notes[0].astype(F32) + notes_other[0].astype(F32)
    return (frame_sum[None], note_sum.astype(BF16)[None])


def solution(mesh):
    placed = (
        P("section", "seq", None),
        P("section", "seq", None),
        P(None, "head"),
        P(None, "head"),
        P(None, "head"),
        P("head", None),
        P("section", None, "seq"),
        P("section", "seq", None),
    )
    return jax.shard_map(
        per_device,
        mesh=mesh,
        in_specs=placed,
        out_specs=(P("section", "seq", "head"), P("section", "seq", "head")),
        check_vma=False,
    )
```

```python
import jax
import jax.numpy as jnp
from jax import lax
from jax.experimental import pallas as pl
from jax.experimental.pallas import tpu as pltpu
from jax.sharding import PartitionSpec as P

D = 2048
HEADS = 16
BLK = 128
HD = D // HEADS
SCALE = HD**-0.5
LOG2E = 1.4426950408889634
CHUNKS = ((0, 4), (4, 4))
VMEM = 64 * 2**20 - 2**16

F32 = jnp.float32
BF16 = jnp.bfloat16
NN = (((1,), (0,)), ((), ()))
NT = (((1,), (1,)), ((), ()))
TN = (((0,), (0,)), ((), ()))


def dot(a, b, dims):
    return lax.dot_general(a, b, dims, preferred_element_type=F32)


def section_shift(block, distance):
    count = lax.axis_size("section")
    return lax.ppermute(
        block, "section", [(i, (i + distance) % count) for i in range(count)]
    )


def near_swap(block):
    count = lax.axis_size("seq")
    return lax.ppermute(block, "seq", [(i, i ^ 1) for i in range(count)])


def far_swap(block):
    count = lax.axis_size("seq")
    pairs = [(i, i + 1) for i in range(1, count - 1, 2)]
    return lax.ppermute(block, "seq", pairs + [(j, i) for i, j in pairs])


def head_swap(block):
    return lax.ppermute(block, "head", [(0, 1), (1, 0)])


def other_columns(give):
    count = lax.axis_size("seq")
    quads = [
        [2 * i, 2 * i + 2, 2 * (i ^ 8) + 1, 2 * (i ^ 8) + 3] for i in range(0, count, 2)
    ]
    return lax.all_gather(give, ("seq", "head"), axis_index_groups=quads)


def call(
    body, grid, in_specs, out_specs, out_shape, args, name, after=(), scalars=0, scratch=(),
    flops=0,
):
    first = scalars + len(in_specs)
    unread = len(after)

    def reads(*refs):
        body(*refs[:first], *refs[first + unread :])

    in_specs = list(in_specs) + [pl.BlockSpec(memory_space=pl.ANY)] * unread
    return pl.pallas_call(
        reads,
        grid_spec=pltpu.PrefetchScalarGridSpec(
            num_scalar_prefetch=scalars,
            grid=grid,
            in_specs=in_specs,
            out_specs=out_specs,
            scratch_shapes=scratch,
        ),
        out_shape=out_shape,
        compiler_params=pltpu.CompilerParams(vmem_limit_bytes=VMEM),
        cost_estimate=pl.CostEstimate(flops=flops, bytes_accessed=0, transcendentals=0),
        name=name,
    )(*args, *after)


def key_values(scalars, notes, w_key, w_value, w_query):
    rows = notes.shape[0]
    cols = w_key.shape[1]
    wide = 2 * HD
    pieces = cols // wide
    quarter = D // 4

    def body(s_ref, notes_ref, wk_ref, wv_ref, wq_ref, *refs):
        outs = refs[: len(CHUNKS)]
        give_ref, wk_scr, wv_scr, wq_scr, *made_scr, sems, out_sems, give_sems = refs[len(CHUNKS) :]
        copies = []
        for p in range(pieces):
            part = slice(p * wide, (p + 1) * wide)
            for i, (src, dst) in enumerate(((wk_ref, wk_scr), (wv_ref, wv_scr))):
                copy = pltpu.make_async_copy(src.at[:, part], dst.at[:, part], sems.at[p, i])
                copy.start()
                copies.append(copy)
        offset = pl.multiple_of((1 - s_ref[0]) * (2 * quarter) + s_ref[1] * quarter, quarter)
        take = pltpu.make_async_copy(wq_ref.at[pl.ds(offset, quarter), :], wq_scr, give_sems.at[0])
        take.start()
        left = notes_ref[...]
        sent = []
        for p in range(pieces):
            part = slice(p * wide, (p + 1) * wide)
            for i, scr in enumerate((wk_scr, wv_scr)):
                copies[2 * p + i].wait()
                made = dot(left, scr[:, part], NN).astype(BF16)
                for k in range(2):
                    head = 2 * p + k
                    for c, (h0, hc) in enumerate(CHUNKS):
                        if h0 <= head < h0 + hc:
                            at = (head - h0) * HD
                            made_scr[c][i, :, at : at + HD] = made[:, k * HD : (k + 1) * HD]
                        if i == 1 and head == h0 + hc - 1:
                            out = pltpu.make_async_copy(made_scr[c], outs[c], out_sems.at[c])
                            out.start()
                            sent.append(out)
        take.wait()
        give = pltpu.make_async_copy(wq_scr, give_ref, give_sems.at[1])
        give.start()
        for copy in sent + [give]:
            copy.wait()

    far = pl.BlockSpec(memory_space=pl.ANY)
    here = pl.BlockSpec(memory_space=pltpu.VMEM)
    return call(
        body,
        (),
        [here, far, far, far],
        [far] * (len(CHUNKS) + 1),
        [jax.ShapeDtypeStruct((2, rows, hc * HD), BF16) for _, hc in CHUNKS]
        + [jax.ShapeDtypeStruct((quarter, cols), BF16)],
        (scalars, notes, w_key, w_value, w_query),
        "key_values",
        scalars=1,
        scratch=[
            pltpu.VMEM((D, cols), BF16),
            pltpu.VMEM((D, cols), BF16),
            pltpu.VMEM((quarter, cols), BF16),
            *[pltpu.VMEM((2, rows, hc * HD), BF16) for _, hc in CHUNKS],
            pltpu.SemaphoreType.DMA((pieces, 2)),
            pltpu.SemaphoreType.DMA((len(CHUNKS),)),
            pltpu.SemaphoreType.DMA((2,)),
        ],
    )


def project(frames, w_query, grad_mixed, w_out, after):
    rows, depth = frames.shape
    width = w_query.shape[1]
    step = 256
    steps = rows // step
    parts = 4

    def body(a_ref, w_ref, b_ref, v_ref, q_ref, g_ref, a_scr, w_scr, b_scr, v_scr, q_scr, g_scr,
             w_sems, row_sems, out_sems):
        waits = []
        for i, (rows_ref, rows_scr, weight_ref, weight_scr) in enumerate(
            ((a_ref, a_scr, w_ref, w_scr), (b_ref, b_scr, v_ref, v_scr))
        ):
            size = weight_ref.shape[0] // parts
            weight_copies = []
            row_copies = []
            for p in range(parts):
                at = slice(p * size, (p + 1) * size)
                copy = pltpu.make_async_copy(weight_ref.at[at], weight_scr.at[at], w_sems.at[i, p])
                copy.start()
                weight_copies.append(copy)
            for m in range(steps):
                at = slice(m * step, (m + 1) * step)
                copy = pltpu.make_async_copy(rows_ref.at[at], rows_scr.at[at], row_sems.at[i, m])
                copy.start()
                row_copies.append(copy)
            waits.append((weight_copies, row_copies))
        sent = []
        for i, (rows_scr, weight_scr, out_scr, out_ref, dims) in enumerate(
            ((a_scr, w_scr, q_scr, q_ref, NN), (b_scr, v_scr, g_scr, g_ref, NT))
        ):
            for copy in waits[i][0]:
                copy.wait()
            for m in range(steps):
                at = slice(m * step, (m + 1) * step)
                waits[i][1][m].wait()
                out_scr[at, :] = dot(rows_scr[at, :], weight_scr[...], dims).astype(BF16)
                copy = pltpu.make_async_copy(out_scr.at[at], out_ref.at[at], out_sems.at[i, m])
                copy.start()
                sent.append(copy)
        for copy in sent:
            copy.wait()

    far = pl.BlockSpec(memory_space=pl.ANY)
    out = jax.ShapeDtypeStruct((rows, width), BF16)
    return call(
        body,
        (),
        [far] * 4,
        [far] * 2,
        [out, out],
        (frames, w_query, grad_mixed, w_out),
        "queries_and_grad_ctx",
        after,
        scratch=[
            pltpu.VMEM(frames.shape, BF16),
            pltpu.VMEM(w_query.shape, BF16),
            pltpu.VMEM(grad_mixed.shape, BF16),
            pltpu.VMEM(w_out.shape, BF16),
            pltpu.VMEM((rows, width), BF16),
            pltpu.VMEM((rows, width), BF16),
            pltpu.SemaphoreType.DMA((2, parts)),
            pltpu.SemaphoreType.DMA((2, steps)),
            pltpu.SemaphoreType.DMA((2, steps)),
        ],
    )


def frame_sum(scalars, grads, grads_other, w_query, w_other, after):
    rows = grads[0].shape[0]
    half = D // 2
    cols = w_query.shape[1]
    quarter = half // 2
    step = 256
    steps = rows // step
    terms = len(grads) * 2
    widths = [g.shape[1] for g in grads] * 2

    def body(s_ref, *refs):
        grad_refs, refs = refs[:terms], refs[terms:]
        wq_ref, wo_ref, out_ref, w_scr, o_scr, *refs = refs
        grad_scrs, refs = refs[:terms], refs[terms:]
        w_sems, grad_sems, out_sems = refs
        weight_copies = []
        for p in range(2):
            at = pl.ds(pl.multiple_of(s_ref[0] * half + p * quarter, quarter), quarter)
            to = slice(p * quarter, (p + 1) * quarter)
            weight_copies.append(
                pltpu.make_async_copy(wq_ref.at[at], w_scr.at[0, to], w_sems.at[0, p])
            )
            weight_copies.append(
                pltpu.make_async_copy(wo_ref.at[2 * (1 - s_ref[0]) + p], w_scr.at[1, to], w_sems.at[1, p])
            )
        for copy in weight_copies:
            copy.start()
        grad_copies = []
        for m in range(steps):
            at = slice(m * step, (m + 1) * step)
            for t in range(terms):
                copy = pltpu.make_async_copy(grad_refs[t].at[at], grad_scrs[t].at[at], grad_sems.at[m, t])
                copy.start()
                grad_copies.append(copy)
        for copy in weight_copies:
            copy.wait()
        sent = []
        for m in range(steps):
            at = slice(m * step, (m + 1) * step)
            total = None
            for group in range(2):
                first = group * len(grads)
                for t in range(first, first + len(grads)):
                    grad_copies[m * terms + t].wait()
                left = jnp.concatenate(
                    [grad_scrs[t][at, :] for t in range(first, first + len(grads))], axis=1
                )
                term = dot(left, w_scr[group], NT)
                total = term if total is None else total + term
            o_scr[at, :] = total.astype(BF16)
            copy = pltpu.make_async_copy(o_scr.at[at], out_ref.at[at], out_sems.at[m])
            copy.start()
            sent.append(copy)
        for copy in sent:
            copy.wait()

    far = pl.BlockSpec(memory_space=pl.ANY)
    return call(
        body,
        (),
        [far] * (terms + 2),
        far,
        jax.ShapeDtypeStruct((rows, half), BF16),
        (scalars, *grads, *grads_other, w_query, w_other),
        "frame_sum",
        after,
        scalars=1,
        scratch=[
            pltpu.VMEM((2, half, cols), BF16),
            pltpu.VMEM((rows, half), BF16),
            *[pltpu.VMEM((rows, width), BF16) for width in widths],
            pltpu.SemaphoreType.DMA((2, 2)),
            pltpu.SemaphoreType.DMA((steps, terms)),
            pltpu.SemaphoreType.DMA((steps,)),
        ],
    )


def note_product(scalars, grads, chunks, w_key, w_value, after, before=None, which=(0, 1)):
    nt = grads[0].shape[1]
    half = D // 2
    heads = [h for h0, hc in chunks for h in range(h0, h0 + hc)]
    hc = len(heads)
    last = before is not None
    start = which[0]

    def body(s_ref, *refs):
        grad_refs, refs = refs[: len(grads)], refs[len(grads) :]
        wk = jnp.concatenate([r[...] for r in refs[:hc]], axis=1)
        wv = jnp.concatenate([r[...] for r in refs[hc : 2 * hc]], axis=1)
        gk = jnp.concatenate([r[0] for r in grad_refs], axis=1)
        gv = jnp.concatenate([r[1] for r in grad_refs], axis=1)
        total = dot(gk, wk, NT) + dot(gv, wv, NT)
        if last:
            total = total + refs[2 * hc][0]
        out_ref = refs[-1]
        out_ref[0] = total.astype(out_ref.dtype)

    def weight_in(h):
        return pl.BlockSpec(
            (half, HD), lambda n, s: (jnp.where(n + start == 0, 1 - s[0], s[0]), h)
        )

    return call(
        body,
        (len(which),),
        [pl.BlockSpec(g.shape, lambda n, s: (0, 0, 0)) for g in grads]
        + [weight_in(h) for h in heads] * 2
        + ([pl.BlockSpec((1, nt, half), lambda n, s: (n + start, 0, 0))] if last else []),
        pl.BlockSpec((1, nt, half), lambda n, s: (n, 0, 0)),
        jax.ShapeDtypeStruct((len(which), nt, half), BF16 if last else F32),
        (scalars, *grads) + (w_key,) * hc + (w_value,) * hc + ((before,) if last else ()),
        "note_product",
        after,
        scalars=1,
    )


def attention_body(
    s_ref, band_ref, q_ref, g_ref, kvo_ref, kvn_ref, kvf_ref, dq_ref, own_ref, near_ref, far_ref,
    p_scr, ds_scr, bias_ref,
):
    @pl.when(pl.program_id(0) == 0)
    def _():
        row = lax.broadcasted_iota(jnp.int32, (8, BLK), 0)
        shard = s_ref[2]
        far = shard - 1 + 2 * s_ref[1]
        block = jnp.where(row < 2, 2 * shard, jnp.where(row < 4, 2 * (shard ^ 1), 2 * far)) + row % 2
        for b in range(q_ref.shape[0] // BLK):
            inside = (block >= band_ref[0, b]) & (block <= band_ref[1, b])
            bias_ref[:, b * BLK : (b + 1) * BLK] = jnp.where(inside, 0.0, -jnp.inf)

    scale2 = SCALE * LOG2E
    frames = q_ref.shape[0]
    nt = kvo_ref.shape[1]
    step = 256
    blocks = 3 * nt // BLK
    keys = jnp.concatenate([kvo_ref[0], kvn_ref[0], kvf_ref[0]], axis=0)
    values = jnp.concatenate([kvo_ref[1], kvn_ref[1], kvf_ref[1]], axis=0)
    for f in range(frames // step):
        cols = slice(f * step, (f + 1) * step)
        s = dot(keys, q_ref[cols, :], NT)
        gp = dot(values, g_ref[cols, :], NT)
        rows = [slice(j * BLK, (j + 1) * BLK) for j in range(blocks)]
        bias = [bias_ref[j : j + 1, cols] for j in range(blocks)]
        peak = None
        for j in range(blocks):
            top = jnp.max(s[rows[j]], axis=0, keepdims=True) + bias[j]
            peak = top if peak is None else jnp.maximum(peak, top)
        expos = []
        total = jnp.zeros((1, step), F32)
        mixed = jnp.zeros((1, step), F32)
        for j in range(blocks):
            e = jnp.exp2(s[rows[j]] * scale2 + (bias[j] - peak) * scale2)
            expos.append(e)
            total = total + jnp.sum(e, axis=0, keepdims=True)
            mixed = mixed + jnp.sum(e * gp[rows[j]], axis=0, keepdims=True)
        inv = 1.0 / total
        delta = mixed * inv
        for j in range(blocks):
            p = expos[j] * inv
            p_scr[rows[j], cols] = p.astype(BF16)
            ds_scr[rows[j], cols] = (p * (gp[rows[j]] - delta)).astype(BF16)
    dq_ref[...] = (dot(ds_scr[...], keys, TN) * SCALE).astype(BF16)
    dv = dot(p_scr[...], g_ref[...], NN)
    dk = dot(ds_scr[...], q_ref[...], NN) * SCALE
    for i, grad in enumerate((dk, dv)):
        own_ref[i] = grad[:nt]
        near_ref[i] = grad[nt : 2 * nt].astype(BF16)
        far_ref[i] = grad[2 * nt :].astype(BF16)


def attention(scalars, band, queries, grad_ctx, kv_own, kv_near, kv_far, h0, hc, after):
    frames = queries.shape[0]
    nt = kv_own.shape[1]
    frame_in = pl.BlockSpec((frames, HD), lambda h, s, b: (0, h0 + h))
    note_io = pl.BlockSpec((2, nt, HD), lambda h, s, b: (0, 0, h))
    notes_out = jax.ShapeDtypeStruct((2, nt, hc * HD), BF16)
    return call(
        attention_body,
        (hc,),
        [frame_in, frame_in, note_io, note_io, note_io],
        [pl.BlockSpec((frames, HD), lambda h, s, b: (0, h)), note_io, note_io, note_io],
        [
            jax.ShapeDtypeStruct((frames, hc * HD), BF16),
            jax.ShapeDtypeStruct((2, nt, hc * HD), F32),
            notes_out,
            notes_out,
        ],
        (scalars, band, queries, grad_ctx, kv_own, kv_near, kv_far),
        "attention",
        after,
        scalars=2,
        scratch=[
            pltpu.VMEM((3 * nt, frames), BF16),
            pltpu.VMEM((3 * nt, frames), BF16),
            pltpu.VMEM((8, frames), F32),
        ],
        flops=90 * frames * nt * hc * HD if h0 else 0,
    )


def per_device(notes, frames, w_query, w_key, w_value, w_out, band_blocks, grad_mixed):
    shard = lax.axis_index("seq")
    group = lax.axis_index("head")
    core = shard % 2
    scalars = jnp.stack([group, core, shard]).astype(jnp.int32)
    band = band_blocks[0]

    *made, given = key_values(scalars, notes[0], w_key, w_value, w_query)
    moved = [section_shift(kv, 1) for kv in made]
    w_other = other_columns(given)
    queries, grad_ctx = project(frames[0], w_query, grad_mixed[0], w_out, (given,))
    moved[0], queries = lax.optimization_barrier((moved[0], queries))

    def attend(step, near, far, after):
        return attention(
            scalars, band, queries, grad_ctx, moved[step], near, far, *CHUNKS[step], after
        )

    def note_sum_of(own, near, far):
        return (own + near.astype(F32) + far.astype(F32)).astype(BF16)

    near0, far0 = near_swap(moved[0]), far_swap(moved[0])
    far0, moved[1] = lax.optimization_barrier((far0, moved[1]))
    near1, far1 = near_swap(moved[1]), far_swap(moved[1])
    dq0, own0, rim_near0, rim_far0 = attend(0, near0, far0, ())
    dq0_other = head_swap(dq0)
    rim_near0, rim_far0, near1, far1 = lax.optimization_barrier((rim_near0, rim_far0, near1, far1))
    in_near0, in_far0 = near_swap(rim_near0), far_swap(rim_far0)
    dq1, own1, rim_near1, rim_far1 = attend(1, near1, far1, (dq0,))
    dq1_other = head_swap(dq1)
    in_near0, in_far0, rim_near1, rim_far1 = lax.optimization_barrier(
        (in_near0, in_far0, rim_near1, rim_far1)
    )
    in_near1, in_far1 = near_swap(rim_near1), far_swap(rim_far1)
    notes0 = section_shift(note_sum_of(own0, in_near0, in_far0), -1)
    in_near1, dq0_other = lax.optimization_barrier((in_near1, dq0_other))
    notes1 = section_shift(note_sum_of(own1, in_near1, in_far1), -1)

    before = note_product(scalars, [notes0], CHUNKS[:1], w_key, w_value, ())
    last = (scalars, [notes1], CHUNKS[1:], w_key, w_value)
    give_notes = note_product(*last, (dq1_other,), before, (0,))
    notes_other = head_swap(give_notes)
    keep_notes = note_product(*last, (give_notes,), before, (1,))
    frame_out = frame_sum(
        scalars, [dq0, dq1], [dq0_other, dq1_other], w_query, w_other, (keep_notes,)
    )
    notes_other, frame_out = lax.optimization_barrier((notes_other, frame_out))
    note_out = keep_notes[0].astype(F32) + notes_other[0].astype(F32)
    return (frame_out[None], note_out.astype(BF16)[None])


def solution(mesh):
    placed = (
        P("section", "seq", None),
        P("section", "seq", None),
        P(None, "head"),
        P(None, "head"),
        P(None, "head"),
        P("head", None),
        P("section", None, "seq"),
        P("section", "seq", None),
    )
    return jax.shard_map(
        per_device,
        mesh=mesh,
        in_specs=placed,
        out_specs=(P("section", "seq", "head"), P("section", "seq", "head")),
        check_vma=False,
    )
```

```python
import jax
import jax.numpy as jnp
from jax import lax
from jax.experimental import pallas as pl
from jax.experimental.pallas import tpu as pltpu
from jax.sharding import PartitionSpec as P

D = 2048
HEADS = 16
BLK = 128
HD = D // HEADS
SCALE = HD**-0.5
LOG2E = 1.4426950408889634
CHUNKS = ((0, 4), (4, 4))
VMEM = 64 * 2**20 - 2**16

F32 = jnp.float32
BF16 = jnp.bfloat16
NN = (((1,), (0,)), ((), ()))
NT = (((1,), (1,)), ((), ()))
TN = (((0,), (0,)), ((), ()))


def dot(a, b, dims):
    return lax.dot_general(a, b, dims, preferred_element_type=F32)


def section_shift(block, distance):
    count = lax.axis_size("section")
    return lax.ppermute(
        block, "section", [(i, (i + distance) % count) for i in range(count)]
    )


def near_swap(block):
    count = lax.axis_size("seq")
    return lax.ppermute(block, "seq", [(i, i ^ 1) for i in range(count)])


def far_swap(block):
    count = lax.axis_size("seq")
    pairs = [(i, i + 1) for i in range(1, count - 1, 2)]
    return lax.ppermute(block, "seq", pairs + [(j, i) for i, j in pairs])


def head_swap(block):
    return lax.ppermute(block, "head", [(0, 1), (1, 0)])


def across(block):
    count = lax.axis_size("seq")
    route = [(2 * i + g, 2 * (i ^ 8) + 1 - g) for i in range(count) for g in range(2)]
    return lax.ppermute(block, ("seq", "head"), route)


def call(
    body, grid, in_specs, out_specs, out_shape, args, name, after=(), scalars=0, scratch=(),
    flops=0,
):
    first = scalars + len(in_specs)
    unread = len(after)

    def reads(*refs):
        body(*refs[:first], *refs[first + unread :])

    in_specs = list(in_specs) + [pl.BlockSpec(memory_space=pl.ANY)] * unread
    return pl.pallas_call(
        reads,
        grid_spec=pltpu.PrefetchScalarGridSpec(
            num_scalar_prefetch=scalars,
            grid=grid,
            in_specs=in_specs,
            out_specs=out_specs,
            scratch_shapes=scratch,
        ),
        out_shape=out_shape,
        compiler_params=pltpu.CompilerParams(vmem_limit_bytes=VMEM),
        cost_estimate=pl.CostEstimate(flops=flops, bytes_accessed=0, transcendentals=0),
        name=name,
    )(*args, *after)


def key_values(scalars, notes, w_key, w_value, w_query, h0, hc, give, after):
    rows = notes.shape[0]
    cols = w_query.shape[1]
    wide = 2 * HD
    pieces = hc * HD // wide
    quarter = D // 4

    def body(s_ref, notes_ref, wk_ref, wv_ref, wq_ref, *refs):
        if give:
            out_ref, give_ref, wk_scr, wv_scr, out_scr, sems, out_sem, wq_scr, give_sems = refs
        else:
            out_ref, wk_scr, wv_scr, out_scr, sems, out_sem = refs
        copies = []
        for p in range(pieces):
            part = slice(h0 * HD + p * wide, h0 * HD + (p + 1) * wide)
            to = slice(p * wide, (p + 1) * wide)
            for i, (src, dst) in enumerate(((wk_ref, wk_scr), (wv_ref, wv_scr))):
                copy = pltpu.make_async_copy(src.at[:, part], dst.at[:, to], sems.at[p, i])
                copy.start()
                copies.append(copy)
        if give:
            offset = pl.multiple_of((1 - s_ref[0]) * (2 * quarter) + s_ref[1] * quarter, quarter)
            take = pltpu.make_async_copy(
                wq_ref.at[pl.ds(offset, quarter), :], wq_scr, give_sems.at[0]
            )
            take.start()
        left = notes_ref[...]
        for p in range(pieces):
            to = slice(p * wide, (p + 1) * wide)
            for i, scr in enumerate((wk_scr, wv_scr)):
                copies[2 * p + i].wait()
                out_scr[i, :, to] = dot(left, scr[:, to], NN).astype(BF16)
        sent = [pltpu.make_async_copy(out_scr, out_ref, out_sem)]
        if give:
            take.wait()
            sent.append(pltpu.make_async_copy(wq_scr, give_ref, give_sems.at[1]))
        for copy in sent:
            copy.start()
        for copy in sent:
            copy.wait()

    far = pl.BlockSpec(memory_space=pl.ANY)
    here = pl.BlockSpec(memory_space=pltpu.VMEM)
    out = jax.ShapeDtypeStruct((2, rows, hc * HD), BF16)
    given = jax.ShapeDtypeStruct((quarter, cols), BF16)
    return call(
        body,
        (),
        [here, far, far, far],
        [far, far] if give else far,
        [out, given] if give else out,
        (scalars, notes, w_key, w_value, w_query),
        "key_values",
        after,
        scalars=1,
        scratch=[
            pltpu.VMEM((D, hc * HD), BF16),
            pltpu.VMEM((D, hc * HD), BF16),
            pltpu.VMEM((2, rows, hc * HD), BF16),
            pltpu.SemaphoreType.DMA((pieces, 2)),
            pltpu.SemaphoreType.DMA,
        ]
        + ([pltpu.VMEM((quarter, cols), BF16), pltpu.SemaphoreType.DMA((2,))] if give else []),
    )


def project(frames, w_query, grad_mixed, w_out, after):
    rows, depth = frames.shape
    width = w_query.shape[1]
    step = 256
    steps = rows // step
    parts = 4

    def body(a_ref, w_ref, b_ref, v_ref, q_ref, g_ref, a_scr, w_scr, b_scr, v_scr, q_scr, g_scr,
             w_sems, row_sems, out_sems):
        waits = []
        for i, (rows_ref, rows_scr, weight_ref, weight_scr) in enumerate(
            ((a_ref, a_scr, w_ref, w_scr), (b_ref, b_scr, v_ref, v_scr))
        ):
            size = weight_ref.shape[0] // parts
            weight_copies = []
            row_copies = []
            for p in range(parts):
                at = slice(p * size, (p + 1) * size)
                copy = pltpu.make_async_copy(weight_ref.at[at], weight_scr.at[at], w_sems.at[i, p])
                copy.start()
                weight_copies.append(copy)
            for m in range(steps):
                at = slice(m * step, (m + 1) * step)
                copy = pltpu.make_async_copy(rows_ref.at[at], rows_scr.at[at], row_sems.at[i, m])
                copy.start()
                row_copies.append(copy)
            waits.append((weight_copies, row_copies))
        sent = []
        for i, (rows_scr, weight_scr, out_scr, out_ref, dims) in enumerate(
            ((a_scr, w_scr, q_scr, q_ref, NN), (b_scr, v_scr, g_scr, g_ref, NT))
        ):
            for copy in waits[i][0]:
                copy.wait()
            for m in range(steps):
                at = slice(m * step, (m + 1) * step)
                waits[i][1][m].wait()
                out_scr[at, :] = dot(rows_scr[at, :], weight_scr[...], dims).astype(BF16)
                copy = pltpu.make_async_copy(out_scr.at[at], out_ref.at[at], out_sems.at[i, m])
                copy.start()
                sent.append(copy)
        for copy in sent:
            copy.wait()

    far = pl.BlockSpec(memory_space=pl.ANY)
    out = jax.ShapeDtypeStruct((rows, width), BF16)
    return call(
        body,
        (),
        [far] * 4,
        [far] * 2,
        [out, out],
        (frames, w_query, grad_mixed, w_out),
        "queries_and_grad_ctx",
        after,
        scratch=[
            pltpu.VMEM(frames.shape, BF16),
            pltpu.VMEM(w_query.shape, BF16),
            pltpu.VMEM(grad_mixed.shape, BF16),
            pltpu.VMEM(w_out.shape, BF16),
            pltpu.VMEM((rows, width), BF16),
            pltpu.VMEM((rows, width), BF16),
            pltpu.SemaphoreType.DMA((2, parts)),
            pltpu.SemaphoreType.DMA((2, steps)),
            pltpu.SemaphoreType.DMA((2, steps)),
        ],
    )


def frame_sum(scalars, grads, grads_other, w_query, w_mine, w_theirs, after):
    rows = grads[0].shape[0]
    half = D // 2
    cols = w_query.shape[1]
    quarter = half // 2
    step = 256
    steps = rows // step
    terms = len(grads) * 2
    widths = [g.shape[1] for g in grads] * 2

    def body(s_ref, *refs):
        grad_refs, refs = refs[:terms], refs[terms:]
        wq_ref, mine_ref, theirs_ref, out_ref, w_scr, o_scr, *refs = refs
        grad_scrs, refs = refs[:terms], refs[terms:]
        w_sems, grad_sems, out_sems = refs
        weight_copies = []
        for p in range(2):
            at = pl.ds(pl.multiple_of(s_ref[0] * half + p * quarter, quarter), quarter)
            to = slice(p * quarter, (p + 1) * quarter)
            weight_copies.append(
                pltpu.make_async_copy(wq_ref.at[at], w_scr.at[0, to], w_sems.at[0, p])
            )
            src, core = (mine_ref, s_ref[1]) if p == 0 else (theirs_ref, 1 - s_ref[1])
            to = pl.ds(pl.multiple_of(core * quarter, quarter), quarter)
            weight_copies.append(pltpu.make_async_copy(src, w_scr.at[1, to], w_sems.at[1, p]))
        for copy in weight_copies:
            copy.start()
        grad_copies = []
        for m in range(steps):
            at = slice(m * step, (m + 1) * step)
            for t in range(terms):
                copy = pltpu.make_async_copy(grad_refs[t].at[at], grad_scrs[t].at[at], grad_sems.at[m, t])
                copy.start()
                grad_copies.append(copy)
        for copy in weight_copies:
            copy.wait()
        sent = []
        for m in range(steps):
            at = slice(m * step, (m + 1) * step)
            total = None
            for group in range(2):
                first = group * len(grads)
                for t in range(first, first + len(grads)):
                    grad_copies[m * terms + t].wait()
                left = jnp.concatenate(
                    [grad_scrs[t][at, :] for t in range(first, first + len(grads))], axis=1
                )
                term = dot(left, w_scr[group], NT)
                total = term if total is None else total + term
            o_scr[at, :] = total.astype(BF16)
            copy = pltpu.make_async_copy(o_scr.at[at], out_ref.at[at], out_sems.at[m])
            copy.start()
            sent.append(copy)
        for copy in sent:
            copy.wait()

    far = pl.BlockSpec(memory_space=pl.ANY)
    return call(
        body,
        (),
        [far] * (terms + 3),
        far,
        jax.ShapeDtypeStruct((rows, half), BF16),
        (scalars, *grads, *grads_other, w_query, w_mine, w_theirs),
        "frame_sum",
        after,
        scalars=1,
        scratch=[
            pltpu.VMEM((2, half, cols), BF16),
            pltpu.VMEM((rows, half), BF16),
            *[pltpu.VMEM((rows, width), BF16) for width in widths],
            pltpu.SemaphoreType.DMA((2, 2)),
            pltpu.SemaphoreType.DMA((steps, terms)),
            pltpu.SemaphoreType.DMA((steps,)),
        ],
    )


def note_product(scalars, grads, chunks, w_key, w_value, after, before=None, which=(0, 1)):
    nt = grads[0].shape[1]
    half = D // 2
    heads = [h for h0, hc in chunks for h in range(h0, h0 + hc)]
    hc = len(heads)
    last = before is not None
    start = which[0]

    def body(s_ref, *refs):
        grad_refs, refs = refs[: len(grads)], refs[len(grads) :]
        wk = jnp.concatenate([r[...] for r in refs[:hc]], axis=1)
        wv = jnp.concatenate([r[...] for r in refs[hc : 2 * hc]], axis=1)
        gk = jnp.concatenate([r[0] for r in grad_refs], axis=1)
        gv = jnp.concatenate([r[1] for r in grad_refs], axis=1)
        total = dot(gk, wk, NT) + dot(gv, wv, NT)
        if last:
            total = total + refs[2 * hc][0]
        out_ref = refs[-1]
        out_ref[0] = total.astype(out_ref.dtype)

    def weight_in(h):
        return pl.BlockSpec(
            (half, HD), lambda n, s: (jnp.where(n + start == 0, 1 - s[0], s[0]), h)
        )

    return call(
        body,
        (len(which),),
        [pl.BlockSpec(g.shape, lambda n, s: (0, 0, 0)) for g in grads]
        + [weight_in(h) for h in heads] * 2
        + ([pl.BlockSpec((1, nt, half), lambda n, s: (n + start, 0, 0))] if last else []),
        pl.BlockSpec((1, nt, half), lambda n, s: (n, 0, 0)),
        jax.ShapeDtypeStruct((len(which), nt, half), BF16 if last else F32),
        (scalars, *grads) + (w_key,) * hc + (w_value,) * hc + ((before,) if last else ()),
        "note_product",
        after,
        scalars=1,
    )


def attention_body(
    s_ref, band_ref, q_ref, g_ref, kvo_ref, kvn_ref, kvf_ref, dq_ref, own_ref, near_ref, far_ref,
    p_scr, ds_scr, bias_ref,
):
    @pl.when(pl.program_id(0) == 0)
    def _():
        row = lax.broadcasted_iota(jnp.int32, (8, BLK), 0)
        shard = s_ref[2]
        far = shard - 1 + 2 * s_ref[1]
        block = jnp.where(row < 2, 2 * shard, jnp.where(row < 4, 2 * (shard ^ 1), 2 * far)) + row % 2
        for b in range(q_ref.shape[0] // BLK):
            inside = (block >= band_ref[0, b]) & (block <= band_ref[1, b])
            bias_ref[:, b * BLK : (b + 1) * BLK] = jnp.where(inside, 0.0, -jnp.inf)

    scale2 = SCALE * LOG2E
    frames = q_ref.shape[0]
    nt = kvo_ref.shape[1]
    step = 256
    blocks = 3 * nt // BLK
    keys = jnp.concatenate([kvo_ref[0], kvn_ref[0], kvf_ref[0]], axis=0)
    values = jnp.concatenate([kvo_ref[1], kvn_ref[1], kvf_ref[1]], axis=0)
    for f in range(frames // step):
        cols = slice(f * step, (f + 1) * step)
        s = dot(keys, q_ref[cols, :], NT)
        gp = dot(values, g_ref[cols, :], NT)
        rows = [slice(j * BLK, (j + 1) * BLK) for j in range(blocks)]
        bias = [bias_ref[j : j + 1, cols] for j in range(blocks)]
        peak = None
        for j in range(blocks):
            top = jnp.max(s[rows[j]], axis=0, keepdims=True) + bias[j]
            peak = top if peak is None else jnp.maximum(peak, top)
        expos = []
        total = jnp.zeros((1, step), F32)
        mixed = jnp.zeros((1, step), F32)
        for j in range(blocks):
            e = jnp.exp2(s[rows[j]] * scale2 + (bias[j] - peak) * scale2)
            expos.append(e)
            total = total + jnp.sum(e, axis=0, keepdims=True)
            mixed = mixed + jnp.sum(e * gp[rows[j]], axis=0, keepdims=True)
        inv = 1.0 / total
        delta = mixed * inv
        for j in range(blocks):
            p = expos[j] * inv
            p_scr[rows[j], cols] = p.astype(BF16)
            ds_scr[rows[j], cols] = (p * (gp[rows[j]] - delta)).astype(BF16)
    dq_ref[...] = (dot(ds_scr[...], keys, TN) * SCALE).astype(BF16)
    dv = dot(p_scr[...], g_ref[...], NN)
    dk = dot(ds_scr[...], q_ref[...], NN) * SCALE
    for i, grad in enumerate((dk, dv)):
        own_ref[i] = grad[:nt]
        near_ref[i] = grad[nt : 2 * nt].astype(BF16)
        far_ref[i] = grad[2 * nt :].astype(BF16)


def attention(scalars, band, queries, grad_ctx, kv_own, kv_near, kv_far, h0, hc, after):
    frames = queries.shape[0]
    nt = kv_own.shape[1]
    frame_in = pl.BlockSpec((frames, HD), lambda h, s, b: (0, h0 + h))
    note_io = pl.BlockSpec((2, nt, HD), lambda h, s, b: (0, 0, h))
    notes_out = jax.ShapeDtypeStruct((2, nt, hc * HD), BF16)
    return call(
        attention_body,
        (hc,),
        [frame_in, frame_in, note_io, note_io, note_io],
        [pl.BlockSpec((frames, HD), lambda h, s, b: (0, h)), note_io, note_io, note_io],
        [
            jax.ShapeDtypeStruct((frames, hc * HD), BF16),
            jax.ShapeDtypeStruct((2, nt, hc * HD), F32),
            notes_out,
            notes_out,
        ],
        (scalars, band, queries, grad_ctx, kv_own, kv_near, kv_far),
        "attention",
        after,
        scalars=2,
        scratch=[
            pltpu.VMEM((3 * nt, frames), BF16),
            pltpu.VMEM((3 * nt, frames), BF16),
            pltpu.VMEM((8, frames), F32),
        ],
        flops=90 * frames * nt * hc * HD if h0 else 0,
    )


def per_device(notes, frames, w_query, w_key, w_value, w_out, band_blocks, grad_mixed):
    shard = lax.axis_index("seq")
    group = lax.axis_index("head")
    core = shard % 2
    scalars = jnp.stack([group, core, shard]).astype(jnp.int32)
    band = band_blocks[0]

    arrays = (scalars, notes[0], w_key, w_value, w_query)
    made0 = key_values(*arrays, *CHUNKS[0], False, ())
    made1, given = key_values(*arrays, *CHUNKS[1], True, (made0,))
    moved = [section_shift(made0, 1), section_shift(made1, 1)]
    w_mine = across(given)
    queries, grad_ctx = project(frames[0], w_query, grad_mixed[0], w_out, (given,))
    moved[0], queries = lax.optimization_barrier((moved[0], queries))

    def attend(step, near, far, after):
        return attention(
            scalars, band, queries, grad_ctx, moved[step], near, far, *CHUNKS[step], after
        )

    def note_sum_of(own, near, far):
        return (own + near.astype(F32) + far.astype(F32)).astype(BF16)

    near0, far0 = near_swap(moved[0]), far_swap(moved[0])
    far0, moved[1] = lax.optimization_barrier((far0, moved[1]))
    near1, far1 = near_swap(moved[1]), far_swap(moved[1])
    dq0, own0, rim_near0, rim_far0 = attend(0, near0, far0, ())
    dq0_other = head_swap(dq0)
    w_mine, dq0 = lax.optimization_barrier((w_mine, dq0))
    w_theirs = near_swap(w_mine)
    rim_near0, rim_far0, near1, far1 = lax.optimization_barrier((rim_near0, rim_far0, near1, far1))
    in_near0, in_far0 = near_swap(rim_near0), far_swap(rim_far0)
    dq1, own1, rim_near1, rim_far1 = attend(1, near1, far1, (dq0,))
    dq1_other = head_swap(dq1)
    in_near0, in_far0, rim_near1, rim_far1 = lax.optimization_barrier(
        (in_near0, in_far0, rim_near1, rim_far1)
    )
    in_near1, in_far1 = near_swap(rim_near1), far_swap(rim_far1)
    notes0 = section_shift(note_sum_of(own0, in_near0, in_far0), -1)
    in_near1, dq0_other = lax.optimization_barrier((in_near1, dq0_other))
    notes1 = section_shift(note_sum_of(own1, in_near1, in_far1), -1)

    before = note_product(scalars, [notes0], CHUNKS[:1], w_key, w_value, ())
    last = (scalars, [notes1], CHUNKS[1:], w_key, w_value)
    give_notes = note_product(*last, (dq1_other,), before, (0,))
    notes_other = head_swap(give_notes)
    keep_notes = note_product(*last, (give_notes,), before, (1,))
    frame_out = frame_sum(
        scalars, [dq0, dq1], [dq0_other, dq1_other], w_query, w_mine, w_theirs, (keep_notes,)
    )
    notes_other, frame_out = lax.optimization_barrier((notes_other, frame_out))
    note_out = keep_notes[0].astype(F32) + notes_other[0].astype(F32)
    return (frame_out[None], note_out.astype(BF16)[None])


def solution(mesh):
    placed = (
        P("section", "seq", None),
        P("section", "seq", None),
        P(None, "head"),
        P(None, "head"),
        P(None, "head"),
        P("head", None),
        P("section", None, "seq"),
        P("section", "seq", None),
    )
    return jax.shard_map(
        per_device,
        mesh=mesh,
        in_specs=placed,
        out_specs=(P("section", "seq", "head"), P("section", "seq", "head")),
        check_vma=False,
    )
```

```python
import jax
import jax.numpy as jnp
from jax import lax
from jax.experimental import pallas as pl
from jax.experimental.pallas import tpu as pltpu
from jax.sharding import PartitionSpec as P

D = 2048
HEADS = 16
BLK = 128
HD = D // HEADS
SCALE = HD**-0.5
LOG2E = 1.4426950408889634
CHUNKS = ((0, 4), (4, 4))
VMEM = 64 * 2**20 - 2**16

F32 = jnp.float32
BF16 = jnp.bfloat16
NN = (((1,), (0,)), ((), ()))
NT = (((1,), (1,)), ((), ()))
TN = (((0,), (0,)), ((), ()))


def dot(a, b, dims):
    return lax.dot_general(a, b, dims, preferred_element_type=F32)


def section_shift(block, distance):
    count = lax.axis_size("section")
    return lax.ppermute(
        block, "section", [(i, (i + distance) % count) for i in range(count)]
    )


def near_swap(block):
    count = lax.axis_size("seq")
    return lax.ppermute(block, "seq", [(i, i ^ 1) for i in range(count)])


def far_swap(block):
    count = lax.axis_size("seq")
    pairs = [(i, i + 1) for i in range(1, count - 1, 2)]
    return lax.ppermute(block, "seq", pairs + [(j, i) for i, j in pairs])


def head_swap(block):
    return lax.ppermute(block, "head", [(0, 1), (1, 0)])


def across(block):
    count = lax.axis_size("seq")
    route = [(2 * i + g, 2 * (i ^ 8) + 1 - g) for i in range(count) for g in range(2)]
    return lax.ppermute(block, ("seq", "head"), route)


def call(
    body, grid, in_specs, out_specs, out_shape, args, name, after=(), scalars=0, scratch=(),
    flops=0,
):
    first = scalars + len(in_specs)
    unread = len(after)

    def reads(*refs):
        body(*refs[:first], *refs[first + unread :])

    in_specs = list(in_specs) + [pl.BlockSpec(memory_space=pl.ANY)] * unread
    return pl.pallas_call(
        reads,
        grid_spec=pltpu.PrefetchScalarGridSpec(
            num_scalar_prefetch=scalars,
            grid=grid,
            in_specs=in_specs,
            out_specs=out_specs,
            scratch_shapes=scratch,
        ),
        out_shape=out_shape,
        compiler_params=pltpu.CompilerParams(vmem_limit_bytes=VMEM),
        cost_estimate=pl.CostEstimate(flops=flops, bytes_accessed=0, transcendentals=0),
        name=name,
    )(*args, *after)


def key_values(scalars, notes, w_key, w_value, w_query, h0, hc, give, after):
    rows = notes.shape[0]
    cols = w_query.shape[1]
    wide = 2 * HD
    pieces = hc * HD // wide
    quarter = D // 4

    def body(s_ref, notes_ref, wk_ref, wv_ref, wq_ref, *refs):
        if give:
            out_ref, give_ref, n_scr, wk_scr, wv_scr, out_scr, sems, out_sems, wq_scr, give_sems = refs
        else:
            out_ref, n_scr, wk_scr, wv_scr, out_scr, sems, out_sems = refs
        notes_in = pltpu.make_async_copy(notes_ref, n_scr, out_sems.at[1])
        notes_in.start()
        copies = []
        for p in range(pieces):
            part = slice(h0 * HD + p * wide, h0 * HD + (p + 1) * wide)
            to = slice(p * wide, (p + 1) * wide)
            for i, (src, dst) in enumerate(((wk_ref, wk_scr), (wv_ref, wv_scr))):
                copy = pltpu.make_async_copy(src.at[:, part], dst.at[:, to], sems.at[p, i])
                copy.start()
                copies.append(copy)
        if give:
            offset = pl.multiple_of((1 - s_ref[0]) * (2 * quarter) + s_ref[1] * quarter, quarter)
            take = pltpu.make_async_copy(
                wq_ref.at[pl.ds(offset, quarter), :], wq_scr, give_sems.at[0]
            )
            take.start()
        notes_in.wait()
        left = n_scr[...]
        for p in range(pieces):
            to = slice(p * wide, (p + 1) * wide)
            for i, scr in enumerate((wk_scr, wv_scr)):
                copies[2 * p + i].wait()
                out_scr[i, :, to] = dot(left, scr[:, to], NN).astype(BF16)
        sent = [pltpu.make_async_copy(out_scr, out_ref, out_sems.at[0])]
        if give:
            take.wait()
            sent.append(pltpu.make_async_copy(wq_scr, give_ref, give_sems.at[1]))
        for copy in sent:
            copy.start()
        for copy in sent:
            copy.wait()

    far = pl.BlockSpec(memory_space=pl.ANY)
    out = jax.ShapeDtypeStruct((2, rows, hc * HD), BF16)
    given = jax.ShapeDtypeStruct((quarter, cols), BF16)
    return call(
        body,
        (),
        [far] * 4,
        [far, far] if give else far,
        [out, given] if give else out,
        (scalars, notes, w_key, w_value, w_query),
        "key_values",
        after,
        scalars=1,
        scratch=[
            pltpu.VMEM((rows, D), BF16),
            pltpu.VMEM((D, hc * HD), BF16),
            pltpu.VMEM((D, hc * HD), BF16),
            pltpu.VMEM((2, rows, hc * HD), BF16),
            pltpu.SemaphoreType.DMA((pieces, 2)),
            pltpu.SemaphoreType.DMA((2,)),
        ]
        + ([pltpu.VMEM((quarter, cols), BF16), pltpu.SemaphoreType.DMA((2,))] if give else []),
    )


def project(rows_in, weight, dims, name, after):
    rows = rows_in.shape[0]
    width = D // 2
    step = 256
    steps = rows // step
    parts = 4

    def body(a_ref, w_ref, out_ref, a_scr, w_scr, o_scr, w_sems, row_sems, out_sems):
        size = w_ref.shape[0] // parts
        weight_copies = []
        row_copies = []
        for p in range(parts):
            at = slice(p * size, (p + 1) * size)
            weight_copies.append(pltpu.make_async_copy(w_ref.at[at], w_scr.at[at], w_sems.at[p]))
        for m in range(steps):
            at = slice(m * step, (m + 1) * step)
            row_copies.append(pltpu.make_async_copy(a_ref.at[at], a_scr.at[at], row_sems.at[m]))
        for copy in row_copies[:1] + weight_copies + row_copies[1:]:
            copy.start()
        for copy in weight_copies:
            copy.wait()
        sent = []
        for m in range(steps):
            at = slice(m * step, (m + 1) * step)
            row_copies[m].wait()
            o_scr[at, :] = dot(a_scr[at, :], w_scr[...], dims).astype(BF16)
            copy = pltpu.make_async_copy(o_scr.at[at], out_ref.at[at], out_sems.at[m])
            copy.start()
            sent.append(copy)
        for copy in sent:
            copy.wait()

    far = pl.BlockSpec(memory_space=pl.ANY)
    return call(
        body,
        (),
        [far] * 2,
        far,
        jax.ShapeDtypeStruct((rows, width), BF16),
        (rows_in, weight),
        name,
        after,
        scratch=[
            pltpu.VMEM(rows_in.shape, BF16),
            pltpu.VMEM(weight.shape, BF16),
            pltpu.VMEM((rows, width), BF16),
            pltpu.SemaphoreType.DMA((parts,)),
            pltpu.SemaphoreType.DMA((steps,)),
            pltpu.SemaphoreType.DMA((steps,)),
        ],
    )


def frame_part(scalars, grads, weights, own, name, after):
    rows = grads[0].shape[0]
    half = D // 2
    cols = sum(g.shape[1] for g in grads)
    quarter = half // 2
    step = 256
    steps = rows // step
    terms = list(grads) + ([] if own is None else [own])
    count = len(terms)

    def body(s_ref, *refs):
        term_refs, refs = refs[:count], refs[count:]
        weight_refs, refs = refs[: len(weights)], refs[len(weights) :]
        out_ref, w_scr, o_scr, *refs = refs
        term_scrs, (w_sems, term_sems, out_sems) = refs[:count], refs[count:]
        weight_copies = []
        for p in range(2):
            if own is None:
                at = pl.ds(pl.multiple_of(s_ref[0] * half + p * quarter, quarter), quarter)
                src, dst = weight_refs[0].at[at], w_scr.at[p * quarter : (p + 1) * quarter]
            else:
                core = s_ref[1] if p == 0 else 1 - s_ref[1]
                to = pl.ds(pl.multiple_of(core * quarter, quarter), quarter)
                src, dst = weight_refs[p], w_scr.at[to]
            weight_copies.append(pltpu.make_async_copy(src, dst, w_sems.at[p]))
        for copy in weight_copies:
            copy.start()
        term_copies = []
        for m in range(steps):
            at = slice(m * step, (m + 1) * step)
            for t in range(count):
                copy = pltpu.make_async_copy(term_refs[t].at[at], term_scrs[t].at[at], term_sems.at[m, t])
                copy.start()
                term_copies.append(copy)
        for copy in weight_copies:
            copy.wait()
        sent = []
        for m in range(steps):
            at = slice(m * step, (m + 1) * step)
            for t in range(count):
                term_copies[m * count + t].wait()
            left = jnp.concatenate([scr[at, :] for scr in term_scrs[: len(grads)]], axis=1)
            total = dot(left, w_scr[...], NT)
            if own is not None:
                total = total + term_scrs[-1][at, :].astype(F32)
            o_scr[at, :] = total.astype(BF16)
            copy = pltpu.make_async_copy(o_scr.at[at], out_ref.at[at], out_sems.at[m])
            copy.start()
            sent.append(copy)
        for copy in sent:
            copy.wait()

    far = pl.BlockSpec(memory_space=pl.ANY)
    return call(
        body,
        (),
        [far] * (count + len(weights)),
        far,
        jax.ShapeDtypeStruct((rows, half), BF16),
        (scalars, *terms, *weights),
        name,
        after,
        scalars=1,
        scratch=[
            pltpu.VMEM((half, cols), BF16),
            pltpu.VMEM((rows, half), BF16),
            *[pltpu.VMEM(term.shape, BF16) for term in terms],
            pltpu.SemaphoreType.DMA((2,)),
            pltpu.SemaphoreType.DMA((steps, count)),
            pltpu.SemaphoreType.DMA((steps,)),
        ],
    )


def note_product(scalars, grads, chunks, w_key, w_value, after, before=None, which=(0, 1)):
    nt = grads[0].shape[1]
    half = D // 2
    heads = [h for h0, hc in chunks for h in range(h0, h0 + hc)]
    hc = len(heads)
    last = before is not None
    start = which[0]

    def body(s_ref, *refs):
        grad_refs, refs = refs[: len(grads)], refs[len(grads) :]
        wk = jnp.concatenate([r[...] for r in refs[:hc]], axis=1)
        wv = jnp.concatenate([r[...] for r in refs[hc : 2 * hc]], axis=1)
        gk = jnp.concatenate([r[0] for r in grad_refs], axis=1)
        gv = jnp.concatenate([r[1] for r in grad_refs], axis=1)
        total = dot(gk, wk, NT) + dot(gv, wv, NT)
        if last:
            total = total + refs[2 * hc][0]
        out_ref = refs[-1]
        out_ref[0] = total.astype(out_ref.dtype)

    def weight_in(h):
        return pl.BlockSpec(
            (half, HD), lambda n, s: (jnp.where(n + start == 0, 1 - s[0], s[0]), h)
        )

    return call(
        body,
        (len(which),),
        [pl.BlockSpec(g.shape, lambda n, s: (0, 0, 0)) for g in grads]
        + [weight_in(h) for h in heads] * 2
        + ([pl.BlockSpec((1, nt, half), lambda n, s: (n + start, 0, 0))] if last else []),
        pl.BlockSpec((1, nt, half), lambda n, s: (n, 0, 0)),
        jax.ShapeDtypeStruct((len(which), nt, half), BF16 if last else F32),
        (scalars, *grads) + (w_key,) * hc + (w_value,) * hc + ((before,) if last else ()),
        "note_product",
        after,
        scalars=1,
    )


def attention_body(
    s_ref, band_ref, q_ref, g_ref, kvo_ref, kvn_ref, kvf_ref, dq_ref, own_ref, near_ref, far_ref,
    p_scr, ds_scr, bias_ref,
):
    @pl.when(pl.program_id(0) == 0)
    def _():
        row = lax.broadcasted_iota(jnp.int32, (8, BLK), 0)
        shard = s_ref[2]
        far = shard - 1 + 2 * s_ref[1]
        block = jnp.where(row < 2, 2 * shard, jnp.where(row < 4, 2 * (shard ^ 1), 2 * far)) + row % 2
        for b in range(q_ref.shape[0] // BLK):
            inside = (block >= band_ref[0, b]) & (block <= band_ref[1, b])
            bias_ref[:, b * BLK : (b + 1) * BLK] = jnp.where(inside, 0.0, -jnp.inf)

    scale2 = SCALE * LOG2E
    frames = q_ref.shape[0]
    nt = kvo_ref.shape[1]
    step = 256
    blocks = 3 * nt // BLK
    keys = jnp.concatenate([kvo_ref[0], kvn_ref[0], kvf_ref[0]], axis=0)
    values = jnp.concatenate([kvo_ref[1], kvn_ref[1], kvf_ref[1]], axis=0)
    for f in range(frames // step):
        cols = slice(f * step, (f + 1) * step)
        s = dot(keys, q_ref[cols, :], NT)
        gp = dot(values, g_ref[cols, :], NT)
        rows = [slice(j * BLK, (j + 1) * BLK) for j in range(blocks)]
        bias = [bias_ref[j : j + 1, cols] for j in range(blocks)]
        peak = None
        for j in range(blocks):
            top = jnp.max(s[rows[j]], axis=0, keepdims=True) + bias[j]
            peak = top if peak is None else jnp.maximum(peak, top)
        expos = []
        total = jnp.zeros((1, step), F32)
        mixed = jnp.zeros((1, step), F32)
        for j in range(blocks):
            e = jnp.exp2(s[rows[j]] * scale2 + (bias[j] - peak) * scale2)
            expos.append(e)
            total = total + jnp.sum(e, axis=0, keepdims=True)
            mixed = mixed + jnp.sum(e * gp[rows[j]], axis=0, keepdims=True)
        inv = 1.0 / total
        delta = mixed * inv
        for j in range(blocks):
            p = expos[j] * inv
            p_scr[rows[j], cols] = p.astype(BF16)
            ds_scr[rows[j], cols] = (p * (gp[rows[j]] - delta)).astype(BF16)
    dq_ref[...] = (dot(ds_scr[...], keys, TN) * SCALE).astype(BF16)
    dv = dot(p_scr[...], g_ref[...], NN)
    dk = dot(ds_scr[...], q_ref[...], NN) * SCALE
    for i, grad in enumerate((dk, dv)):
        own_ref[i] = grad[:nt]
        near_ref[i] = grad[nt : 2 * nt].astype(BF16)
        far_ref[i] = grad[2 * nt :].astype(BF16)


def attention(scalars, band, queries, grad_ctx, kv_own, kv_near, kv_far, h0, hc, after):
    frames = queries.shape[0]
    nt = kv_own.shape[1]
    frame_in = pl.BlockSpec((frames, HD), lambda h, s, b: (0, h0 + h))
    note_io = pl.BlockSpec((2, nt, HD), lambda h, s, b: (0, 0, h))
    notes_out = jax.ShapeDtypeStruct((2, nt, hc * HD), BF16)
    return call(
        attention_body,
        (hc,),
        [frame_in, frame_in, note_io, note_io, note_io],
        [pl.BlockSpec((frames, HD), lambda h, s, b: (0, h)), note_io, note_io, note_io],
        [
            jax.ShapeDtypeStruct((frames, hc * HD), BF16),
            jax.ShapeDtypeStruct((2, nt, hc * HD), F32),
            notes_out,
            notes_out,
        ],
        (scalars, band, queries, grad_ctx, kv_own, kv_near, kv_far),
        "attention",
        after,
        scalars=2,
        scratch=[
            pltpu.VMEM((3 * nt, frames), BF16),
            pltpu.VMEM((3 * nt, frames), BF16),
            pltpu.VMEM((8, frames), F32),
        ],
        flops=90 * frames * nt * hc * HD if h0 else 0,
    )


def per_device(notes, frames, w_query, w_key, w_value, w_out, band_blocks, grad_mixed):
    shard = lax.axis_index("seq")
    group = lax.axis_index("head")
    core = shard % 2
    scalars = jnp.stack([group, core, shard]).astype(jnp.int32)
    band = band_blocks[0]

    arrays = (scalars, notes[0], w_key, w_value, w_query)
    made0 = key_values(*arrays, *CHUNKS[0], False, ())
    made1, given = key_values(*arrays, *CHUNKS[1], True, (made0,))
    moved = [section_shift(made0, 1), section_shift(made1, 1)]
    w_mine = across(given)
    queries = project(frames[0], w_query, NN, "queries", (given,))
    moved[0], queries = lax.optimization_barrier((moved[0], queries))
    near0, far0 = near_swap(moved[0]), far_swap(moved[0])
    grad_ctx = project(grad_mixed[0], w_out, NT, "grad_ctx", (queries, moved[0]))
    moved[1], grad_ctx = lax.optimization_barrier((moved[1], grad_ctx))

    def attend(step, near, far, after):
        return attention(
            scalars, band, queries, grad_ctx, moved[step], near, far, *CHUNKS[step], after
        )

    def note_sum_of(own, near, far):
        return (own + near.astype(F32) + far.astype(F32)).astype(BF16)

    near1, far1 = near_swap(moved[1]), far_swap(moved[1])
    dq0, own0, rim_near0, rim_far0 = attend(0, near0, far0, ())
    dq0_other = head_swap(dq0)
    w_mine, dq0 = lax.optimization_barrier((w_mine, dq0))
    w_theirs = near_swap(w_mine)
    rim_near0, rim_far0, near1, far1 = lax.optimization_barrier((rim_near0, rim_far0, near1, far1))
    in_near0, in_far0 = near_swap(rim_near0), far_swap(rim_far0)
    dq1, own1, rim_near1, rim_far1 = attend(1, near1, far1, (dq0,))
    dq1_other = head_swap(dq1)
    in_near0, in_far0, rim_near1, rim_far1 = lax.optimization_barrier(
        (in_near0, in_far0, rim_near1, rim_far1)
    )
    in_near1, in_far1 = near_swap(rim_near1), far_swap(rim_far1)
    notes0 = section_shift(note_sum_of(own0, in_near0, in_far0), -1)
    owned1 = note_sum_of(own1, in_near1, in_far1)
    owned1, dq0_other = lax.optimization_barrier((owned1, dq0_other))
    notes1 = section_shift(owned1, -1)

    own_part = frame_part(scalars, [dq0, dq1], [w_query], None, "frame_own", (owned1,))
    before = note_product(scalars, [notes0], CHUNKS[:1], w_key, w_value, (own_part,))
    last = (scalars, [notes1], CHUNKS[1:], w_key, w_value)
    give_notes = note_product(*last, (), before, (0,))
    notes_other = head_swap(give_notes)
    keep_notes = note_product(*last, (give_notes,), before, (1,))
    frame_out = frame_part(
        scalars, [dq0_other, dq1_other], [w_mine, w_theirs], own_part, "frame_sum", (keep_notes,)
    )
    notes_other, frame_out = lax.optimization_barrier((notes_other, frame_out))
    note_out = keep_notes[0].astype(F32) + notes_other[0].astype(F32)
    return (frame_out[None], note_out.astype(BF16)[None])


def solution(mesh):
    placed = (
        P("section", "seq", None),
        P("section", "seq", None),
        P(None, "head"),
        P(None, "head"),
        P(None, "head"),
        P("head", None),
        P("section", None, "seq"),
        P("section", "seq", None),
    )
    return jax.shard_map(
        per_device,
        mesh=mesh,
        in_specs=placed,
        out_specs=(P("section", "seq", "head"), P("section", "seq", "head")),
        check_vma=False,
    )
```

```python
import jax
import jax.numpy as jnp
from jax import lax
from jax.experimental import pallas as pl
from jax.experimental.pallas import tpu as pltpu
from jax.sharding import PartitionSpec as P

D = 2048
HEADS = 16
BLK = 128
HD = D // HEADS
SCALE = HD**-0.5
LOG2E = 1.4426950408889634
CHUNKS = ((0, 4), (4, 4))
VMEM = 64 * 2**20 - 2**16

F32 = jnp.float32
BF16 = jnp.bfloat16
NN = (((1,), (0,)), ((), ()))
NT = (((1,), (1,)), ((), ()))
TN = (((0,), (0,)), ((), ()))


def dot(a, b, dims):
    return lax.dot_general(a, b, dims, preferred_element_type=F32)


def section_shift(block, distance):
    count = lax.axis_size("section")
    return lax.ppermute(
        block, "section", [(i, (i + distance) % count) for i in range(count)]
    )


def near_swap(block):
    count = lax.axis_size("seq")
    return lax.ppermute(block, "seq", [(i, i ^ 1) for i in range(count)])


def far_swap(block):
    count = lax.axis_size("seq")
    pairs = [(i, i + 1) for i in range(1, count - 1, 2)]
    return lax.ppermute(block, "seq", pairs + [(j, i) for i, j in pairs])


def head_swap(block):
    return lax.ppermute(block, "head", [(0, 1), (1, 0)])


def across(block):
    count = lax.axis_size("seq")
    route = [(2 * i + g, 2 * (i ^ 8) + 1 - g) for i in range(count) for g in range(2)]
    return lax.ppermute(block, ("seq", "head"), route)


def call(
    body, grid, in_specs, out_specs, out_shape, args, name, after=(), scalars=0, scratch=(),
    flops=0,
):
    first = scalars + len(in_specs)
    unread = len(after)

    def reads(*refs):
        body(*refs[:first], *refs[first + unread :])

    in_specs = list(in_specs) + [pl.BlockSpec(memory_space=pl.ANY)] * unread
    return pl.pallas_call(
        reads,
        grid_spec=pltpu.PrefetchScalarGridSpec(
            num_scalar_prefetch=scalars,
            grid=grid,
            in_specs=in_specs,
            out_specs=out_specs,
            scratch_shapes=scratch,
        ),
        out_shape=out_shape,
        compiler_params=pltpu.CompilerParams(vmem_limit_bytes=VMEM),
        cost_estimate=pl.CostEstimate(flops=flops, bytes_accessed=0, transcendentals=0),
        name=name,
    )(*args, *after)


def start_all(copies):
    for copy in copies:
        copy.start()
    return copies


def key_value_copies(wk_ref, wv_ref, wk_scr, wv_scr, sems, h0, hc):
    part = slice(h0 * HD, (h0 + hc) * HD)
    return start_all(
        [
            pltpu.make_async_copy(wk_ref.at[:, part], wk_scr, sems.at[0]),
            pltpu.make_async_copy(wv_ref.at[:, part], wv_scr, sems.at[1]),
        ]
    )


def key_values(notes, w_key, w_value, h0, hc):
    rows = notes.shape[0]

    def body(notes_ref, wk_ref, wv_ref, out_ref, n_scr, wk_scr, wv_scr, out_scr, sems):
        (notes_in,) = start_all([pltpu.make_async_copy(notes_ref, n_scr, sems.at[2])])
        weights_in = key_value_copies(wk_ref, wv_ref, wk_scr, wv_scr, sems, h0, hc)
        notes_in.wait()
        for i, scr in enumerate((wk_scr, wv_scr)):
            weights_in[i].wait()
            out_scr[i] = dot(n_scr[...], scr[...], NN).astype(BF16)
        for copy in start_all([pltpu.make_async_copy(out_scr, out_ref, sems.at[3])]):
            copy.wait()

    far = pl.BlockSpec(memory_space=pl.ANY)
    return call(
        body,
        (),
        [far] * 3,
        far,
        jax.ShapeDtypeStruct((2, rows, hc * HD), BF16),
        (notes, w_key, w_value),
        "key_values",
        scratch=[
            pltpu.VMEM((rows, D), BF16),
            pltpu.VMEM((D, hc * HD), BF16),
            pltpu.VMEM((D, hc * HD), BF16),
            pltpu.VMEM((2, rows, hc * HD), BF16),
            pltpu.SemaphoreType.DMA((4,)),
        ],
    )


class Product:
    step = 256
    parts = 2

    def __init__(self, rows_in, weight, dims):
        self.dims = dims
        self.steps = rows_in.shape[0] // self.step
        self.size = D // 2 // self.parts
        self.out = jax.ShapeDtypeStruct((rows_in.shape[0], D // 2), BF16)
        self.scratch = [
            pltpu.VMEM(rows_in.shape, BF16),
            pltpu.VMEM(weight.shape, BF16),
            pltpu.VMEM(self.out.shape, BF16),
            pltpu.SemaphoreType.DMA((self.parts,)),
            pltpu.SemaphoreType.DMA((self.steps,)),
            pltpu.SemaphoreType.DMA((self.steps,)),
        ]

    def rows(self, m):
        return slice(m * self.step, (m + 1) * self.step)

    def part(self, p):
        cols = slice(p * self.size, (p + 1) * self.size)
        return (slice(None), cols) if self.dims is NN else (cols, slice(None))

    def start(self, a_ref, w_ref, a_scr, w_scr, o_scr, w_sems, row_sems, out_sems):
        rows_in = [
            pltpu.make_async_copy(a_ref.at[self.rows(m)], a_scr.at[self.rows(m)], row_sems.at[m])
            for m in range(self.steps)
        ]
        weight_in = [
            pltpu.make_async_copy(w_ref.at[self.part(p)], w_scr.at[self.part(p)], w_sems.at[p])
            for p in range(self.parts)
        ]
        start_all(rows_in[:1] + weight_in + rows_in[1:])
        return rows_in, weight_in

    def finish(self, copies, out_ref, a_scr, w_scr, o_scr, w_sems, row_sems, out_sems):
        rows_in, weight_in = copies
        sent = []
        for m in range(self.steps):
            at = self.rows(m)
            rows_in[m].wait()
            for p in range(self.parts):
                if m == 0:
                    weight_in[p].wait()
                cols = slice(p * self.size, (p + 1) * self.size)
                term = dot(a_scr[at, :], w_scr[self.part(p)], self.dims)
                o_scr[at, cols] = term.astype(BF16)
            copy = pltpu.make_async_copy(o_scr.at[at], out_ref.at[at], out_sems.at[m])
            sent += start_all([copy])
        return sent


def key_values_and_queries(scalars, notes, w_key, w_value, frames, w_query, h0, hc, after):
    rows = notes.shape[0]
    quarter = D // 4
    product = Product(frames, w_query, NN)

    def body(s_ref, notes_ref, wk_ref, wv_ref, f_ref, wq_ref, out_ref, q_ref, give_ref,
             n_scr, wk_scr, wv_scr, out_scr, sems, *scrs):
        (notes_in,) = start_all([pltpu.make_async_copy(notes_ref, n_scr, sems.at[2])])
        weights_in = key_value_copies(wk_ref, wv_ref, wk_scr, wv_scr, sems, h0, hc)
        copies = product.start(f_ref, wq_ref, *scrs)
        notes_in.wait()
        for i, scr in enumerate((wk_scr, wv_scr)):
            weights_in[i].wait()
            out_scr[i] = dot(n_scr[...], scr[...], NN).astype(BF16)
        sent = start_all([pltpu.make_async_copy(out_scr, out_ref, sems.at[3])])
        sent += product.finish(copies, q_ref, *scrs)
        offset = pl.multiple_of((1 - s_ref[0]) * (2 * quarter) + s_ref[1] * quarter, quarter)
        give = pltpu.make_async_copy(scrs[1].at[pl.ds(offset, quarter), :], give_ref, sems.at[4])
        sent += start_all([give])
        for copy in sent:
            copy.wait()

    far = pl.BlockSpec(memory_space=pl.ANY)
    return call(
        body,
        (),
        [far] * 5,
        [far] * 3,
        [
            jax.ShapeDtypeStruct((2, rows, hc * HD), BF16),
            product.out,
            jax.ShapeDtypeStruct((quarter, w_query.shape[1]), BF16),
        ],
        (scalars, notes, w_key, w_value, frames, w_query),
        "key_values_and_queries",
        after,
        scalars=1,
        scratch=[
            pltpu.VMEM((rows, D), BF16),
            pltpu.VMEM((D, hc * HD), BF16),
            pltpu.VMEM((D, hc * HD), BF16),
            pltpu.VMEM((2, rows, hc * HD), BF16),
            pltpu.SemaphoreType.DMA((5,)),
            *product.scratch,
        ],
    )


def context_gradient(grad_mixed, w_out, after):
    product = Product(grad_mixed, w_out, NT)

    def body(a_ref, w_ref, out_ref, *scrs):
        copies = product.start(a_ref, w_ref, *scrs)
        for copy in product.finish(copies, out_ref, *scrs):
            copy.wait()

    far = pl.BlockSpec(memory_space=pl.ANY)
    return call(
        body, (), [far] * 2, far, product.out, (grad_mixed, w_out), "grad_ctx", after,
        scratch=product.scratch,
    )


def frame_part(scalars, grads, weights, own, name, after):
    rows = grads[0].shape[0]
    half = D // 2
    cols = sum(g.shape[1] for g in grads)
    quarter = half // 2
    step = 256
    steps = rows // step
    terms = list(grads) + ([] if own is None else [own])
    count = len(terms)

    def body(s_ref, *refs):
        term_refs, refs = refs[:count], refs[count:]
        weight_refs, refs = refs[: len(weights)], refs[len(weights) :]
        out_ref, w_scr, o_scr, *refs = refs
        term_scrs, (w_sems, term_sems, out_sems) = refs[:count], refs[count:]
        weight_copies = []
        for p in range(2):
            if own is None:
                at = pl.ds(pl.multiple_of(s_ref[0] * half + p * quarter, quarter), quarter)
                src, dst = weight_refs[0].at[at], w_scr.at[p * quarter : (p + 1) * quarter]
            else:
                core = s_ref[1] if p == 0 else 1 - s_ref[1]
                to = pl.ds(pl.multiple_of(core * quarter, quarter), quarter)
                src, dst = weight_refs[p], w_scr.at[to]
            weight_copies.append(pltpu.make_async_copy(src, dst, w_sems.at[p]))
        for copy in weight_copies:
            copy.start()
        term_copies = []
        for m in range(steps):
            at = slice(m * step, (m + 1) * step)
            for t in range(count):
                copy = pltpu.make_async_copy(term_refs[t].at[at], term_scrs[t].at[at], term_sems.at[m, t])
                copy.start()
                term_copies.append(copy)
        for copy in weight_copies:
            copy.wait()
        sent = []
        for m in range(steps):
            at = slice(m * step, (m + 1) * step)
            for t in range(count):
                term_copies[m * count + t].wait()
            left = jnp.concatenate([scr[at, :] for scr in term_scrs[: len(grads)]], axis=1)
            total = dot(left, w_scr[...], NT)
            if own is not None:
                total = total + term_scrs[-1][at, :].astype(F32)
            o_scr[at, :] = total.astype(BF16)
            copy = pltpu.make_async_copy(o_scr.at[at], out_ref.at[at], out_sems.at[m])
            copy.start()
            sent.append(copy)
        for copy in sent:
            copy.wait()

    far = pl.BlockSpec(memory_space=pl.ANY)
    return call(
        body,
        (),
        [far] * (count + len(weights)),
        far,
        jax.ShapeDtypeStruct((rows, half), BF16),
        (scalars, *terms, *weights),
        name,
        after,
        scalars=1,
        scratch=[
            pltpu.VMEM((half, cols), BF16),
            pltpu.VMEM((rows, half), BF16),
            *[pltpu.VMEM(term.shape, BF16) for term in terms],
            pltpu.SemaphoreType.DMA((2,)),
            pltpu.SemaphoreType.DMA((steps, count)),
            pltpu.SemaphoreType.DMA((steps,)),
        ],
    )


def note_product(scalars, grads, chunks, w_key, w_value, after, before=None, which=(0, 1)):
    nt = grads[0].shape[1]
    half = D // 2
    heads = [h for h0, hc in chunks for h in range(h0, h0 + hc)]
    hc = len(heads)
    last = before is not None
    start = which[0]

    def body(s_ref, *refs):
        grad_refs, refs = refs[: len(grads)], refs[len(grads) :]
        wk = jnp.concatenate([r[...] for r in refs[:hc]], axis=1)
        wv = jnp.concatenate([r[...] for r in refs[hc : 2 * hc]], axis=1)
        gk = jnp.concatenate([r[0] for r in grad_refs], axis=1)
        gv = jnp.concatenate([r[1] for r in grad_refs], axis=1)
        total = dot(gk, wk, NT) + dot(gv, wv, NT)
        if last:
            total = total + refs[2 * hc][0]
        out_ref = refs[-1]
        out_ref[0] = total.astype(out_ref.dtype)

    def weight_in(h):
        return pl.BlockSpec(
            (half, HD), lambda n, s: (jnp.where(n + start == 0, 1 - s[0], s[0]), h)
        )

    return call(
        body,
        (len(which),),
        [pl.BlockSpec(g.shape, lambda n, s: (0, 0, 0)) for g in grads]
        + [weight_in(h) for h in heads] * 2
        + ([pl.BlockSpec((1, nt, half), lambda n, s: (n + start, 0, 0))] if last else []),
        pl.BlockSpec((1, nt, half), lambda n, s: (n, 0, 0)),
        jax.ShapeDtypeStruct((len(which), nt, half), BF16 if last else F32),
        (scalars, *grads) + (w_key,) * hc + (w_value,) * hc + ((before,) if last else ()),
        "note_product",
        after,
        scalars=1,
    )


def attention_body(
    s_ref, band_ref, q_ref, g_ref, kvo_ref, kvn_ref, kvf_ref, dq_ref, own_ref, near_ref, far_ref,
    p_scr, ds_scr, bias_ref,
):
    @pl.when(pl.program_id(0) == 0)
    def _():
        row = lax.broadcasted_iota(jnp.int32, (8, BLK), 0)
        shard = s_ref[2]
        far = shard - 1 + 2 * s_ref[1]
        block = jnp.where(row < 2, 2 * shard, jnp.where(row < 4, 2 * (shard ^ 1), 2 * far)) + row % 2
        for b in range(q_ref.shape[0] // BLK):
            inside = (block >= band_ref[0, b]) & (block <= band_ref[1, b])
            bias_ref[:, b * BLK : (b + 1) * BLK] = jnp.where(inside, 0.0, -jnp.inf)

    scale2 = SCALE * LOG2E
    frames = q_ref.shape[0]
    nt = kvo_ref.shape[1]
    step = 256
    blocks = 3 * nt // BLK
    keys = jnp.concatenate([kvo_ref[0], kvn_ref[0], kvf_ref[0]], axis=0)
    values = jnp.concatenate([kvo_ref[1], kvn_ref[1], kvf_ref[1]], axis=0)
    for f in range(frames // step):
        cols = slice(f * step, (f + 1) * step)
        s = dot(keys, q_ref[cols, :], NT)
        gp = dot(values, g_ref[cols, :], NT)
        rows = [slice(j * BLK, (j + 1) * BLK) for j in range(blocks)]
        bias = [bias_ref[j : j + 1, cols] for j in range(blocks)]
        peak = None
        for j in range(blocks):
            top = jnp.max(s[rows[j]], axis=0, keepdims=True) + bias[j]
            peak = top if peak is None else jnp.maximum(peak, top)
        expos = []
        total = jnp.zeros((1, step), F32)
        mixed = jnp.zeros((1, step), F32)
        for j in range(blocks):
            e = jnp.exp2(s[rows[j]] * scale2 + (bias[j] - peak) * scale2)
            expos.append(e)
            total = total + jnp.sum(e, axis=0, keepdims=True)
            mixed = mixed + jnp.sum(e * gp[rows[j]], axis=0, keepdims=True)
        inv = 1.0 / total
        delta = mixed * inv
        for j in range(blocks):
            p = expos[j] * inv
            p_scr[rows[j], cols] = p.astype(BF16)
            ds_scr[rows[j], cols] = (p * (gp[rows[j]] - delta)).astype(BF16)
    dq_ref[...] = (dot(ds_scr[...], keys, TN) * SCALE).astype(BF16)
    dv = dot(p_scr[...], g_ref[...], NN)
    dk = dot(ds_scr[...], q_ref[...], NN) * SCALE
    for i, grad in enumerate((dk, dv)):
        own_ref[i] = grad[:nt]
        near_ref[i] = grad[nt : 2 * nt].astype(BF16)
        far_ref[i] = grad[2 * nt :].astype(BF16)


def attention(scalars, band, queries, grad_ctx, kv_own, kv_near, kv_far, h0, hc, after):
    frames = queries.shape[0]
    nt = kv_own.shape[1]
    frame_in = pl.BlockSpec((frames, HD), lambda h, s, b: (0, h0 + h))
    note_io = pl.BlockSpec((2, nt, HD), lambda h, s, b: (0, 0, h))
    notes_out = jax.ShapeDtypeStruct((2, nt, hc * HD), BF16)
    return call(
        attention_body,
        (hc,),
        [frame_in, frame_in, note_io, note_io, note_io],
        [pl.BlockSpec((frames, HD), lambda h, s, b: (0, h)), note_io, note_io, note_io],
        [
            jax.ShapeDtypeStruct((frames, hc * HD), BF16),
            jax.ShapeDtypeStruct((2, nt, hc * HD), F32),
            notes_out,
            notes_out,
        ],
        (scalars, band, queries, grad_ctx, kv_own, kv_near, kv_far),
        "attention",
        after,
        scalars=2,
        scratch=[
            pltpu.VMEM((3 * nt, frames), BF16),
            pltpu.VMEM((3 * nt, frames), BF16),
            pltpu.VMEM((8, frames), F32),
        ],
        flops=90 * frames * nt * hc * HD if h0 else 0,
    )


def per_device(notes, frames, w_query, w_key, w_value, w_out, band_blocks, grad_mixed):
    shard = lax.axis_index("seq")
    group = lax.axis_index("head")
    core = shard % 2
    scalars = jnp.stack([group, core, shard]).astype(jnp.int32)
    band = band_blocks[0]

    made0 = key_values(notes[0], w_key, w_value, *CHUNKS[0])
    made1, queries, given = key_values_and_queries(
        scalars, notes[0], w_key, w_value, frames[0], w_query, *CHUNKS[1], (made0,)
    )
    moved = [section_shift(made0, 1), section_shift(made1, 1)]
    w_mine = across(given)
    moved[0], queries = lax.optimization_barrier((moved[0], queries))
    near0, far0 = near_swap(moved[0]), far_swap(moved[0])
    grad_ctx = context_gradient(grad_mixed[0], w_out, (queries, moved[0]))
    moved[1], grad_ctx = lax.optimization_barrier((moved[1], grad_ctx))

    def attend(step, near, far, after):
        return attention(
            scalars, band, queries, grad_ctx, moved[step], near, far, *CHUNKS[step], after
        )

    def note_sum_of(own, near, far):
        return (own + near.astype(F32) + far.astype(F32)).astype(BF16)

    near1, far1 = near_swap(moved[1]), far_swap(moved[1])
    dq0, own0, rim_near0, rim_far0 = attend(0, near0, far0, ())
    dq0_other = head_swap(dq0)
    w_mine, dq0 = lax.optimization_barrier((w_mine, dq0))
    w_theirs = near_swap(w_mine)
    rim_near0, rim_far0, near1, far1 = lax.optimization_barrier((rim_near0, rim_far0, near1, far1))
    in_near0, in_far0 = near_swap(rim_near0), far_swap(rim_far0)
    dq1, own1, rim_near1, rim_far1 = attend(1, near1, far1, (dq0,))
    dq1_other = head_swap(dq1)
    in_near0, in_far0, rim_near1, rim_far1 = lax.optimization_barrier(
        (in_near0, in_far0, rim_near1, rim_far1)
    )
    in_near1, in_far1 = near_swap(rim_near1), far_swap(rim_far1)
    notes0 = section_shift(note_sum_of(own0, in_near0, in_far0), -1)
    owned1 = note_sum_of(own1, in_near1, in_far1)
    owned1, dq0_other = lax.optimization_barrier((owned1, dq0_other))
    notes1 = section_shift(owned1, -1)

    own_part = frame_part(scalars, [dq0, dq1], [w_query], None, "frame_own", (owned1,))
    before = note_product(scalars, [notes0], CHUNKS[:1], w_key, w_value, (own_part,))
    last = (scalars, [notes1], CHUNKS[1:], w_key, w_value)
    give_notes = note_product(*last, (), before, (0,))
    notes_other = head_swap(give_notes)
    keep_notes = note_product(*last, (give_notes,), before, (1,))
    frame_out = frame_part(
        scalars, [dq0_other, dq1_other], [w_mine, w_theirs], own_part, "frame_sum", (keep_notes,)
    )
    notes_other, frame_out = lax.optimization_barrier((notes_other, frame_out))
    note_out = keep_notes[0].astype(F32) + notes_other[0].astype(F32)
    return (frame_out[None], note_out.astype(BF16)[None])


def solution(mesh):
    placed = (
        P("section", "seq", None),
        P("section", "seq", None),
        P(None, "head"),
        P(None, "head"),
        P(None, "head"),
        P("head", None),
        P("section", None, "seq"),
        P("section", "seq", None),
    )
    return jax.shard_map(
        per_device,
        mesh=mesh,
        in_specs=placed,
        out_specs=(P("section", "seq", "head"), P("section", "seq", "head")),
        check_vma=False,
    )
```

```python
import jax
import jax.numpy as jnp
from jax import lax
from jax.experimental import pallas as pl
from jax.experimental.pallas import tpu as pltpu
from jax.sharding import PartitionSpec as P

D = 2048
HEADS = 16
BLK = 128
HD = D // HEADS
SCALE = HD**-0.5
LOG2E = 1.4426950408889634
CHUNKS = ((0, 4), (4, 4))
VMEM = 64 * 2**20 - 2**16

F32 = jnp.float32
BF16 = jnp.bfloat16
NN = (((1,), (0,)), ((), ()))
NT = (((1,), (1,)), ((), ()))
TN = (((0,), (0,)), ((), ()))


def dot(a, b, dims):
    return lax.dot_general(a, b, dims, preferred_element_type=F32)


def section_shift(block, distance):
    count = lax.axis_size("section")
    return lax.ppermute(
        block, "section", [(i, (i + distance) % count) for i in range(count)]
    )


def near_swap(block):
    count = lax.axis_size("seq")
    return lax.ppermute(block, "seq", [(i, i ^ 1) for i in range(count)])


def far_swap(block):
    count = lax.axis_size("seq")
    pairs = [(i, i + 1) for i in range(1, count - 1, 2)]
    return lax.ppermute(block, "seq", pairs + [(j, i) for i, j in pairs])


def head_swap(block):
    return lax.ppermute(block, "head", [(0, 1), (1, 0)])


def across(block):
    count = lax.axis_size("seq")
    route = [(2 * i + g, 2 * (i ^ 8) + 1 - g) for i in range(count) for g in range(2)]
    return lax.ppermute(block, ("seq", "head"), route)


def call(
    body, grid, in_specs, out_specs, out_shape, args, name, after=(), scalars=0, scratch=(),
    flops=0,
):
    first = scalars + len(in_specs)
    unread = len(after)

    def reads(*refs):
        body(*refs[:first], *refs[first + unread :])

    in_specs = list(in_specs) + [pl.BlockSpec(memory_space=pl.ANY)] * unread
    return pl.pallas_call(
        reads,
        grid_spec=pltpu.PrefetchScalarGridSpec(
            num_scalar_prefetch=scalars,
            grid=grid,
            in_specs=in_specs,
            out_specs=out_specs,
            scratch_shapes=scratch,
        ),
        out_shape=out_shape,
        compiler_params=pltpu.CompilerParams(vmem_limit_bytes=VMEM),
        cost_estimate=pl.CostEstimate(flops=flops, bytes_accessed=0, transcendentals=0),
        name=name,
    )(*args, *after)


def start_all(copies):
    for copy in copies:
        copy.start()
    return copies


def key_value_copies(wk_ref, wv_ref, wk_scr, wv_scr, sems, h0, hc):
    part = slice(h0 * HD, (h0 + hc) * HD)
    return start_all(
        [
            pltpu.make_async_copy(wk_ref.at[:, part], wk_scr, sems.at[0]),
            pltpu.make_async_copy(wv_ref.at[:, part], wv_scr, sems.at[1]),
        ]
    )


def key_values(notes, w_key, w_value, h0, hc):
    rows = notes.shape[0]

    def body(notes_ref, wk_ref, wv_ref, out_ref, n_scr, wk_scr, wv_scr, out_scr, sems):
        (notes_in,) = start_all([pltpu.make_async_copy(notes_ref, n_scr, sems.at[2])])
        weights_in = key_value_copies(wk_ref, wv_ref, wk_scr, wv_scr, sems, h0, hc)
        notes_in.wait()
        for i, scr in enumerate((wk_scr, wv_scr)):
            weights_in[i].wait()
            out_scr[i] = dot(n_scr[...], scr[...], NN).astype(BF16)
        for copy in start_all([pltpu.make_async_copy(out_scr, out_ref, sems.at[3])]):
            copy.wait()

    far = pl.BlockSpec(memory_space=pl.ANY)
    return call(
        body,
        (),
        [far] * 3,
        far,
        jax.ShapeDtypeStruct((2, rows, hc * HD), BF16),
        (notes, w_key, w_value),
        "key_values",
        scratch=[
            pltpu.VMEM((rows, D), BF16),
            pltpu.VMEM((D, hc * HD), BF16),
            pltpu.VMEM((D, hc * HD), BF16),
            pltpu.VMEM((2, rows, hc * HD), BF16),
            pltpu.SemaphoreType.DMA((4,)),
        ],
    )


class Product:
    step = 256
    parts = 2

    def __init__(self, rows_in, weight, dims):
        self.dims = dims
        self.steps = rows_in.shape[0] // self.step
        self.size = D // 2 // self.parts
        self.out = jax.ShapeDtypeStruct((rows_in.shape[0], D // 2), BF16)
        self.scratch = [
            pltpu.VMEM(rows_in.shape, BF16),
            pltpu.VMEM(weight.shape, BF16),
            pltpu.VMEM(self.out.shape, BF16),
            pltpu.SemaphoreType.DMA((self.parts,)),
            pltpu.SemaphoreType.DMA((self.steps,)),
            pltpu.SemaphoreType.DMA((self.steps,)),
        ]

    def rows(self, m):
        return slice(m * self.step, (m + 1) * self.step)

    def part(self, p):
        cols = slice(p * self.size, (p + 1) * self.size)
        return (slice(None), cols) if self.dims is NN else (cols, slice(None))

    def start(self, a_ref, w_ref, a_scr, w_scr, o_scr, w_sems, row_sems, out_sems):
        rows_in = [
            pltpu.make_async_copy(a_ref.at[self.rows(m)], a_scr.at[self.rows(m)], row_sems.at[m])
            for m in range(self.steps)
        ]
        weight_in = [
            pltpu.make_async_copy(w_ref.at[self.part(p)], w_scr.at[self.part(p)], w_sems.at[p])
            for p in range(self.parts)
        ]
        start_all(rows_in[:1] + weight_in + rows_in[1:])
        return rows_in, weight_in

    def finish(self, copies, out_ref, a_scr, w_scr, o_scr, w_sems, row_sems, out_sems):
        rows_in, weight_in = copies
        sent = []
        for m in range(self.steps):
            at = self.rows(m)
            rows_in[m].wait()
            for p in range(self.parts):
                if m == 0:
                    weight_in[p].wait()
                cols = slice(p * self.size, (p + 1) * self.size)
                term = dot(a_scr[at, :], w_scr[self.part(p)], self.dims)
                o_scr[at, cols] = term.astype(BF16)
            copy = pltpu.make_async_copy(o_scr.at[at], out_ref.at[at], out_sems.at[m])
            sent += start_all([copy])
        return sent


def key_values_and_queries(scalars, notes, w_key, w_value, frames, w_query, h0, hc, after):
    rows = notes.shape[0]
    quarter = D // 4
    product = Product(frames, w_query, NN)

    def body(s_ref, notes_ref, wk_ref, wv_ref, f_ref, wq_ref, out_ref, q_ref, give_ref,
             n_scr, wk_scr, wv_scr, out_scr, sems, *scrs):
        (notes_in,) = start_all([pltpu.make_async_copy(notes_ref, n_scr, sems.at[2])])
        weights_in = key_value_copies(wk_ref, wv_ref, wk_scr, wv_scr, sems, h0, hc)
        copies = product.start(f_ref, wq_ref, *scrs)
        notes_in.wait()
        for i, scr in enumerate((wk_scr, wv_scr)):
            weights_in[i].wait()
            out_scr[i] = dot(n_scr[...], scr[...], NN).astype(BF16)
        sent = start_all([pltpu.make_async_copy(out_scr, out_ref, sems.at[3])])
        sent += product.finish(copies, q_ref, *scrs)
        offset = pl.multiple_of((1 - s_ref[0]) * (2 * quarter) + s_ref[1] * quarter, quarter)
        give = pltpu.make_async_copy(scrs[1].at[pl.ds(offset, quarter), :], give_ref, sems.at[4])
        sent += start_all([give])
        for copy in sent:
            copy.wait()

    far = pl.BlockSpec(memory_space=pl.ANY)
    return call(
        body,
        (),
        [far] * 5,
        [far] * 3,
        [
            jax.ShapeDtypeStruct((2, rows, hc * HD), BF16),
            product.out,
            jax.ShapeDtypeStruct((quarter, w_query.shape[1]), BF16),
        ],
        (scalars, notes, w_key, w_value, frames, w_query),
        "key_values_and_queries",
        after,
        scalars=1,
        scratch=[
            pltpu.VMEM((rows, D), BF16),
            pltpu.VMEM((D, hc * HD), BF16),
            pltpu.VMEM((D, hc * HD), BF16),
            pltpu.VMEM((2, rows, hc * HD), BF16),
            pltpu.SemaphoreType.DMA((5,)),
            *product.scratch,
        ],
    )


def context_gradient(grad_mixed, w_out, after):
    product = Product(grad_mixed, w_out, NT)

    def body(a_ref, w_ref, out_ref, *scrs):
        copies = product.start(a_ref, w_ref, *scrs)
        for copy in product.finish(copies, out_ref, *scrs):
            copy.wait()

    far = pl.BlockSpec(memory_space=pl.ANY)
    return call(
        body, (), [far] * 2, far, product.out, (grad_mixed, w_out), "grad_ctx", after,
        scratch=product.scratch,
    )


def frame_part(scalars, grads, weights, own, name, after):
    rows = grads[0].shape[0]
    half = D // 2
    cols = sum(g.shape[1] for g in grads)
    quarter = half // 2
    step = 256
    steps = rows // step
    terms = list(grads) + ([] if own is None else [own])
    count = len(terms)

    def body(s_ref, *refs):
        term_refs, refs = refs[:count], refs[count:]
        weight_refs, refs = refs[: len(weights)], refs[len(weights) :]
        out_ref, w_scr, o_scr, *refs = refs
        term_scrs, (w_sems, term_sems, out_sems) = refs[:count], refs[count:]
        weight_copies = []
        for p in range(2):
            if own is None:
                at = pl.ds(pl.multiple_of(s_ref[0] * half + p * quarter, quarter), quarter)
                src, dst = weight_refs[0].at[at], w_scr.at[p * quarter : (p + 1) * quarter]
            else:
                core = s_ref[1] if p == 0 else 1 - s_ref[1]
                to = pl.ds(pl.multiple_of(core * quarter, quarter), quarter)
                src, dst = weight_refs[p], w_scr.at[to]
            weight_copies.append(pltpu.make_async_copy(src, dst, w_sems.at[p]))
        for copy in weight_copies:
            copy.start()
        term_copies = []
        for m in range(steps):
            at = slice(m * step, (m + 1) * step)
            for t in range(count):
                copy = pltpu.make_async_copy(term_refs[t].at[at], term_scrs[t].at[at], term_sems.at[m, t])
                copy.start()
                term_copies.append(copy)
        for copy in weight_copies:
            copy.wait()
        sent = []
        for m in range(steps):
            at = slice(m * step, (m + 1) * step)
            for t in range(count):
                term_copies[m * count + t].wait()
            left = jnp.concatenate([scr[at, :] for scr in term_scrs[: len(grads)]], axis=1)
            total = dot(left, w_scr[...], NT)
            if own is not None:
                total = total + term_scrs[-1][at, :].astype(F32)
            o_scr[at, :] = total.astype(BF16)
            copy = pltpu.make_async_copy(o_scr.at[at], out_ref.at[at], out_sems.at[m])
            copy.start()
            sent.append(copy)
        for copy in sent:
            copy.wait()

    far = pl.BlockSpec(memory_space=pl.ANY)
    return call(
        body,
        (),
        [far] * (count + len(weights)),
        far,
        jax.ShapeDtypeStruct((rows, half), BF16),
        (scalars, *terms, *weights),
        name,
        after,
        scalars=1,
        flops=8 * rows * half * cols if own is None else 0,
        scratch=[
            pltpu.VMEM((half, cols), BF16),
            pltpu.VMEM((rows, half), BF16),
            *[pltpu.VMEM(term.shape, BF16) for term in terms],
            pltpu.SemaphoreType.DMA((2,)),
            pltpu.SemaphoreType.DMA((steps, count)),
            pltpu.SemaphoreType.DMA((steps,)),
        ],
    )


def note_product(scalars, grads, chunks, w_key, w_value, after, before=None, which=(0, 1)):
    nt = grads[0].shape[1]
    half = D // 2
    heads = [h for h0, hc in chunks for h in range(h0, h0 + hc)]
    hc = len(heads)
    last = before is not None
    start = which[0]

    def body(s_ref, *refs):
        grad_refs, refs = refs[: len(grads)], refs[len(grads) :]
        wk = jnp.concatenate([r[...] for r in refs[:hc]], axis=1)
        wv = jnp.concatenate([r[...] for r in refs[hc : 2 * hc]], axis=1)
        gk = jnp.concatenate([r[0] for r in grad_refs], axis=1)
        gv = jnp.concatenate([r[1] for r in grad_refs], axis=1)
        total = dot(gk, wk, NT) + dot(gv, wv, NT)
        if last:
            total = total + refs[2 * hc][0]
        out_ref = refs[-1]
        out_ref[0] = total.astype(out_ref.dtype)

    def weight_in(h):
        return pl.BlockSpec(
            (half, HD), lambda n, s: (jnp.where(n + start == 0, 1 - s[0], s[0]), h)
        )

    return call(
        body,
        (len(which),),
        [pl.BlockSpec(g.shape, lambda n, s: (0, 0, 0)) for g in grads]
        + [weight_in(h) for h in heads] * 2
        + ([pl.BlockSpec((1, nt, half), lambda n, s: (n + start, 0, 0))] if last else []),
        pl.BlockSpec((1, nt, half), lambda n, s: (n, 0, 0)),
        jax.ShapeDtypeStruct((len(which), nt, half), BF16 if last else F32),
        (scalars, *grads) + (w_key,) * hc + (w_value,) * hc + ((before,) if last else ()),
        "note_product",
        after,
        scalars=1,
    )


def attention_body(
    s_ref, band_ref, q_ref, g_ref, kvo_ref, kvn_ref, kvf_ref, dq_ref, own_ref, near_ref, far_ref,
    p_scr, ds_scr, bias_ref,
):
    @pl.when(pl.program_id(0) == 0)
    def _():
        row = lax.broadcasted_iota(jnp.int32, (8, BLK), 0)
        shard = s_ref[2]
        far = shard - 1 + 2 * s_ref[1]
        block = jnp.where(row < 2, 2 * shard, jnp.where(row < 4, 2 * (shard ^ 1), 2 * far)) + row % 2
        for b in range(q_ref.shape[0] // BLK):
            inside = (block >= band_ref[0, b]) & (block <= band_ref[1, b])
            bias_ref[:, b * BLK : (b + 1) * BLK] = jnp.where(inside, 0.0, -jnp.inf)

    scale2 = SCALE * LOG2E
    frames = q_ref.shape[0]
    nt = kvo_ref.shape[1]
    step = 256
    blocks = 3 * nt // BLK
    keys = jnp.concatenate([kvo_ref[0], kvn_ref[0], kvf_ref[0]], axis=0)
    values = jnp.concatenate([kvo_ref[1], kvn_ref[1], kvf_ref[1]], axis=0)
    for f in range(frames // step):
        cols = slice(f * step, (f + 1) * step)
        s = dot(keys, q_ref[cols, :], NT)
        gp = dot(values, g_ref[cols, :], NT)
        rows = [slice(j * BLK, (j + 1) * BLK) for j in range(blocks)]
        bias = [bias_ref[j : j + 1, cols] for j in range(blocks)]
        peak = None
        for j in range(blocks):
            top = jnp.max(s[rows[j]], axis=0, keepdims=True) + bias[j]
            peak = top if peak is None else jnp.maximum(peak, top)
        expos = []
        total = jnp.zeros((1, step), F32)
        mixed = jnp.zeros((1, step), F32)
        for j in range(blocks):
            e = jnp.exp2(s[rows[j]] * scale2 + (bias[j] - peak) * scale2)
            expos.append(e)
            total = total + jnp.sum(e, axis=0, keepdims=True)
            mixed = mixed + jnp.sum(e * gp[rows[j]], axis=0, keepdims=True)
        inv = 1.0 / total
        delta = mixed * inv
        for j in range(blocks):
            p = expos[j] * inv
            p_scr[rows[j], cols] = p.astype(BF16)
            ds_scr[rows[j], cols] = (p * (gp[rows[j]] - delta)).astype(BF16)
    dq_ref[...] = (dot(ds_scr[...], keys, TN) * SCALE).astype(BF16)
    dv = dot(p_scr[...], g_ref[...], NN)
    dk = dot(ds_scr[...], q_ref[...], NN) * SCALE
    for i, grad in enumerate((dk, dv)):
        own_ref[i] = grad[:nt]
        near_ref[i] = grad[nt : 2 * nt].astype(BF16)
        far_ref[i] = grad[2 * nt :].astype(BF16)


def attention(scalars, band, queries, grad_ctx, kv_own, kv_near, kv_far, h0, hc, after):
    frames = queries.shape[0]
    nt = kv_own.shape[1]
    frame_in = pl.BlockSpec((frames, HD), lambda h, s, b: (0, h0 + h))
    note_io = pl.BlockSpec((2, nt, HD), lambda h, s, b: (0, 0, h))
    notes_out = jax.ShapeDtypeStruct((2, nt, hc * HD), BF16)
    return call(
        attention_body,
        (hc,),
        [frame_in, frame_in, note_io, note_io, note_io],
        [pl.BlockSpec((frames, HD), lambda h, s, b: (0, h)), note_io, note_io, note_io],
        [
            jax.ShapeDtypeStruct((frames, hc * HD), BF16),
            jax.ShapeDtypeStruct((2, nt, hc * HD), F32),
            notes_out,
            notes_out,
        ],
        (scalars, band, queries, grad_ctx, kv_own, kv_near, kv_far),
        "attention",
        after,
        scalars=2,
        scratch=[
            pltpu.VMEM((3 * nt, frames), BF16),
            pltpu.VMEM((3 * nt, frames), BF16),
            pltpu.VMEM((8, frames), F32),
        ],
        flops=90 * frames * nt * hc * HD if h0 else 0,
    )


def per_device(notes, frames, w_query, w_key, w_value, w_out, band_blocks, grad_mixed):
    shard = lax.axis_index("seq")
    group = lax.axis_index("head")
    core = shard % 2
    scalars = jnp.stack([group, core, shard]).astype(jnp.int32)
    band = band_blocks[0]

    made0 = key_values(notes[0], w_key, w_value, *CHUNKS[0])
    made1, queries, given = key_values_and_queries(
        scalars, notes[0], w_key, w_value, frames[0], w_query, *CHUNKS[1], (made0,)
    )
    moved = [section_shift(made0, 1), section_shift(made1, 1)]
    w_mine = across(given)
    moved[0], queries = lax.optimization_barrier((moved[0], queries))
    near0, far0 = near_swap(moved[0]), far_swap(moved[0])
    grad_ctx = context_gradient(grad_mixed[0], w_out, (queries, moved[0]))
    moved[1], grad_ctx = lax.optimization_barrier((moved[1], grad_ctx))

    def attend(step, near, far, after):
        return attention(
            scalars, band, queries, grad_ctx, moved[step], near, far, *CHUNKS[step], after
        )

    def note_sum_of(own, near, far):
        return (own + near.astype(F32) + far.astype(F32)).astype(BF16)

    near1, far1 = near_swap(moved[1]), far_swap(moved[1])
    dq0, own0, rim_near0, rim_far0 = attend(0, near0, far0, ())
    dq0_other = head_swap(dq0)
    w_mine, dq0 = lax.optimization_barrier((w_mine, dq0))
    rim_near0, rim_far0, near1, far1 = lax.optimization_barrier((rim_near0, rim_far0, near1, far1))
    in_near0, in_far0 = near_swap(rim_near0), far_swap(rim_far0)
    dq1, own1, rim_near1, rim_far1 = attend(1, near1, far1, (dq0,))
    in_near0, in_far0, rim_near1, rim_far1 = lax.optimization_barrier(
        (in_near0, in_far0, rim_near1, rim_far1)
    )
    in_near1, in_far1 = near_swap(rim_near1), far_swap(rim_far1)
    owned0 = note_sum_of(own0, in_near0, in_far0)
    notes0 = section_shift(owned0, -1)
    dq1, owned0 = lax.optimization_barrier((dq1, owned0))
    dq1_other = head_swap(dq1)
    owned1 = note_sum_of(own1, in_near1, in_far1)
    owned1, dq0_other = lax.optimization_barrier((owned1, dq0_other))
    notes1 = section_shift(owned1, -1)

    own_part = frame_part(scalars, [dq0, dq1], [w_query], None, "frame_own", (owned1,))
    before = note_product(scalars, [notes0], CHUNKS[:1], w_key, w_value, (own_part,))
    last = (scalars, [notes1], CHUNKS[1:], w_key, w_value)
    w_mine, before = lax.optimization_barrier((w_mine, before))
    w_theirs = near_swap(w_mine)
    give_notes = note_product(*last, (), before, (0,))
    notes_other = head_swap(give_notes)
    keep_notes = note_product(*last, (give_notes,), before, (1,))
    frame_out = frame_part(
        scalars, [dq0_other, dq1_other], [w_mine, w_theirs], own_part, "frame_sum", (keep_notes,)
    )
    notes_other, frame_out = lax.optimization_barrier((notes_other, frame_out))
    note_out = keep_notes[0].astype(F32) + notes_other[0].astype(F32)
    return (frame_out[None], note_out.astype(BF16)[None])


def solution(mesh):
    placed = (
        P("section", "seq", None),
        P("section", "seq", None),
        P(None, "head"),
        P(None, "head"),
        P(None, "head"),
        P("head", None),
        P("section", None, "seq"),
        P("section", "seq", None),
    )
    return jax.shard_map(
        per_device,
        mesh=mesh,
        in_specs=placed,
        out_specs=(P("section", "seq", "head"), P("section", "seq", "head")),
        check_vma=False,
    )
```

```python
import jax
import jax.numpy as jnp
from jax import lax
from jax.experimental import pallas as pl
from jax.experimental.pallas import tpu as pltpu
from jax.sharding import PartitionSpec as P

D = 2048
HEADS = 16
BLK = 128
HD = D // HEADS
SCALE = HD**-0.5
LOG2E = 1.4426950408889634
CHUNKS = ((0, 4), (4, 4))
VMEM = 64 * 2**20 - 2**16

F32 = jnp.float32
BF16 = jnp.bfloat16
NN = (((1,), (0,)), ((), ()))
NT = (((1,), (1,)), ((), ()))
TN = (((0,), (0,)), ((), ()))


def dot(a, b, dims):
    return lax.dot_general(a, b, dims, preferred_element_type=F32)


def section_shift(block, distance):
    count = lax.axis_size("section")
    return lax.ppermute(
        block, "section", [(i, (i + distance) % count) for i in range(count)]
    )


def near_swap(block):
    count = lax.axis_size("seq")
    return lax.ppermute(block, "seq", [(i, i ^ 1) for i in range(count)])


def far_swap(block):
    count = lax.axis_size("seq")
    pairs = [(i, i + 1) for i in range(1, count - 1, 2)]
    return lax.ppermute(block, "seq", pairs + [(j, i) for i, j in pairs])


def head_swap(block):
    return lax.ppermute(block, "head", [(0, 1), (1, 0)])


def across(block):
    count = lax.axis_size("seq")
    route = [(2 * i + g, 2 * (i ^ 8) + 1 - g) for i in range(count) for g in range(2)]
    return lax.ppermute(block, ("seq", "head"), route)


def call(
    body, grid, in_specs, out_specs, out_shape, args, name, after=(), scalars=0, scratch=(),
    flops=0,
):
    first = scalars + len(in_specs)
    unread = len(after)

    def reads(*refs):
        body(*refs[:first], *refs[first + unread :])

    in_specs = list(in_specs) + [pl.BlockSpec(memory_space=pl.ANY)] * unread
    return pl.pallas_call(
        reads,
        grid_spec=pltpu.PrefetchScalarGridSpec(
            num_scalar_prefetch=scalars,
            grid=grid,
            in_specs=in_specs,
            out_specs=out_specs,
            scratch_shapes=scratch,
        ),
        out_shape=out_shape,
        compiler_params=pltpu.CompilerParams(vmem_limit_bytes=VMEM),
        cost_estimate=pl.CostEstimate(flops=flops, bytes_accessed=0, transcendentals=0),
        name=name,
    )(*args, *after)


def start_all(copies):
    for copy in copies:
        copy.start()
    return copies


def key_value_copies(wk_ref, wv_ref, wk_scr, wv_scr, sems, h0, hc):
    part = slice(h0 * HD, (h0 + hc) * HD)
    return start_all(
        [
            pltpu.make_async_copy(wk_ref.at[:, part], wk_scr, sems.at[0]),
            pltpu.make_async_copy(wv_ref.at[:, part], wv_scr, sems.at[1]),
        ]
    )


def key_values(notes, w_key, w_value, h0, hc):
    rows = notes.shape[0]

    def body(notes_ref, wk_ref, wv_ref, out_ref, n_scr, wk_scr, wv_scr, out_scr, sems):
        (notes_in,) = start_all([pltpu.make_async_copy(notes_ref, n_scr, sems.at[2])])
        weights_in = key_value_copies(wk_ref, wv_ref, wk_scr, wv_scr, sems, h0, hc)
        notes_in.wait()
        for i, scr in enumerate((wk_scr, wv_scr)):
            weights_in[i].wait()
            out_scr[i] = dot(n_scr[...], scr[...], NN).astype(BF16)
        for copy in start_all([pltpu.make_async_copy(out_scr, out_ref, sems.at[3])]):
            copy.wait()

    far = pl.BlockSpec(memory_space=pl.ANY)
    return call(
        body,
        (),
        [far] * 3,
        far,
        jax.ShapeDtypeStruct((2, rows, hc * HD), BF16),
        (notes, w_key, w_value),
        "key_values",
        scratch=[
            pltpu.VMEM((rows, D), BF16),
            pltpu.VMEM((D, hc * HD), BF16),
            pltpu.VMEM((D, hc * HD), BF16),
            pltpu.VMEM((2, rows, hc * HD), BF16),
            pltpu.SemaphoreType.DMA((4,)),
        ],
    )


class Product:
    step = 256
    parts = 2

    def __init__(self, rows_in, weight, dims):
        self.dims = dims
        self.steps = rows_in.shape[0] // self.step
        self.size = D // 2 // self.parts
        self.out = jax.ShapeDtypeStruct((rows_in.shape[0], D // 2), BF16)
        self.scratch = [
            pltpu.VMEM(rows_in.shape, BF16),
            pltpu.VMEM(weight.shape, BF16),
            pltpu.VMEM(self.out.shape, BF16),
            pltpu.SemaphoreType.DMA((self.parts,)),
            pltpu.SemaphoreType.DMA((self.steps,)),
            pltpu.SemaphoreType.DMA((self.steps,)),
        ]

    def rows(self, m):
        return slice(m * self.step, (m + 1) * self.step)

    def part(self, p):
        cols = slice(p * self.size, (p + 1) * self.size)
        return (slice(None), cols) if self.dims is NN else (cols, slice(None))

    def start(self, a_ref, w_ref, a_scr, w_scr, o_scr, w_sems, row_sems, out_sems):
        rows_in = [
            pltpu.make_async_copy(a_ref.at[self.rows(m)], a_scr.at[self.rows(m)], row_sems.at[m])
            for m in range(self.steps)
        ]
        weight_in = [
            pltpu.make_async_copy(w_ref.at[self.part(p)], w_scr.at[self.part(p)], w_sems.at[p])
            for p in range(self.parts)
        ]
        start_all(rows_in[:1] + weight_in + rows_in[1:])
        return rows_in, weight_in

    def finish(self, copies, out_ref, a_scr, w_scr, o_scr, w_sems, row_sems, out_sems):
        rows_in, weight_in = copies
        sent = []
        for m in range(self.steps):
            at = self.rows(m)
            rows_in[m].wait()
            for p in range(self.parts):
                if m == 0:
                    weight_in[p].wait()
                cols = slice(p * self.size, (p + 1) * self.size)
                term = dot(a_scr[at, :], w_scr[self.part(p)], self.dims)
                o_scr[at, cols] = term.astype(BF16)
            copy = pltpu.make_async_copy(o_scr.at[at], out_ref.at[at], out_sems.at[m])
            sent += start_all([copy])
        return sent


def key_values_and_queries(scalars, notes, w_key, w_value, frames, w_query, h0, hc, after):
    rows = notes.shape[0]
    quarter = D // 4
    product = Product(frames, w_query, NN)

    def body(s_ref, notes_ref, wk_ref, wv_ref, f_ref, wq_ref, out_ref, q_ref, give_ref,
             n_scr, wk_scr, wv_scr, out_scr, sems, *scrs):
        (notes_in,) = start_all([pltpu.make_async_copy(notes_ref, n_scr, sems.at[2])])
        weights_in = key_value_copies(wk_ref, wv_ref, wk_scr, wv_scr, sems, h0, hc)
        copies = product.start(f_ref, wq_ref, *scrs)
        notes_in.wait()
        for i, scr in enumerate((wk_scr, wv_scr)):
            weights_in[i].wait()
            out_scr[i] = dot(n_scr[...], scr[...], NN).astype(BF16)
        sent = start_all([pltpu.make_async_copy(out_scr, out_ref, sems.at[3])])
        sent += product.finish(copies, q_ref, *scrs)
        offset = pl.multiple_of((1 - s_ref[0]) * (2 * quarter) + s_ref[1] * quarter, quarter)
        give = pltpu.make_async_copy(scrs[1].at[pl.ds(offset, quarter), :], give_ref, sems.at[4])
        sent += start_all([give])
        for copy in sent:
            copy.wait()

    far = pl.BlockSpec(memory_space=pl.ANY)
    return call(
        body,
        (),
        [far] * 5,
        [far] * 3,
        [
            jax.ShapeDtypeStruct((2, rows, hc * HD), BF16),
            product.out,
            jax.ShapeDtypeStruct((quarter, w_query.shape[1]), BF16),
        ],
        (scalars, notes, w_key, w_value, frames, w_query),
        "key_values_and_queries",
        after,
        scalars=1,
        scratch=[
            pltpu.VMEM((rows, D), BF16),
            pltpu.VMEM((D, hc * HD), BF16),
            pltpu.VMEM((D, hc * HD), BF16),
            pltpu.VMEM((2, rows, hc * HD), BF16),
            pltpu.SemaphoreType.DMA((5,)),
            *product.scratch,
        ],
    )


def context_gradient(grad_mixed, w_out, after):
    product = Product(grad_mixed, w_out, NT)

    def body(a_ref, w_ref, out_ref, *scrs):
        copies = product.start(a_ref, w_ref, *scrs)
        for copy in product.finish(copies, out_ref, *scrs):
            copy.wait()

    far = pl.BlockSpec(memory_space=pl.ANY)
    return call(
        body, (), [far] * 2, far, product.out, (grad_mixed, w_out), "grad_ctx", after,
        scratch=product.scratch,
    )


def frame_part(scalars, grads, weights, own, name, after):
    rows = grads[0].shape[0]
    half = D // 2
    cols = sum(g.shape[1] for g in grads)
    quarter = half // 2
    step = 256
    steps = rows // step
    terms = list(grads) + ([] if own is None else [own])
    count = len(terms)

    def body(s_ref, *refs):
        term_refs, refs = refs[:count], refs[count:]
        weight_refs, refs = refs[: len(weights)], refs[len(weights) :]
        out_ref, w_scr, o_scr, *refs = refs
        term_scrs, (w_sems, term_sems, out_sems) = refs[:count], refs[count:]
        weight_copies = []
        for p in range(2):
            if own is None:
                at = pl.ds(pl.multiple_of(s_ref[0] * half + p * quarter, quarter), quarter)
                src, dst = weight_refs[0].at[at], w_scr.at[p * quarter : (p + 1) * quarter]
            else:
                core = s_ref[1] if p == 0 else 1 - s_ref[1]
                to = pl.ds(pl.multiple_of(core * quarter, quarter), quarter)
                src, dst = weight_refs[p], w_scr.at[to]
            weight_copies.append(pltpu.make_async_copy(src, dst, w_sems.at[p]))
        for copy in weight_copies:
            copy.start()
        term_copies = []
        for m in range(steps):
            at = slice(m * step, (m + 1) * step)
            for t in range(count):
                copy = pltpu.make_async_copy(term_refs[t].at[at], term_scrs[t].at[at], term_sems.at[m, t])
                copy.start()
                term_copies.append(copy)
        for copy in weight_copies:
            copy.wait()
        sent = []
        for m in range(steps):
            at = slice(m * step, (m + 1) * step)
            for t in range(count):
                term_copies[m * count + t].wait()
            left = jnp.concatenate([scr[at, :] for scr in term_scrs[: len(grads)]], axis=1)
            total = dot(left, w_scr[...], NT)
            if own is not None:
                total = total + term_scrs[-1][at, :].astype(F32)
            o_scr[at, :] = total.astype(BF16)
            copy = pltpu.make_async_copy(o_scr.at[at], out_ref.at[at], out_sems.at[m])
            copy.start()
            sent.append(copy)
        for copy in sent:
            copy.wait()

    far = pl.BlockSpec(memory_space=pl.ANY)
    return call(
        body,
        (),
        [far] * (count + len(weights)),
        far,
        jax.ShapeDtypeStruct((rows, half), BF16),
        (scalars, *terms, *weights),
        name,
        after,
        scalars=1,
        flops=8 * rows * half * cols if own is None else 0,
        scratch=[
            pltpu.VMEM((half, cols), BF16),
            pltpu.VMEM((rows, half), BF16),
            *[pltpu.VMEM(term.shape, BF16) for term in terms],
            pltpu.SemaphoreType.DMA((2,)),
            pltpu.SemaphoreType.DMA((steps, count)),
            pltpu.SemaphoreType.DMA((steps,)),
        ],
    )


def note_product(scalars, grads, chunks, w_key, w_value, after, before=None, which=(0, 1)):
    nt = grads[0].shape[1]
    half = D // 2
    heads = [h for h0, hc in chunks for h in range(h0, h0 + hc)]
    hc = len(heads)
    last = before is not None
    start = which[0]

    def body(s_ref, *refs):
        grad_refs, refs = refs[: len(grads)], refs[len(grads) :]
        wk = jnp.concatenate([r[...] for r in refs[:hc]], axis=1)
        wv = jnp.concatenate([r[...] for r in refs[hc : 2 * hc]], axis=1)
        gk = jnp.concatenate([r[0] for r in grad_refs], axis=1)
        gv = jnp.concatenate([r[1] for r in grad_refs], axis=1)
        total = dot(gk, wk, NT) + dot(gv, wv, NT)
        if last:
            total = total + refs[2 * hc][0]
        out_ref = refs[-1]
        out_ref[0] = total.astype(out_ref.dtype)

    def weight_in(h):
        return pl.BlockSpec(
            (half, HD), lambda n, s: (jnp.where(n + start == 0, 1 - s[0], s[0]), h)
        )

    return call(
        body,
        (len(which),),
        [pl.BlockSpec(g.shape, lambda n, s: (0, 0, 0)) for g in grads]
        + [weight_in(h) for h in heads] * 2
        + ([pl.BlockSpec((1, nt, half), lambda n, s: (n + start, 0, 0))] if last else []),
        pl.BlockSpec((1, nt, half), lambda n, s: (n, 0, 0)),
        jax.ShapeDtypeStruct((len(which), nt, half), BF16 if last else F32),
        (scalars, *grads) + (w_key,) * hc + (w_value,) * hc + ((before,) if last else ()),
        "note_product",
        after,
        scalars=1,
    )


def attention_body(
    s_ref, band_ref, q_ref, g_ref, kvo_ref, kvn_ref, kvf_ref, dq_ref, own_ref, near_ref, far_ref,
    p_scr, ds_scr, bias_ref,
):
    @pl.when(pl.program_id(0) == 0)
    def _():
        row = lax.broadcasted_iota(jnp.int32, (8, BLK), 0)
        shard = s_ref[2]
        far = shard - 1 + 2 * s_ref[1]
        block = jnp.where(row < 2, 2 * shard, jnp.where(row < 4, 2 * (shard ^ 1), 2 * far)) + row % 2
        for b in range(q_ref.shape[0] // BLK):
            inside = (block >= band_ref[0, b]) & (block <= band_ref[1, b])
            bias_ref[:, b * BLK : (b + 1) * BLK] = jnp.where(inside, 0.0, -jnp.inf)

    scale2 = SCALE * LOG2E
    frames = q_ref.shape[0]
    nt = kvo_ref.shape[1]
    step = 256
    blocks = 3 * nt // BLK
    keys = jnp.concatenate([kvo_ref[0], kvn_ref[0], kvf_ref[0]], axis=0)
    values = jnp.concatenate([kvo_ref[1], kvn_ref[1], kvf_ref[1]], axis=0)
    for f in range(frames // step):
        cols = slice(f * step, (f + 1) * step)
        s = dot(keys, q_ref[cols, :], NT)
        gp = dot(values, g_ref[cols, :], NT)
        rows = [slice(j * BLK, (j + 1) * BLK) for j in range(blocks)]
        bias = [bias_ref[j : j + 1, cols] for j in range(blocks)]
        peak = None
        for j in range(blocks):
            top = jnp.max(s[rows[j]], axis=0, keepdims=True) + bias[j]
            peak = top if peak is None else jnp.maximum(peak, top)
        expos = []
        total = jnp.zeros((1, step), F32)
        mixed = jnp.zeros((1, step), F32)
        for j in range(blocks):
            e = jnp.exp2(s[rows[j]] * scale2 + (bias[j] - peak) * scale2)
            expos.append(e)
            total = total + jnp.sum(e, axis=0, keepdims=True)
            mixed = mixed + jnp.sum(e * gp[rows[j]], axis=0, keepdims=True)
        inv = 1.0 / total
        delta = mixed * inv
        for j in range(blocks):
            p = expos[j] * inv
            p_scr[rows[j], cols] = p.astype(BF16)
            ds_scr[rows[j], cols] = (p * (gp[rows[j]] - delta)).astype(BF16)
    dq_ref[...] = (dot(ds_scr[...], keys, TN) * SCALE).astype(BF16)
    dv = dot(p_scr[...], g_ref[...], NN)
    dk = dot(ds_scr[...], q_ref[...], NN) * SCALE
    for i, grad in enumerate((dk, dv)):
        own_ref[i] = grad[:nt]
        near_ref[i] = grad[nt : 2 * nt].astype(BF16)
        far_ref[i] = grad[2 * nt :].astype(BF16)


def attention(scalars, band, queries, grad_ctx, kv_own, kv_near, kv_far, h0, hc, after):
    frames = queries.shape[0]
    nt = kv_own.shape[1]
    frame_in = pl.BlockSpec((frames, HD), lambda h, s, b: (0, h0 + h))
    note_io = pl.BlockSpec((2, nt, HD), lambda h, s, b: (0, 0, h))
    notes_out = jax.ShapeDtypeStruct((2, nt, hc * HD), BF16)
    return call(
        attention_body,
        (hc,),
        [frame_in, frame_in, note_io, note_io, note_io],
        [pl.BlockSpec((frames, HD), lambda h, s, b: (0, h)), note_io, note_io, note_io],
        [
            jax.ShapeDtypeStruct((frames, hc * HD), BF16),
            jax.ShapeDtypeStruct((2, nt, hc * HD), F32),
            notes_out,
            notes_out,
        ],
        (scalars, band, queries, grad_ctx, kv_own, kv_near, kv_far),
        "attention",
        after,
        scalars=2,
        scratch=[
            pltpu.VMEM((3 * nt, frames), BF16),
            pltpu.VMEM((3 * nt, frames), BF16),
            pltpu.VMEM((8, frames), F32),
        ],
        flops=90 * frames * nt * hc * HD if h0 else 0,
    )


def per_device(notes, frames, w_query, w_key, w_value, w_out, band_blocks, grad_mixed):
    shard = lax.axis_index("seq")
    group = lax.axis_index("head")
    core = shard % 2
    scalars = jnp.stack([group, core, shard]).astype(jnp.int32)
    band = band_blocks[0]

    made0 = key_values(notes[0], w_key, w_value, *CHUNKS[0])
    made1, queries, given = key_values_and_queries(
        scalars, notes[0], w_key, w_value, frames[0], w_query, *CHUNKS[1], (made0,)
    )
    moved = [section_shift(made0, 1), section_shift(made1, 1)]
    w_mine = across(given)
    moved[0], queries = lax.optimization_barrier((moved[0], queries))
    near0, far0 = near_swap(moved[0]), far_swap(moved[0])
    grad_ctx = context_gradient(grad_mixed[0], w_out, (queries, moved[0]))
    moved[1], grad_ctx = lax.optimization_barrier((moved[1], grad_ctx))

    def attend(step, near, far, after):
        return attention(
            scalars, band, queries, grad_ctx, moved[step], near, far, *CHUNKS[step], after
        )

    def note_sum_of(own, near, far):
        return (own + near.astype(F32) + far.astype(F32)).astype(BF16)

    near1, far1 = near_swap(moved[1]), far_swap(moved[1])
    dq0, own0, rim_near0, rim_far0 = attend(0, near0, far0, ())
    dq0_other = head_swap(dq0)
    w_mine, dq0 = lax.optimization_barrier((w_mine, dq0))
    rim_near0, rim_far0, near1, far1 = lax.optimization_barrier((rim_near0, rim_far0, near1, far1))
    in_near0, in_far0 = near_swap(rim_near0), far_swap(rim_far0)
    dq1, own1, rim_near1, rim_far1 = attend(1, near1, far1, (dq0,))
    in_near0, in_far0, rim_near1, rim_far1 = lax.optimization_barrier(
        (in_near0, in_far0, rim_near1, rim_far1)
    )
    in_near1, in_far1 = near_swap(rim_near1), far_swap(rim_far1)
    owned0 = note_sum_of(own0, in_near0, in_far0)
    notes0 = section_shift(owned0, -1)
    dq1, owned0 = lax.optimization_barrier((dq1, owned0))
    dq1_other = head_swap(dq1)
    owned1 = note_sum_of(own1, in_near1, in_far1)
    notes1 = section_shift(owned1, -1)

    before = note_product(scalars, [notes0], CHUNKS[:1], w_key, w_value, (owned1,))
    own_part = frame_part(
        scalars, [dq0, dq1], [w_query], None, "frame_own", (before, dq0_other)
    )
    last = (scalars, [notes1], CHUNKS[1:], w_key, w_value)
    w_mine, own_part = lax.optimization_barrier((w_mine, own_part))
    w_theirs = near_swap(w_mine)
    give_notes = note_product(*last, (own_part,), before, (0,))
    notes_other = head_swap(give_notes)
    keep_notes = note_product(*last, (give_notes,), before, (1,))
    frame_out = frame_part(
        scalars, [dq0_other, dq1_other], [w_mine, w_theirs], own_part, "frame_sum", (keep_notes,)
    )
    notes_other, frame_out = lax.optimization_barrier((notes_other, frame_out))
    note_out = keep_notes[0].astype(F32) + notes_other[0].astype(F32)
    return (frame_out[None], note_out.astype(BF16)[None])


def solution(mesh):
    placed = (
        P("section", "seq", None),
        P("section", "seq", None),
        P(None, "head"),
        P(None, "head"),
        P(None, "head"),
        P("head", None),
        P("section", None, "seq"),
        P("section", "seq", None),
    )
    return jax.shard_map(
        per_device,
        mesh=mesh,
        in_specs=placed,
        out_specs=(P("section", "seq", "head"), P("section", "seq", "head")),
        check_vma=False,
    )
```

```python
import jax
import jax.numpy as jnp
from jax import lax
from jax.experimental import pallas as pl
from jax.experimental.pallas import tpu as pltpu
from jax.sharding import PartitionSpec as P

D = 2048
HEADS = 16
BLK = 128
HD = D // HEADS
SCALE = HD**-0.5
LOG2E = 1.4426950408889634
CHUNKS = ((0, 4), (4, 4))
VMEM = 64 * 2**20 - 2**16

F32 = jnp.float32
BF16 = jnp.bfloat16
NN = (((1,), (0,)), ((), ()))
NT = (((1,), (1,)), ((), ()))
TN = (((0,), (0,)), ((), ()))


def dot(a, b, dims):
    return lax.dot_general(a, b, dims, preferred_element_type=F32)


def section_shift(block, distance):
    count = lax.axis_size("section")
    return lax.ppermute(
        block, "section", [(i, (i + distance) % count) for i in range(count)]
    )


def near_swap(block):
    count = lax.axis_size("seq")
    return lax.ppermute(block, "seq", [(i, i ^ 1) for i in range(count)])


def far_swap(block):
    count = lax.axis_size("seq")
    pairs = [(i, i + 1) for i in range(1, count - 1, 2)]
    return lax.ppermute(block, "seq", pairs + [(j, i) for i, j in pairs])


def head_swap(block):
    return lax.ppermute(block, "head", [(0, 1), (1, 0)])


def across(block):
    count = lax.axis_size("seq")
    route = [(2 * i + g, 2 * (i ^ 8) + 1 - g) for i in range(count) for g in range(2)]
    return lax.ppermute(block, ("seq", "head"), route)


def call(
    body, grid, in_specs, out_specs, out_shape, args, name, after=(), scalars=0, scratch=(),
    flops=0,
):
    first = scalars + len(in_specs)
    unread = len(after)

    def reads(*refs):
        body(*refs[:first], *refs[first + unread :])

    in_specs = list(in_specs) + [pl.BlockSpec(memory_space=pl.ANY)] * unread
    return pl.pallas_call(
        reads,
        grid_spec=pltpu.PrefetchScalarGridSpec(
            num_scalar_prefetch=scalars,
            grid=grid,
            in_specs=in_specs,
            out_specs=out_specs,
            scratch_shapes=scratch,
        ),
        out_shape=out_shape,
        compiler_params=pltpu.CompilerParams(vmem_limit_bytes=VMEM),
        cost_estimate=pl.CostEstimate(flops=flops, bytes_accessed=0, transcendentals=0),
        name=name,
    )(*args, *after)


def start_all(copies):
    for copy in copies:
        copy.start()
    return copies


def key_value_copies(wk_ref, wv_ref, wk_scr, wv_scr, sems, h0, hc):
    part = slice(h0 * HD, (h0 + hc) * HD)
    return start_all(
        [
            pltpu.make_async_copy(wk_ref.at[:, part], wk_scr, sems.at[0]),
            pltpu.make_async_copy(wv_ref.at[:, part], wv_scr, sems.at[1]),
        ]
    )


def key_values(notes, w_key, w_value, h0, hc):
    rows = notes.shape[0]

    def body(notes_ref, wk_ref, wv_ref, out_ref, n_scr, wk_scr, wv_scr, out_scr, sems):
        (notes_in,) = start_all([pltpu.make_async_copy(notes_ref, n_scr, sems.at[2])])
        weights_in = key_value_copies(wk_ref, wv_ref, wk_scr, wv_scr, sems, h0, hc)
        notes_in.wait()
        for i, scr in enumerate((wk_scr, wv_scr)):
            weights_in[i].wait()
            out_scr[i] = dot(n_scr[...], scr[...], NN).astype(BF16)
        for copy in start_all([pltpu.make_async_copy(out_scr, out_ref, sems.at[3])]):
            copy.wait()

    far = pl.BlockSpec(memory_space=pl.ANY)
    return call(
        body,
        (),
        [far] * 3,
        far,
        jax.ShapeDtypeStruct((2, rows, hc * HD), BF16),
        (notes, w_key, w_value),
        "key_values",
        scratch=[
            pltpu.VMEM((rows, D), BF16),
            pltpu.VMEM((D, hc * HD), BF16),
            pltpu.VMEM((D, hc * HD), BF16),
            pltpu.VMEM((2, rows, hc * HD), BF16),
            pltpu.SemaphoreType.DMA((4,)),
        ],
    )


class Product:
    step = 256
    parts = 2

    def __init__(self, rows_in, weight, dims):
        self.dims = dims
        self.steps = rows_in.shape[0] // self.step
        self.size = D // 2 // self.parts
        self.out = jax.ShapeDtypeStruct((rows_in.shape[0], D // 2), BF16)
        self.scratch = [
            pltpu.VMEM(rows_in.shape, BF16),
            pltpu.VMEM(weight.shape, BF16),
            pltpu.VMEM(self.out.shape, BF16),
            pltpu.SemaphoreType.DMA((self.parts,)),
            pltpu.SemaphoreType.DMA((self.steps,)),
            pltpu.SemaphoreType.DMA((self.steps,)),
        ]

    def rows(self, m):
        return slice(m * self.step, (m + 1) * self.step)

    def part(self, p):
        cols = slice(p * self.size, (p + 1) * self.size)
        return (slice(None), cols) if self.dims is NN else (cols, slice(None))

    def start(self, a_ref, w_ref, a_scr, w_scr, o_scr, w_sems, row_sems, out_sems):
        rows_in = [
            pltpu.make_async_copy(a_ref.at[self.rows(m)], a_scr.at[self.rows(m)], row_sems.at[m])
            for m in range(self.steps)
        ]
        weight_in = [
            pltpu.make_async_copy(w_ref.at[self.part(p)], w_scr.at[self.part(p)], w_sems.at[p])
            for p in range(self.parts)
        ]
        start_all(rows_in[:1] + weight_in + rows_in[1:])
        return rows_in, weight_in

    def finish(self, copies, out_ref, a_scr, w_scr, o_scr, w_sems, row_sems, out_sems):
        rows_in, weight_in = copies
        sent = []
        for m in range(self.steps):
            at = self.rows(m)
            rows_in[m].wait()
            for p in range(self.parts):
                if m == 0:
                    weight_in[p].wait()
                cols = slice(p * self.size, (p + 1) * self.size)
                term = dot(a_scr[at, :], w_scr[self.part(p)], self.dims)
                o_scr[at, cols] = term.astype(BF16)
            copy = pltpu.make_async_copy(o_scr.at[at], out_ref.at[at], out_sems.at[m])
            sent += start_all([copy])
        return sent


def key_values_and_queries(notes, w_key, w_value, frames, w_query, h0, hc, after):
    rows = notes.shape[0]
    quarter = D // 4
    product = Product(frames, w_query, NN)

    def body(notes_ref, wk_ref, wv_ref, f_ref, wq_ref, out_ref, q_ref, give_ref,
             n_scr, wk_scr, wv_scr, out_scr, sems, *scrs):
        (notes_in,) = start_all([pltpu.make_async_copy(notes_ref, n_scr, sems.at[2])])
        weights_in = key_value_copies(wk_ref, wv_ref, wk_scr, wv_scr, sems, h0, hc)
        copies = product.start(f_ref, wq_ref, *scrs)
        notes_in.wait()
        for i, scr in enumerate((wk_scr, wv_scr)):
            weights_in[i].wait()
            out_scr[i] = dot(n_scr[...], scr[...], NN).astype(BF16)
        sent = start_all([pltpu.make_async_copy(out_scr, out_ref, sems.at[3])])
        sent += product.finish(copies, q_ref, *scrs)
        group = lax.axis_index("head")
        core = lax.rem(lax.axis_index("seq"), 2)
        offset = pl.multiple_of((1 - group) * (2 * quarter) + core * quarter, quarter)
        give = pltpu.make_async_copy(scrs[1].at[pl.ds(offset, quarter), :], give_ref, sems.at[4])
        sent += start_all([give])
        for copy in sent:
            copy.wait()

    far = pl.BlockSpec(memory_space=pl.ANY)
    return call(
        body,
        (),
        [far] * 5,
        [far] * 3,
        [
            jax.ShapeDtypeStruct((2, rows, hc * HD), BF16),
            product.out,
            jax.ShapeDtypeStruct((quarter, w_query.shape[1]), BF16),
        ],
        (notes, w_key, w_value, frames, w_query),
        "key_values_and_queries",
        after,
        scratch=[
            pltpu.VMEM((rows, D), BF16),
            pltpu.VMEM((D, hc * HD), BF16),
            pltpu.VMEM((D, hc * HD), BF16),
            pltpu.VMEM((2, rows, hc * HD), BF16),
            pltpu.SemaphoreType.DMA((5,)),
            *product.scratch,
        ],
    )


def context_gradient(grad_mixed, w_out, after):
    product = Product(grad_mixed, w_out, NT)

    def body(a_ref, w_ref, out_ref, *scrs):
        copies = product.start(a_ref, w_ref, *scrs)
        for copy in product.finish(copies, out_ref, *scrs):
            copy.wait()

    far = pl.BlockSpec(memory_space=pl.ANY)
    return call(
        body, (), [far] * 2, far, product.out, (grad_mixed, w_out), "grad_ctx", after,
        scratch=product.scratch,
    )


def frame_part(scalars, grads, weights, own, name, after):
    rows = grads[0].shape[0]
    half = D // 2
    cols = sum(g.shape[1] for g in grads)
    quarter = half // 2
    step = 256
    steps = rows // step
    terms = list(grads) + ([] if own is None else [own])
    count = len(terms)

    def body(s_ref, *refs):
        term_refs, refs = refs[:count], refs[count:]
        weight_refs, refs = refs[: len(weights)], refs[len(weights) :]
        out_ref, w_scr, o_scr, *refs = refs
        term_scrs, (w_sems, term_sems, out_sems) = refs[:count], refs[count:]
        weight_copies = []
        for p in range(2):
            if own is None:
                at = pl.ds(pl.multiple_of(s_ref[0] * half + p * quarter, quarter), quarter)
                src, dst = weight_refs[0].at[at], w_scr.at[p * quarter : (p + 1) * quarter]
            else:
                core = s_ref[1] if p == 0 else 1 - s_ref[1]
                to = pl.ds(pl.multiple_of(core * quarter, quarter), quarter)
                src, dst = weight_refs[p], w_scr.at[to]
            weight_copies.append(pltpu.make_async_copy(src, dst, w_sems.at[p]))
        for copy in weight_copies:
            copy.start()
        term_copies = []
        for m in range(steps):
            at = slice(m * step, (m + 1) * step)
            for t in range(count):
                copy = pltpu.make_async_copy(term_refs[t].at[at], term_scrs[t].at[at], term_sems.at[m, t])
                copy.start()
                term_copies.append(copy)
        for copy in weight_copies:
            copy.wait()
        sent = []
        for m in range(steps):
            at = slice(m * step, (m + 1) * step)
            for t in range(count):
                term_copies[m * count + t].wait()
            left = jnp.concatenate([scr[at, :] for scr in term_scrs[: len(grads)]], axis=1)
            total = dot(left, w_scr[...], NT)
            if own is not None:
                total = total + term_scrs[-1][at, :].astype(F32)
            o_scr[at, :] = total.astype(BF16)
            copy = pltpu.make_async_copy(o_scr.at[at], out_ref.at[at], out_sems.at[m])
            copy.start()
            sent.append(copy)
        for copy in sent:
            copy.wait()

    far = pl.BlockSpec(memory_space=pl.ANY)
    return call(
        body,
        (),
        [far] * (count + len(weights)),
        far,
        jax.ShapeDtypeStruct((rows, half), BF16),
        (scalars, *terms, *weights),
        name,
        after,
        scalars=1,
        flops=8 * rows * half * cols if own is None else 0,
        scratch=[
            pltpu.VMEM((half, cols), BF16),
            pltpu.VMEM((rows, half), BF16),
            *[pltpu.VMEM(term.shape, BF16) for term in terms],
            pltpu.SemaphoreType.DMA((2,)),
            pltpu.SemaphoreType.DMA((steps, count)),
            pltpu.SemaphoreType.DMA((steps,)),
        ],
    )


def note_product(scalars, grads, chunks, w_key, w_value, after, before=None, which=(0, 1)):
    nt = grads[0].shape[1]
    half = D // 2
    ((h0, hc),) = chunks
    last = before is not None
    start = which[0]

    def body(s_ref, *refs):
        grad_refs, refs = refs[: len(grads)], refs[len(grads) :]
        grad_ref = grad_refs[0]
        total = dot(grad_ref[0], refs[0][...], NT) + dot(grad_ref[1], refs[1][...], NT)
        if last:
            total = total + refs[2][0]
        out_ref = refs[-1]
        out_ref[0] = total.astype(out_ref.dtype)

    weight_in = pl.BlockSpec(
        (half, hc * HD), lambda n, s: (jnp.where(n + start == 0, 1 - s[0], s[0]), h0 // hc)
    )

    return call(
        body,
        (len(which),),
        [pl.BlockSpec(g.shape, lambda n, s: (0, 0, 0)) for g in grads]
        + [weight_in] * 2
        + ([pl.BlockSpec((1, nt, half), lambda n, s: (n + start, 0, 0))] if last else []),
        pl.BlockSpec((1, nt, half), lambda n, s: (n, 0, 0)),
        jax.ShapeDtypeStruct((len(which), nt, half), BF16 if last else F32),
        (scalars, *grads, w_key, w_value) + ((before,) if last else ()),
        "note_product",
        after,
        scalars=1,
    )


def attention_body(
    band_ref, q_ref, g_ref, kvo_ref, kvn_ref, kvf_ref, dq_ref, own_ref, near_ref, far_ref,
    p_scr, ds_scr, bias_ref,
):
    @pl.when(pl.program_id(0) == 0)
    def _():
        row = lax.broadcasted_iota(jnp.int32, (8, BLK), 0)
        shard = lax.axis_index("seq")
        far = shard - 1 + 2 * lax.rem(shard, 2)
        block = jnp.where(row < 2, 2 * shard, jnp.where(row < 4, 2 * (shard ^ 1), 2 * far)) + row % 2
        for b in range(q_ref.shape[0] // BLK):
            inside = (block >= band_ref[0, b]) & (block <= band_ref[1, b])
            bias_ref[:, b * BLK : (b + 1) * BLK] = jnp.where(inside, 0.0, -jnp.inf)

    scale2 = SCALE * LOG2E
    frames = q_ref.shape[0]
    nt = kvo_ref.shape[1]
    step = 256
    blocks = 3 * nt // BLK
    keys = jnp.concatenate([kvo_ref[0], kvn_ref[0], kvf_ref[0]], axis=0)
    values = jnp.concatenate([kvo_ref[1], kvn_ref[1], kvf_ref[1]], axis=0)
    for f in range(frames // step):
        cols = slice(f * step, (f + 1) * step)
        s = dot(keys, q_ref[cols, :], NT)
        gp = dot(values, g_ref[cols, :], NT)
        rows = [slice(j * BLK, (j + 1) * BLK) for j in range(blocks)]
        bias = [bias_ref[j : j + 1, cols] for j in range(blocks)]
        peak = None
        for j in range(blocks):
            top = jnp.max(s[rows[j]], axis=0, keepdims=True) + bias[j]
            peak = top if peak is None else jnp.maximum(peak, top)
        expos = []
        total = jnp.zeros((1, step), F32)
        mixed = jnp.zeros((1, step), F32)
        for j in range(blocks):
            e = jnp.exp2(s[rows[j]] * scale2 + (bias[j] - peak) * scale2)
            expos.append(e)
            total = total + jnp.sum(e, axis=0, keepdims=True)
            mixed = mixed + jnp.sum(e * gp[rows[j]], axis=0, keepdims=True)
        inv = 1.0 / total
        delta = mixed * inv
        for j in range(blocks):
            p = expos[j] * inv
            p_scr[rows[j], cols] = p.astype(BF16)
            ds_scr[rows[j], cols] = (p * (gp[rows[j]] - delta)).astype(BF16)
    dq_ref[...] = (dot(ds_scr[...], keys, TN) * SCALE).astype(BF16)
    dv = dot(p_scr[...], g_ref[...], NN)
    dk = dot(ds_scr[...], q_ref[...], NN) * SCALE
    for i, grad in enumerate((dk, dv)):
        own_ref[i] = grad[:nt]
        near_ref[i] = grad[nt : 2 * nt].astype(BF16)
        far_ref[i] = grad[2 * nt :].astype(BF16)


def attention(band, queries, grad_ctx, kv_own, kv_near, kv_far, h0, hc, after):
    frames = queries.shape[0]
    nt = kv_own.shape[1]
    frame_in = pl.BlockSpec((frames, HD), lambda h, b: (0, h0 + h))
    note_io = pl.BlockSpec((2, nt, HD), lambda h, b: (0, 0, h))
    notes_out = jax.ShapeDtypeStruct((2, nt, hc * HD), BF16)
    return call(
        attention_body,
        (hc,),
        [frame_in, frame_in, note_io, note_io, note_io],
        [pl.BlockSpec((frames, HD), lambda h, b: (0, h)), note_io, note_io, note_io],
        [
            jax.ShapeDtypeStruct((frames, hc * HD), BF16),
            jax.ShapeDtypeStruct((2, nt, hc * HD), F32),
            notes_out,
            notes_out,
        ],
        (band, queries, grad_ctx, kv_own, kv_near, kv_far),
        "attention",
        after,
        scalars=1,
        scratch=[
            pltpu.VMEM((3 * nt, frames), BF16),
            pltpu.VMEM((3 * nt, frames), BF16),
            pltpu.VMEM((8, frames), F32),
        ],
        flops=90 * frames * nt * hc * HD if h0 else 0,
    )


def per_device(notes, frames, w_query, w_key, w_value, w_out, band_blocks, grad_mixed):
    shard = lax.axis_index("seq")
    group = lax.axis_index("head")
    core = shard % 2
    scalars = jnp.stack([group, core, shard]).astype(jnp.int32)
    band = band_blocks[0]

    made0 = key_values(notes[0], w_key, w_value, *CHUNKS[0])
    made1, queries, given = key_values_and_queries(
        notes[0], w_key, w_value, frames[0], w_query, *CHUNKS[1], (made0,)
    )
    moved = [section_shift(made0, 1), section_shift(made1, 1)]
    w_mine = across(given)
    moved[0], queries = lax.optimization_barrier((moved[0], queries))
    near0, far0 = near_swap(moved[0]), far_swap(moved[0])
    grad_ctx = context_gradient(grad_mixed[0], w_out, (queries, moved[0]))
    moved[1], grad_ctx = lax.optimization_barrier((moved[1], grad_ctx))

    def attend(step, near, far, after):
        return attention(
            band, queries, grad_ctx, moved[step], near, far, *CHUNKS[step], after
        )

    def note_sum_of(own, near, far):
        return (own + near.astype(F32) + far.astype(F32)).astype(BF16)

    near1, far1 = near_swap(moved[1]), far_swap(moved[1])
    dq0, own0, rim_near0, rim_far0 = attend(0, near0, far0, ())
    dq0_other = head_swap(dq0)
    w_mine, dq0 = lax.optimization_barrier((w_mine, dq0))
    rim_near0, rim_far0, near1, far1 = lax.optimization_barrier((rim_near0, rim_far0, near1, far1))
    in_near0, in_far0 = near_swap(rim_near0), far_swap(rim_far0)
    dq1, own1, rim_near1, rim_far1 = attend(1, near1, far1, (dq0,))
    in_near0, in_far0, rim_near1, rim_far1 = lax.optimization_barrier(
        (in_near0, in_far0, rim_near1, rim_far1)
    )
    in_near1, in_far1 = near_swap(rim_near1), far_swap(rim_far1)
    owned0 = note_sum_of(own0, in_near0, in_far0)
    notes0 = section_shift(owned0, -1)
    dq1, owned0 = lax.optimization_barrier((dq1, owned0))
    dq1_other = head_swap(dq1)
    owned1 = note_sum_of(own1, in_near1, in_far1)
    notes1 = section_shift(owned1, -1)

    before = note_product(scalars, [notes0], CHUNKS[:1], w_key, w_value, (owned1,))
    own_part = frame_part(
        scalars, [dq0, dq1], [w_query], None, "frame_own", (before, dq0_other)
    )
    last = (scalars, [notes1], CHUNKS[1:], w_key, w_value)
    w_mine, own_part = lax.optimization_barrier((w_mine, own_part))
    w_theirs = near_swap(w_mine)
    give_notes = note_product(*last, (own_part,), before, (0,))
    notes_other = head_swap(give_notes)
    keep_notes = note_product(*last, (give_notes,), before, (1,))
    frame_out = frame_part(
        scalars, [dq0_other, dq1_other], [w_mine, w_theirs], own_part, "frame_sum", (keep_notes,)
    )
    notes_other, frame_out = lax.optimization_barrier((notes_other, frame_out))
    note_out = keep_notes[0].astype(F32) + notes_other[0].astype(F32)
    return (frame_out[None], note_out.astype(BF16)[None])


def solution(mesh):
    placed = (
        P("section", "seq", None),
        P("section", "seq", None),
        P(None, "head"),
        P(None, "head"),
        P(None, "head"),
        P("head", None),
        P("section", None, "seq"),
        P("section", "seq", None),
    )
    return jax.shard_map(
        per_device,
        mesh=mesh,
        in_specs=placed,
        out_specs=(P("section", "seq", "head"), P("section", "seq", "head")),
        check_vma=False,
    )
```

```python
import jax
import jax.numpy as jnp
from jax import lax
from jax.experimental import pallas as pl
from jax.experimental.pallas import tpu as pltpu
from jax.sharding import PartitionSpec as P

D = 2048
HEADS = 16
BLK = 128
HD = D // HEADS
SCALE = HD**-0.5
LOG2E = 1.4426950408889634
CHUNKS = ((0, 4), (4, 4))
VMEM = 64 * 2**20 - 2**16

F32 = jnp.float32
BF16 = jnp.bfloat16
NN = (((1,), (0,)), ((), ()))
NT = (((1,), (1,)), ((), ()))
TN = (((0,), (0,)), ((), ()))


def dot(a, b, dims):
    return lax.dot_general(a, b, dims, preferred_element_type=F32)


def section_shift(block, distance):
    count = lax.axis_size("section")
    return lax.ppermute(
        block, "section", [(i, (i + distance) % count) for i in range(count)]
    )


def near_swap(block):
    count = lax.axis_size("seq")
    return lax.ppermute(block, "seq", [(i, i ^ 1) for i in range(count)])


def far_swap(block):
    count = lax.axis_size("seq")
    pairs = [(i, i + 1) for i in range(1, count - 1, 2)]
    return lax.ppermute(block, "seq", pairs + [(j, i) for i, j in pairs])


def head_swap(block):
    return lax.ppermute(block, "head", [(0, 1), (1, 0)])


def across(block):
    count = lax.axis_size("seq")
    route = [(2 * i + g, 2 * (i ^ 8) + 1 - g) for i in range(count) for g in range(2)]
    return lax.ppermute(block, ("seq", "head"), route)


def call(
    body, grid, in_specs, out_specs, out_shape, args, name, after=(), scalars=0, scratch=(),
    flops=0,
):
    first = scalars + len(in_specs)
    unread = len(after)

    def reads(*refs):
        body(*refs[:first], *refs[first + unread :])

    in_specs = list(in_specs) + [pl.BlockSpec(memory_space=pl.ANY)] * unread
    return pl.pallas_call(
        reads,
        grid_spec=pltpu.PrefetchScalarGridSpec(
            num_scalar_prefetch=scalars,
            grid=grid,
            in_specs=in_specs,
            out_specs=out_specs,
            scratch_shapes=scratch,
        ),
        out_shape=out_shape,
        compiler_params=pltpu.CompilerParams(vmem_limit_bytes=VMEM),
        cost_estimate=pl.CostEstimate(flops=flops, bytes_accessed=0, transcendentals=0),
        name=name,
    )(*args, *after)


def start_all(copies):
    for copy in copies:
        copy.start()
    return copies


def key_value_copies(wk_ref, wv_ref, wk_scr, wv_scr, sems, h0, hc):
    part = slice(h0 * HD, (h0 + hc) * HD)
    return start_all(
        [
            pltpu.make_async_copy(wk_ref.at[:, part], wk_scr, sems.at[0]),
            pltpu.make_async_copy(wv_ref.at[:, part], wv_scr, sems.at[1]),
        ]
    )


def key_values(notes, w_key, w_value, h0, hc):
    rows = notes.shape[0]

    def body(notes_ref, wk_ref, wv_ref, out_ref, n_scr, wk_scr, wv_scr, out_scr, sems):
        (notes_in,) = start_all([pltpu.make_async_copy(notes_ref, n_scr, sems.at[2])])
        weights_in = key_value_copies(wk_ref, wv_ref, wk_scr, wv_scr, sems, h0, hc)
        notes_in.wait()
        for i, scr in enumerate((wk_scr, wv_scr)):
            weights_in[i].wait()
            out_scr[i] = dot(n_scr[...], scr[...], NN).astype(BF16)
        for copy in start_all([pltpu.make_async_copy(out_scr, out_ref, sems.at[3])]):
            copy.wait()

    far = pl.BlockSpec(memory_space=pl.ANY)
    return call(
        body,
        (),
        [far] * 3,
        far,
        jax.ShapeDtypeStruct((2, rows, hc * HD), BF16),
        (notes, w_key, w_value),
        "key_values",
        scratch=[
            pltpu.VMEM((rows, D), BF16),
            pltpu.VMEM((D, hc * HD), BF16),
            pltpu.VMEM((D, hc * HD), BF16),
            pltpu.VMEM((2, rows, hc * HD), BF16),
            pltpu.SemaphoreType.DMA((4,)),
        ],
    )


class Product:
    step = 256
    parts = 2

    def __init__(self, rows_in, weight, dims):
        self.dims = dims
        self.steps = rows_in.shape[0] // self.step
        self.size = D // 2 // self.parts
        self.out = jax.ShapeDtypeStruct((rows_in.shape[0], D // 2), BF16)
        self.scratch = [
            pltpu.VMEM(rows_in.shape, BF16),
            pltpu.VMEM(weight.shape, BF16),
            pltpu.VMEM(self.out.shape, BF16),
            pltpu.SemaphoreType.DMA((self.parts,)),
            pltpu.SemaphoreType.DMA((self.steps,)),
            pltpu.SemaphoreType.DMA((self.steps,)),
        ]

    def rows(self, m):
        return slice(m * self.step, (m + 1) * self.step)

    def part(self, p):
        cols = slice(p * self.size, (p + 1) * self.size)
        return (slice(None), cols) if self.dims is NN else (cols, slice(None))

    def start(self, a_ref, w_ref, a_scr, w_scr, o_scr, w_sems, row_sems, out_sems):
        rows_in = [
            pltpu.make_async_copy(a_ref.at[self.rows(m)], a_scr.at[self.rows(m)], row_sems.at[m])
            for m in range(self.steps)
        ]
        weight_in = [
            pltpu.make_async_copy(w_ref.at[self.part(p)], w_scr.at[self.part(p)], w_sems.at[p])
            for p in range(self.parts)
        ]
        start_all(rows_in[:1] + weight_in + rows_in[1:])
        return rows_in, weight_in

    def finish(self, copies, out_ref, a_scr, w_scr, o_scr, w_sems, row_sems, out_sems):
        rows_in, weight_in = copies
        sent = []
        for m in range(self.steps):
            at = self.rows(m)
            rows_in[m].wait()
            for p in range(self.parts):
                if m == 0:
                    weight_in[p].wait()
                cols = slice(p * self.size, (p + 1) * self.size)
                term = dot(a_scr[at, :], w_scr[self.part(p)], self.dims)
                o_scr[at, cols] = term.astype(BF16)
            copy = pltpu.make_async_copy(o_scr.at[at], out_ref.at[at], out_sems.at[m])
            sent += start_all([copy])
        return sent


def key_values_and_queries(notes, w_key, w_value, frames, w_query, h0, hc, after):
    rows = notes.shape[0]
    quarter = D // 4
    product = Product(frames, w_query, NN)

    def body(notes_ref, wk_ref, wv_ref, f_ref, wq_ref, out_ref, q_ref, give_ref,
             n_scr, wk_scr, wv_scr, out_scr, sems, *scrs):
        (notes_in,) = start_all([pltpu.make_async_copy(notes_ref, n_scr, sems.at[2])])
        weights_in = key_value_copies(wk_ref, wv_ref, wk_scr, wv_scr, sems, h0, hc)
        copies = product.start(f_ref, wq_ref, *scrs)
        notes_in.wait()
        for i, scr in enumerate((wk_scr, wv_scr)):
            weights_in[i].wait()
            out_scr[i] = dot(n_scr[...], scr[...], NN).astype(BF16)
        sent = start_all([pltpu.make_async_copy(out_scr, out_ref, sems.at[3])])
        sent += product.finish(copies, q_ref, *scrs)
        group = lax.axis_index("head")
        core = lax.rem(lax.axis_index("seq"), 2)
        offset = pl.multiple_of((1 - group) * (2 * quarter) + core * quarter, quarter)
        give = pltpu.make_async_copy(scrs[1].at[pl.ds(offset, quarter), :], give_ref, sems.at[4])
        sent += start_all([give])
        for copy in sent:
            copy.wait()

    far = pl.BlockSpec(memory_space=pl.ANY)
    return call(
        body,
        (),
        [far] * 5,
        [far] * 3,
        [
            jax.ShapeDtypeStruct((2, rows, hc * HD), BF16),
            product.out,
            jax.ShapeDtypeStruct((quarter, w_query.shape[1]), BF16),
        ],
        (notes, w_key, w_value, frames, w_query),
        "key_values_and_queries",
        after,
        scratch=[
            pltpu.VMEM((rows, D), BF16),
            pltpu.VMEM((D, hc * HD), BF16),
            pltpu.VMEM((D, hc * HD), BF16),
            pltpu.VMEM((2, rows, hc * HD), BF16),
            pltpu.SemaphoreType.DMA((5,)),
            *product.scratch,
        ],
    )


def context_gradient(grad_mixed, w_out, after):
    product = Product(grad_mixed, w_out, NT)

    def body(a_ref, w_ref, out_ref, *scrs):
        copies = product.start(a_ref, w_ref, *scrs)
        for copy in product.finish(copies, out_ref, *scrs):
            copy.wait()

    far = pl.BlockSpec(memory_space=pl.ANY)
    return call(
        body, (), [far] * 2, far, product.out, (grad_mixed, w_out), "grad_ctx", after,
        scratch=product.scratch,
    )


def frame_part(grads, weights, own, name, after):
    rows = grads[0].shape[0]
    half = D // 2
    cols = sum(g.shape[1] for g in grads)
    quarter = half // 2
    step = 256
    steps = rows // step
    terms = list(grads) + ([] if own is None else [own])
    count = len(terms)

    def body(*refs):
        group = lax.axis_index("head")
        odd = lax.rem(lax.axis_index("seq"), 2)
        term_refs, refs = refs[:count], refs[count:]
        weight_refs, refs = refs[: len(weights)], refs[len(weights) :]
        out_ref, w_scr, o_scr, *refs = refs
        term_scrs, (w_sems, term_sems, out_sems) = refs[:count], refs[count:]
        weight_copies = []
        for p in range(2):
            if own is None:
                at = pl.ds(pl.multiple_of(group * half + p * quarter, quarter), quarter)
                src, dst = weight_refs[0].at[at], w_scr.at[p * quarter : (p + 1) * quarter]
            else:
                core = odd if p == 0 else 1 - odd
                to = pl.ds(pl.multiple_of(core * quarter, quarter), quarter)
                src, dst = weight_refs[p], w_scr.at[to]
            weight_copies.append(pltpu.make_async_copy(src, dst, w_sems.at[p]))
        for copy in weight_copies:
            copy.start()
        term_copies = []
        for m in range(steps):
            at = slice(m * step, (m + 1) * step)
            for t in range(count):
                copy = pltpu.make_async_copy(term_refs[t].at[at], term_scrs[t].at[at], term_sems.at[m, t])
                copy.start()
                term_copies.append(copy)
        for copy in weight_copies:
            copy.wait()
        sent = []
        for m in range(steps):
            at = slice(m * step, (m + 1) * step)
            for t in range(count):
                term_copies[m * count + t].wait()
            left = jnp.concatenate([scr[at, :] for scr in term_scrs[: len(grads)]], axis=1)
            total = dot(left, w_scr[...], NT)
            if own is not None:
                total = total + term_scrs[-1][at, :].astype(F32)
            o_scr[at, :] = total.astype(BF16)
            copy = pltpu.make_async_copy(o_scr.at[at], out_ref.at[at], out_sems.at[m])
            copy.start()
            sent.append(copy)
        for copy in sent:
            copy.wait()

    far = pl.BlockSpec(memory_space=pl.ANY)
    return call(
        body,
        (),
        [far] * (count + len(weights)),
        far,
        jax.ShapeDtypeStruct((rows, half), BF16),
        (*terms, *weights),
        name,
        after,
        flops=8 * rows * half * cols if own is None else 0,
        scratch=[
            pltpu.VMEM((half, cols), BF16),
            pltpu.VMEM((rows, half), BF16),
            *[pltpu.VMEM(term.shape, BF16) for term in terms],
            pltpu.SemaphoreType.DMA((2,)),
            pltpu.SemaphoreType.DMA((steps, count)),
            pltpu.SemaphoreType.DMA((steps,)),
        ],
    )


def note_product(grads, chunks, w_key, w_value, after, before=None, which=(0, 1)):
    nt = grads[0].shape[1]
    half = D // 2
    ((h0, hc),) = chunks
    last = before is not None
    start = which[0]

    def body(*refs):
        grad_refs, refs = refs[: len(grads)], refs[len(grads) :]
        grad_ref = grad_refs[0]
        total = dot(grad_ref[0], refs[0][...], NT) + dot(grad_ref[1], refs[1][...], NT)
        if last:
            total = total + refs[2][0]
        out_ref = refs[-1]
        out_ref[0] = total.astype(out_ref.dtype)

    def rows_of(n):
        group = lax.axis_index("head")
        return jnp.where(n + start == 0, 1 - group, group), h0 // hc

    weight_in = pl.BlockSpec((half, hc * HD), rows_of)

    return call(
        body,
        (len(which),),
        [pl.BlockSpec(g.shape, lambda n: (0, 0, 0)) for g in grads]
        + [weight_in] * 2
        + ([pl.BlockSpec((1, nt, half), lambda n: (n + start, 0, 0))] if last else []),
        pl.BlockSpec((1, nt, half), lambda n: (n, 0, 0)),
        jax.ShapeDtypeStruct((len(which), nt, half), BF16 if last else F32),
        (*grads, w_key, w_value) + ((before,) if last else ()),
        "note_product",
        after,
    )


def attention_body(
    band_ref, q_ref, g_ref, kvo_ref, kvn_ref, kvf_ref, dq_ref, own_ref, near_ref, far_ref,
    p_scr, ds_scr, bias_ref,
):
    @pl.when(pl.program_id(0) == 0)
    def _():
        row = lax.broadcasted_iota(jnp.int32, (8, BLK), 0)
        shard = lax.axis_index("seq")
        far = shard - 1 + 2 * lax.rem(shard, 2)
        block = jnp.where(row < 2, 2 * shard, jnp.where(row < 4, 2 * (shard ^ 1), 2 * far)) + row % 2
        for b in range(q_ref.shape[0] // BLK):
            inside = (block >= band_ref[0, b]) & (block <= band_ref[1, b])
            bias_ref[:, b * BLK : (b + 1) * BLK] = jnp.where(inside, 0.0, -jnp.inf)

    scale2 = SCALE * LOG2E
    frames = q_ref.shape[0]
    nt = kvo_ref.shape[1]
    step = 256
    blocks = 3 * nt // BLK
    keys = jnp.concatenate([kvo_ref[0], kvn_ref[0], kvf_ref[0]], axis=0)
    values = jnp.concatenate([kvo_ref[1], kvn_ref[1], kvf_ref[1]], axis=0)
    for f in range(frames // step):
        cols = slice(f * step, (f + 1) * step)
        s = dot(keys, q_ref[cols, :], NT)
        gp = dot(values, g_ref[cols, :], NT)
        rows = [slice(j * BLK, (j + 1) * BLK) for j in range(blocks)]
        bias = [bias_ref[j : j + 1, cols] for j in range(blocks)]
        peak = None
        for j in range(blocks):
            top = jnp.max(s[rows[j]], axis=0, keepdims=True) + bias[j]
            peak = top if peak is None else jnp.maximum(peak, top)
        expos = []
        total = jnp.zeros((1, step), F32)
        mixed = jnp.zeros((1, step), F32)
        for j in range(blocks):
            e = jnp.exp2(s[rows[j]] * scale2 + (bias[j] - peak) * scale2)
            expos.append(e)
            total = total + jnp.sum(e, axis=0, keepdims=True)
            mixed = mixed + jnp.sum(e * gp[rows[j]], axis=0, keepdims=True)
        inv = 1.0 / total
        delta = mixed * inv
        for j in range(blocks):
            p = expos[j] * inv
            p_scr[rows[j], cols] = p.astype(BF16)
            ds_scr[rows[j], cols] = (p * (gp[rows[j]] - delta)).astype(BF16)
    dq_ref[...] = (dot(ds_scr[...], keys, TN) * SCALE).astype(BF16)
    dv = dot(p_scr[...], g_ref[...], NN)
    dk = dot(ds_scr[...], q_ref[...], NN) * SCALE
    for i, grad in enumerate((dk, dv)):
        own_ref[i] = grad[:nt]
        near_ref[i] = grad[nt : 2 * nt].astype(BF16)
        far_ref[i] = grad[2 * nt :].astype(BF16)


def attention(band, queries, grad_ctx, kv_own, kv_near, kv_far, h0, hc, after):
    frames = queries.shape[0]
    nt = kv_own.shape[1]
    frame_in = pl.BlockSpec((frames, HD), lambda h, b: (0, h0 + h))
    note_io = pl.BlockSpec((2, nt, HD), lambda h, b: (0, 0, h))
    notes_out = jax.ShapeDtypeStruct((2, nt, hc * HD), BF16)
    return call(
        attention_body,
        (hc,),
        [frame_in, frame_in, note_io, note_io, note_io],
        [pl.BlockSpec((frames, HD), lambda h, b: (0, h)), note_io, note_io, note_io],
        [
            jax.ShapeDtypeStruct((frames, hc * HD), BF16),
            jax.ShapeDtypeStruct((2, nt, hc * HD), F32),
            notes_out,
            notes_out,
        ],
        (band, queries, grad_ctx, kv_own, kv_near, kv_far),
        "attention",
        after,
        scalars=1,
        scratch=[
            pltpu.VMEM((3 * nt, frames), BF16),
            pltpu.VMEM((3 * nt, frames), BF16),
            pltpu.VMEM((8, frames), F32),
        ],
        flops=90 * frames * nt * hc * HD if h0 else 0,
    )


def per_device(notes, frames, w_query, w_key, w_value, w_out, band_blocks, grad_mixed):
    band = band_blocks[0]

    made0 = key_values(notes[0], w_key, w_value, *CHUNKS[0])
    made1, queries, given = key_values_and_queries(
        notes[0], w_key, w_value, frames[0], w_query, *CHUNKS[1], (made0,)
    )
    moved = [section_shift(made0, 1), section_shift(made1, 1)]
    w_mine = across(given)
    moved[0], queries = lax.optimization_barrier((moved[0], queries))
    near0, far0 = near_swap(moved[0]), far_swap(moved[0])
    grad_ctx = context_gradient(grad_mixed[0], w_out, (queries, moved[0]))
    moved[1], grad_ctx = lax.optimization_barrier((moved[1], grad_ctx))

    def attend(step, near, far, after):
        return attention(
            band, queries, grad_ctx, moved[step], near, far, *CHUNKS[step], after
        )

    def note_sum_of(own, near, far):
        return (own + near.astype(F32) + far.astype(F32)).astype(BF16)

    near1, far1 = near_swap(moved[1]), far_swap(moved[1])
    dq0, own0, rim_near0, rim_far0 = attend(0, near0, far0, ())
    dq0_other = head_swap(dq0)
    w_mine, dq0 = lax.optimization_barrier((w_mine, dq0))
    rim_near0, rim_far0, near1, far1 = lax.optimization_barrier((rim_near0, rim_far0, near1, far1))
    in_near0, in_far0 = near_swap(rim_near0), far_swap(rim_far0)
    dq1, own1, rim_near1, rim_far1 = attend(1, near1, far1, (dq0,))
    in_near0, in_far0, rim_near1, rim_far1 = lax.optimization_barrier(
        (in_near0, in_far0, rim_near1, rim_far1)
    )
    in_near1, in_far1 = near_swap(rim_near1), far_swap(rim_far1)
    owned0 = note_sum_of(own0, in_near0, in_far0)
    notes0 = section_shift(owned0, -1)
    dq1, owned0 = lax.optimization_barrier((dq1, owned0))
    dq1_other = head_swap(dq1)
    owned1 = note_sum_of(own1, in_near1, in_far1)
    notes1 = section_shift(owned1, -1)

    before = note_product([notes0], CHUNKS[:1], w_key, w_value, (owned1,))
    own_part = frame_part(
        [dq0, dq1], [w_query], None, "frame_own", (before, dq0_other)
    )
    w_mine, own_part = lax.optimization_barrier((w_mine, own_part))
    w_theirs = near_swap(w_mine)
    last = ([notes1], CHUNKS[1:], w_key, w_value)
    give_notes = note_product(*last, (own_part,), before, (0,))
    notes_other = head_swap(give_notes)
    keep_notes = note_product(*last, (give_notes,), before, (1,))
    frame_out = frame_part(
        [dq0_other, dq1_other], [w_mine, w_theirs], own_part, "frame_sum", (keep_notes,)
    )
    notes_other, frame_out = lax.optimization_barrier((notes_other, frame_out))
    note_out = keep_notes[0].astype(F32) + notes_other[0].astype(F32)
    return (frame_out[None], note_out.astype(BF16)[None])


def solution(mesh):
    placed = (
        P("section", "seq", None),
        P("section", "seq", None),
        P(None, "head"),
        P(None, "head"),
        P(None, "head"),
        P("head", None),
        P("section", None, "seq"),
        P("section", "seq", None),
    )
    return jax.shard_map(
        per_device,
        mesh=mesh,
        in_specs=placed,
        out_specs=(P("section", "seq", "head"), P("section", "seq", "head")),
        check_vma=False,
    )
```

```python
import jax
import jax.numpy as jnp
from jax import lax
from jax.experimental import pallas as pl
from jax.experimental.pallas import tpu as pltpu
from jax.sharding import PartitionSpec as P

D = 2048
HEADS = 16
BLK = 128
HD = D // HEADS
SCALE = HD**-0.5
LOG2E = 1.4426950408889634
CHUNKS = ((0, 4), (4, 4))
VMEM = 64 * 2**20 - 2**16

F32 = jnp.float32
BF16 = jnp.bfloat16
NN = (((1,), (0,)), ((), ()))
NT = (((1,), (1,)), ((), ()))
TN = (((0,), (0,)), ((), ()))


def dot(a, b, dims):
    return lax.dot_general(a, b, dims, preferred_element_type=F32)


def section_shift(block, distance):
    count = lax.axis_size("section")
    return lax.ppermute(
        block, "section", [(i, (i + distance) % count) for i in range(count)]
    )


def near_swap(block):
    count = lax.axis_size("seq")
    return lax.ppermute(block, "seq", [(i, i ^ 1) for i in range(count)])


def far_swap(block):
    count = lax.axis_size("seq")
    pairs = [(i, i + 1) for i in range(1, count - 1, 2)]
    return lax.ppermute(block, "seq", pairs + [(j, i) for i, j in pairs])


def head_swap(block):
    return lax.ppermute(block, "head", [(0, 1), (1, 0)])


def across(block):
    count = lax.axis_size("seq")
    route = [(2 * i + g, 2 * (i ^ 8) + 1 - g) for i in range(count) for g in range(2)]
    return lax.ppermute(block, ("seq", "head"), route)


def call(
    body, grid, in_specs, out_specs, out_shape, args, name, after=(), scalars=0, scratch=(),
    flops=0,
):
    first = scalars + len(in_specs)
    unread = len(after)

    def reads(*refs):
        body(*refs[:first], *refs[first + unread :])

    in_specs = list(in_specs) + [pl.BlockSpec(memory_space=pl.ANY)] * unread
    return pl.pallas_call(
        reads,
        grid_spec=pltpu.PrefetchScalarGridSpec(
            num_scalar_prefetch=scalars,
            grid=grid,
            in_specs=in_specs,
            out_specs=out_specs,
            scratch_shapes=scratch,
        ),
        out_shape=out_shape,
        compiler_params=pltpu.CompilerParams(vmem_limit_bytes=VMEM),
        cost_estimate=pl.CostEstimate(flops=flops, bytes_accessed=0, transcendentals=0),
        name=name,
    )(*args, *after)


def start_all(copies):
    for copy in copies:
        copy.start()
    return copies


def key_value_copies(wk_ref, wv_ref, wk_scr, wv_scr, sems, h0, hc):
    part = slice(h0 * HD, (h0 + hc) * HD)
    return start_all(
        [
            pltpu.make_async_copy(wk_ref.at[:, part], wk_scr, sems.at[0]),
            pltpu.make_async_copy(wv_ref.at[:, part], wv_scr, sems.at[1]),
        ]
    )


def key_values(notes, w_key, w_value, h0, hc):
    rows = notes.shape[0]

    def body(notes_ref, wk_ref, wv_ref, out_ref, n_scr, wk_scr, wv_scr, out_scr, sems):
        (notes_in,) = start_all([pltpu.make_async_copy(notes_ref, n_scr, sems.at[2])])
        weights_in = key_value_copies(wk_ref, wv_ref, wk_scr, wv_scr, sems, h0, hc)
        sent = []
        notes_in.wait()
        for i, scr in enumerate((wk_scr, wv_scr)):
            weights_in[i].wait()
            out_scr[i] = dot(n_scr[...], scr[...], NN).astype(BF16)
            sent += start_all(
                [pltpu.make_async_copy(out_scr.at[i], out_ref.at[i], sems.at[3 + i])]
            )
        for copy in sent:
            copy.wait()

    far = pl.BlockSpec(memory_space=pl.ANY)
    return call(
        body,
        (),
        [far] * 3,
        far,
        jax.ShapeDtypeStruct((2, rows, hc * HD), BF16),
        (notes, w_key, w_value),
        "key_values",
        scratch=[
            pltpu.VMEM((rows, D), BF16),
            pltpu.VMEM((D, hc * HD), BF16),
            pltpu.VMEM((D, hc * HD), BF16),
            pltpu.VMEM((2, rows, hc * HD), BF16),
            pltpu.SemaphoreType.DMA((5,)),
        ],
    )


class Product:
    step = 256
    parts = 2

    def __init__(self, rows_in, weight, dims):
        self.dims = dims
        self.steps = rows_in.shape[0] // self.step
        self.size = D // 2 // self.parts
        self.out = jax.ShapeDtypeStruct((rows_in.shape[0], D // 2), BF16)
        self.scratch = [
            pltpu.VMEM(rows_in.shape, BF16),
            pltpu.VMEM(weight.shape, BF16),
            pltpu.VMEM(self.out.shape, BF16),
            pltpu.SemaphoreType.DMA((self.parts,)),
            pltpu.SemaphoreType.DMA((self.steps,)),
            pltpu.SemaphoreType.DMA((self.steps,)),
        ]

    def rows(self, m):
        return slice(m * self.step, (m + 1) * self.step)

    def part(self, p):
        cols = slice(p * self.size, (p + 1) * self.size)
        return (slice(None), cols) if self.dims is NN else (cols, slice(None))

    def start(self, a_ref, w_ref, a_scr, w_scr, o_scr, w_sems, row_sems, out_sems):
        rows_in = [
            pltpu.make_async_copy(a_ref.at[self.rows(m)], a_scr.at[self.rows(m)], row_sems.at[m])
            for m in range(self.steps)
        ]
        weight_in = [
            pltpu.make_async_copy(w_ref.at[self.part(p)], w_scr.at[self.part(p)], w_sems.at[p])
            for p in range(self.parts)
        ]
        start_all(rows_in[:1] + weight_in + rows_in[1:])
        return rows_in, weight_in

    def finish(self, copies, out_ref, a_scr, w_scr, o_scr, w_sems, row_sems, out_sems):
        rows_in, weight_in = copies
        sent = []
        for m in range(self.steps):
            at = self.rows(m)
            rows_in[m].wait()
            for p in range(self.parts):
                if m == 0:
                    weight_in[p].wait()
                cols = slice(p * self.size, (p + 1) * self.size)
                term = dot(a_scr[at, :], w_scr[self.part(p)], self.dims)
                o_scr[at, cols] = term.astype(BF16)
            copy = pltpu.make_async_copy(o_scr.at[at], out_ref.at[at], out_sems.at[m])
            sent += start_all([copy])
        return sent


def key_values_and_queries(notes, w_key, w_value, frames, w_query, h0, hc, after):
    rows = notes.shape[0]
    quarter = D // 4
    product = Product(frames, w_query, NN)

    def body(notes_ref, wk_ref, wv_ref, f_ref, wq_ref, out_ref, q_ref, give_ref,
             n_scr, wk_scr, wv_scr, out_scr, sems, *scrs):
        (notes_in,) = start_all([pltpu.make_async_copy(notes_ref, n_scr, sems.at[2])])
        weights_in = key_value_copies(wk_ref, wv_ref, wk_scr, wv_scr, sems, h0, hc)
        copies = product.start(f_ref, wq_ref, *scrs)
        notes_in.wait()
        for i, scr in enumerate((wk_scr, wv_scr)):
            weights_in[i].wait()
            out_scr[i] = dot(n_scr[...], scr[...], NN).astype(BF16)
        sent = start_all([pltpu.make_async_copy(out_scr, out_ref, sems.at[3])])
        sent += product.finish(copies, q_ref, *scrs)
        group = lax.axis_index("head")
        core = lax.rem(lax.axis_index("seq"), 2)
        offset = pl.multiple_of((1 - group) * (2 * quarter) + core * quarter, quarter)
        give = pltpu.make_async_copy(scrs[1].at[pl.ds(offset, quarter), :], give_ref, sems.at[4])
        sent += start_all([give])
        for copy in sent:
            copy.wait()

    far = pl.BlockSpec(memory_space=pl.ANY)
    return call(
        body,
        (),
        [far] * 5,
        [far] * 3,
        [
            jax.ShapeDtypeStruct((2, rows, hc * HD), BF16),
            product.out,
            jax.ShapeDtypeStruct((quarter, w_query.shape[1]), BF16),
        ],
        (notes, w_key, w_value, frames, w_query),
        "key_values_and_queries",
        after,
        scratch=[
            pltpu.VMEM((rows, D), BF16),
            pltpu.VMEM((D, hc * HD), BF16),
            pltpu.VMEM((D, hc * HD), BF16),
            pltpu.VMEM((2, rows, hc * HD), BF16),
            pltpu.SemaphoreType.DMA((5,)),
            *product.scratch,
        ],
    )


def context_gradient(grad_mixed, w_out, after):
    product = Product(grad_mixed, w_out, NT)

    def body(a_ref, w_ref, out_ref, *scrs):
        copies = product.start(a_ref, w_ref, *scrs)
        for copy in product.finish(copies, out_ref, *scrs):
            copy.wait()

    far = pl.BlockSpec(memory_space=pl.ANY)
    return call(
        body, (), [far] * 2, far, product.out, (grad_mixed, w_out), "grad_ctx", after,
        scratch=product.scratch,
    )


def frame_part(grads, weights, own, name, after):
    rows = grads[0].shape[0]
    half = D // 2
    cols = sum(g.shape[1] for g in grads)
    quarter = half // 2
    step = 256
    steps = rows // step
    terms = list(grads) + ([] if own is None else [own])
    count = len(terms)

    def body(*refs):
        group = lax.axis_index("head")
        odd = lax.rem(lax.axis_index("seq"), 2)
        term_refs, refs = refs[:count], refs[count:]
        weight_refs, refs = refs[: len(weights)], refs[len(weights) :]
        out_ref, w_scr, o_scr, *refs = refs
        term_scrs, (w_sems, term_sems, out_sems) = refs[:count], refs[count:]
        weight_copies = []
        for p in range(2):
            if own is None:
                at = pl.ds(pl.multiple_of(group * half + p * quarter, quarter), quarter)
                src, dst = weight_refs[0].at[at], w_scr.at[p * quarter : (p + 1) * quarter]
            else:
                core = odd if p == 0 else 1 - odd
                to = pl.ds(pl.multiple_of(core * quarter, quarter), quarter)
                src, dst = weight_refs[p], w_scr.at[to]
            weight_copies.append(pltpu.make_async_copy(src, dst, w_sems.at[p]))
        for copy in weight_copies:
            copy.start()
        term_copies = []
        for m in range(steps):
            at = slice(m * step, (m + 1) * step)
            for t in range(count):
                copy = pltpu.make_async_copy(term_refs[t].at[at], term_scrs[t].at[at], term_sems.at[m, t])
                copy.start()
                term_copies.append(copy)
        for copy in weight_copies:
            copy.wait()
        sent = []
        for m in range(steps):
            at = slice(m * step, (m + 1) * step)
            for t in range(count):
                term_copies[m * count + t].wait()
            left = jnp.concatenate([scr[at, :] for scr in term_scrs[: len(grads)]], axis=1)
            total = dot(left, w_scr[...], NT)
            if own is not None:
                total = total + term_scrs[-1][at, :].astype(F32)
            o_scr[at, :] = total.astype(BF16)
            copy = pltpu.make_async_copy(o_scr.at[at], out_ref.at[at], out_sems.at[m])
            copy.start()
            sent.append(copy)
        for copy in sent:
            copy.wait()

    far = pl.BlockSpec(memory_space=pl.ANY)
    return call(
        body,
        (),
        [far] * (count + len(weights)),
        far,
        jax.ShapeDtypeStruct((rows, half), BF16),
        (*terms, *weights),
        name,
        after,
        flops=8 * rows * half * cols if own is None else 0,
        scratch=[
            pltpu.VMEM((half, cols), BF16),
            pltpu.VMEM((rows, half), BF16),
            *[pltpu.VMEM(term.shape, BF16) for term in terms],
            pltpu.SemaphoreType.DMA((2,)),
            pltpu.SemaphoreType.DMA((steps, count)),
            pltpu.SemaphoreType.DMA((steps,)),
        ],
    )


def note_product(grads, chunks, w_key, w_value, after, before=None, which=(0, 1)):
    nt = grads[0].shape[1]
    half = D // 2
    ((h0, hc),) = chunks
    last = before is not None
    start = which[0]

    def body(*refs):
        grad_refs, refs = refs[: len(grads)], refs[len(grads) :]
        grad_ref = grad_refs[0]
        total = dot(grad_ref[0], refs[0][...], NT) + dot(grad_ref[1], refs[1][...], NT)
        if last:
            total = total + refs[2][0]
        out_ref = refs[-1]
        out_ref[0] = total.astype(out_ref.dtype)

    def rows_of(n):
        group = lax.axis_index("head")
        return jnp.where(n + start == 0, 1 - group, group), h0 // hc

    weight_in = pl.BlockSpec((half, hc * HD), rows_of)

    return call(
        body,
        (len(which),),
        [pl.BlockSpec(g.shape, lambda n: (0, 0, 0)) for g in grads]
        + [weight_in] * 2
        + ([pl.BlockSpec((1, nt, half), lambda n: (n + start, 0, 0))] if last else []),
        pl.BlockSpec((1, nt, half), lambda n: (n, 0, 0)),
        jax.ShapeDtypeStruct((len(which), nt, half), BF16 if last else F32),
        (*grads, w_key, w_value) + ((before,) if last else ()),
        "note_product",
        after,
    )


def attention_body(
    band_ref, q_ref, g_ref, kvo_ref, kvn_ref, kvf_ref, dq_ref, own_ref, near_ref, far_ref,
    p_scr, ds_scr, bias_ref,
):
    @pl.when(pl.program_id(0) == 0)
    def _():
        row = lax.broadcasted_iota(jnp.int32, (8, BLK), 0)
        shard = lax.axis_index("seq")
        far = shard - 1 + 2 * lax.rem(shard, 2)
        block = jnp.where(row < 2, 2 * shard, jnp.where(row < 4, 2 * (shard ^ 1), 2 * far)) + row % 2
        for b in range(q_ref.shape[0] // BLK):
            inside = (block >= band_ref[0, b]) & (block <= band_ref[1, b])
            bias_ref[:, b * BLK : (b + 1) * BLK] = jnp.where(inside, 0.0, -jnp.inf)

    scale2 = SCALE * LOG2E
    frames = q_ref.shape[0]
    nt = kvo_ref.shape[1]
    step = 256
    blocks = 3 * nt // BLK
    keys = jnp.concatenate([kvo_ref[0], kvn_ref[0], kvf_ref[0]], axis=0)
    values = jnp.concatenate([kvo_ref[1], kvn_ref[1], kvf_ref[1]], axis=0)
    for f in range(frames // step):
        cols = slice(f * step, (f + 1) * step)
        s = dot(keys, q_ref[cols, :], NT)
        gp = dot(values, g_ref[cols, :], NT)
        rows = [slice(j * BLK, (j + 1) * BLK) for j in range(blocks)]
        bias = [bias_ref[j : j + 1, cols] for j in range(blocks)]
        peak = None
        for j in range(blocks):
            top = jnp.max(s[rows[j]], axis=0, keepdims=True) + bias[j]
            peak = top if peak is None else jnp.maximum(peak, top)
        expos = []
        total = jnp.zeros((1, step), F32)
        mixed = jnp.zeros((1, step), F32)
        for j in range(blocks):
            e = jnp.exp2(s[rows[j]] * scale2 + (bias[j] - peak) * scale2)
            expos.append(e)
            total = total + jnp.sum(e, axis=0, keepdims=True)
            mixed = mixed + jnp.sum(e * gp[rows[j]], axis=0, keepdims=True)
        inv = 1.0 / total
        delta = mixed * inv
        for j in range(blocks):
            p = expos[j] * inv
            p_scr[rows[j], cols] = p.astype(BF16)
            ds_scr[rows[j], cols] = (p * (gp[rows[j]] - delta)).astype(BF16)
    dq_ref[...] = (dot(ds_scr[...], keys, TN) * SCALE).astype(BF16)
    dv = dot(p_scr[...], g_ref[...], NN)
    dk = dot(ds_scr[...], q_ref[...], NN) * SCALE
    for i, grad in enumerate((dk, dv)):
        own_ref[i] = grad[:nt]
        near_ref[i] = grad[nt : 2 * nt].astype(BF16)
        far_ref[i] = grad[2 * nt :].astype(BF16)


def attention(band, queries, grad_ctx, kv_own, kv_near, kv_far, h0, hc, after):
    frames = queries.shape[0]
    nt = kv_own.shape[1]
    frame_in = pl.BlockSpec((frames, HD), lambda h, b: (0, h0 + h))
    note_io = pl.BlockSpec((2, nt, HD), lambda h, b: (0, 0, h))
    notes_out = jax.ShapeDtypeStruct((2, nt, hc * HD), BF16)
    return call(
        attention_body,
        (hc,),
        [frame_in, frame_in, note_io, note_io, note_io],
        [pl.BlockSpec((frames, HD), lambda h, b: (0, h)), note_io, note_io, note_io],
        [
            jax.ShapeDtypeStruct((frames, hc * HD), BF16),
            jax.ShapeDtypeStruct((2, nt, hc * HD), F32),
            notes_out,
            notes_out,
        ],
        (band, queries, grad_ctx, kv_own, kv_near, kv_far),
        "attention",
        after,
        scalars=1,
        scratch=[
            pltpu.VMEM((3 * nt, frames), BF16),
            pltpu.VMEM((3 * nt, frames), BF16),
            pltpu.VMEM((8, frames), F32),
        ],
        flops=90 * frames * nt * hc * HD if h0 else 0,
    )


def per_device(notes, frames, w_query, w_key, w_value, w_out, band_blocks, grad_mixed):
    band = band_blocks[0]

    made0 = key_values(notes[0], w_key, w_value, *CHUNKS[0])
    made1, queries, given = key_values_and_queries(
        notes[0], w_key, w_value, frames[0], w_query, *CHUNKS[1], (made0,)
    )
    moved = [section_shift(made0, 1), section_shift(made1, 1)]
    w_mine = across(given)
    moved[0], queries = lax.optimization_barrier((moved[0], queries))
    near0, far0 = near_swap(moved[0]), far_swap(moved[0])
    grad_ctx = context_gradient(grad_mixed[0], w_out, (queries, moved[0]))
    moved[1], grad_ctx = lax.optimization_barrier((moved[1], grad_ctx))

    def attend(step, near, far, after):
        return attention(
            band, queries, grad_ctx, moved[step], near, far, *CHUNKS[step], after
        )

    def note_sum_of(own, near, far):
        return (own + near.astype(F32) + far.astype(F32)).astype(BF16)

    near1, far1 = near_swap(moved[1]), far_swap(moved[1])
    dq0, own0, rim_near0, rim_far0 = attend(0, near0, far0, ())
    dq0_other = head_swap(dq0)
    w_mine, dq0 = lax.optimization_barrier((w_mine, dq0))
    rim_near0, rim_far0, near1, far1 = lax.optimization_barrier((rim_near0, rim_far0, near1, far1))
    in_near0, in_far0 = near_swap(rim_near0), far_swap(rim_far0)
    dq1, own1, rim_near1, rim_far1 = attend(1, near1, far1, (dq0,))
    in_near0, in_far0, rim_near1, rim_far1 = lax.optimization_barrier(
        (in_near0, in_far0, rim_near1, rim_far1)
    )
    in_near1, in_far1 = near_swap(rim_near1), far_swap(rim_far1)
    owned0 = note_sum_of(own0, in_near0, in_far0)
    notes0 = section_shift(owned0, -1)
    dq1, owned0 = lax.optimization_barrier((dq1, owned0))
    dq1_other = head_swap(dq1)
    owned1 = note_sum_of(own1, in_near1, in_far1)
    notes1 = section_shift(owned1, -1)

    before = note_product([notes0], CHUNKS[:1], w_key, w_value, (owned1,))
    own_part = frame_part(
        [dq0, dq1], [w_query], None, "frame_own", (before, dq0_other)
    )
    w_mine, own_part = lax.optimization_barrier((w_mine, own_part))
    w_theirs = near_swap(w_mine)
    last = ([notes1], CHUNKS[1:], w_key, w_value)
    give_notes = note_product(*last, (own_part,), before, (0,))
    notes_other = head_swap(give_notes)
    keep_notes = note_product(*last, (give_notes,), before, (1,))
    frame_out = frame_part(
        [dq0_other, dq1_other], [w_mine, w_theirs], own_part, "frame_sum", (keep_notes,)
    )
    notes_other, frame_out = lax.optimization_barrier((notes_other, frame_out))
    note_out = keep_notes[0].astype(F32) + notes_other[0].astype(F32)
    return (frame_out[None], note_out.astype(BF16)[None])


def solution(mesh):
    placed = (
        P("section", "seq", None),
        P("section", "seq", None),
        P(None, "head"),
        P(None, "head"),
        P(None, "head"),
        P("head", None),
        P("section", None, "seq"),
        P("section", "seq", None),
    )
    return jax.shard_map(
        per_device,
        mesh=mesh,
        in_specs=placed,
        out_specs=(P("section", "seq", "head"), P("section", "seq", "head")),
        check_vma=False,
    )
```
